256 devices in a mesh: wide: 64 (over y, z, x_hi), narrow: 4 (over x_lo, core).
Axes of the slice: x: 4 (x_hi: 2, x_lo: 2; x = x_hi * 2 + x_lo), y: 4, z: 8, core: 2. Of those that a mesh axis runs over, the one named last changes fastest.
Arguments:
- volume: bfloat16 [128, 64, 64, 128], P('wide', 'narrow'), may hold values from -16 to 16
- down_weight: bfloat16 [1024, 256], replicated, may hold values from -0.1875 to 0.1875
- conv_weight: bfloat16 [27, 256, 256], replicated, may hold values from -0.078125 to 0.078125
- cotangent: bfloat16 [64, 32, 32, 256], P('wide', None, None, 'narrow'), may hold values from -16 to 16
Outputs:
- activated: bfloat16 [64, 32, 32, 256], P('wide', None, None, 'narrow')
- volume_grad: bfloat16 [128, 64, 64, 128], P('wide', 'narrow')
- down_grad: float32 [1024, 256], P(('wide', 'narrow'))
- conv_grad: float32 [27, 256, 256], P(None, 'narrow', 'wide')
The draws below stay inside these ranges and needn't reach their ends.
All inputs are finite; a program needn't handle non-finite values.
Results may differ from the reference program's by a relative error of at most 0.0095.
Values may be sent and summed in bfloat16 or wider, within the bound.
A program may use at most 64 MiB of HBM per device.

```python
import math
import jax
import jax.numpy as jnp

C1 = 128
C2 = 256
SIDE = 32
DEEP = 64


def strengthened(drawn, rng, source, target, parts, factor):
    def block_of(position):
        return (jnp.arange(drawn.shape[position]) // (drawn.shape[position] // parts)).reshape((-1,) + (1,) * (drawn.ndim - 1 - position))

    one_side = jax.random.permutation(rng, parts)[block_of(target)]
    second = (block_of(target) + parts // 2) % parts
    return jnp.where((block_of(source) == one_side) | (block_of(source) == second), factor * drawn, drawn)


def block_scale(own_key, shape, split, low, top_value):
    loudness = 1.0
    for position, shards_of in split:
        draws = jax.random.uniform(jax.random.fold_in(jax.random.fold_in(own_key, 6), position), (shards_of,), jnp.float32, low / len(split), top_value / len(split))
        loudness = loudness * jnp.repeat(jnp.exp(draws), shape[position] // shards_of).reshape((-1,) + (1,) * (len(shape) - 1 - position))
    return loudness


def centred(stream_key, shape, width, bound, pieces=(), dtype=jnp.bfloat16):
    values = width * jax.random.normal(stream_key, shape, jnp.float32)
    if pieces:
        values = values * block_scale(stream_key, shape, pieces, -0.22, 0.18)
    return jnp.clip(values, -bound, bound).astype(dtype)


def noise_with(stream_key, shape, deviation, bound, cuts, heavy, held_as=jnp.bfloat16):
    result = deviation * jax.random.normal(stream_key, shape, jnp.float32)
    if cuts:
        result = result * block_scale(stream_key, shape, cuts, -0.22, 0.18)
    return jnp.clip(strengthened(result, jax.random.fold_in(stream_key, 3), *heavy), -bound, bound).astype(held_as)


def setup_inputs(seed: int = 0) -> dict:
    splits = jax.random.split(jax.random.key(seed), 5)
    volume = noise_with(splits[0], (2 * DEEP, 2 * SIDE, 2 * SIDE, C1), 1.0, 16.0, ((0, 64), (1, 4)), (0, 3, 64, 4.0))
    down_weight = centred(splits[1], (8 * C1, C2), (8 * C1) ** -0.5, 0.1875)
    conv_weight = centred(splits[2], (27, C2, C2), (27 * C2) ** -0.5, 0.078125)
    cotangent = noise_with(splits[3], (DEEP, SIDE, SIDE, C2), 1.0, 16.0, ((0, 64), (3, 4)), (0, 3, 64, 4.0))
    return dict(volume=volume, down_weight=down_weight, conv_weight=conv_weight, cotangent=cotangent)


def silu_slope(values):
    sigma = jax.nn.sigmoid(values)
    return sigma * (1.0 + values * (1.0 - sigma))

def reference(volume, down_weight, conv_weight, cotangent):
    deep_n = volume.shape[0] // 2
    side_n = volume.shape[1] // 2
    chan_in = volume.shape[3]
    chan_out = down_weight.shape[1]
    patches = volume.reshape(deep_n, 2, side_n, 2, side_n, 2, chan_in)
    patches = patches.transpose(0, 2, 4, 1, 3, 5, 6).reshape(deep_n * side_n * side_n, 8 * chan_in)
    deep = jnp.dot(patches, down_weight, preferred_element_type=jnp.float32).astype(jnp.bfloat16)
    deep = deep.reshape(deep_n, side_n, side_n, chan_out)
    padded = jnp.pad(deep, ((1, 1), (1, 1), (1, 1), (0, 0)))
    preact = jnp.zeros((deep_n * side_n * side_n, chan_out), jnp.float32)
    for t in range(27):
        i, j, k = (t // 9, t // 3 % 3, t % 3)
        slab = padded[i:i + deep_n, j:j + side_n, k:k + side_n].reshape(-1, chan_out)
        preact = preact + jnp.dot(slab, conv_weight[t], preferred_element_type=jnp.float32)
    activated = jax.nn.silu(preact).astype(jnp.bfloat16).reshape(deep_n, side_n, side_n, chan_out)
    grad_pre = (cotangent.astype(jnp.float32).reshape(-1, chan_out) * silu_slope(preact)).astype(jnp.bfloat16)
    grad_pad = jnp.pad(grad_pre.reshape(deep_n, side_n, side_n, chan_out), ((1, 1), (1, 1), (1, 1), (0, 0)))
    grad_deep = jnp.zeros((deep_n * side_n * side_n, chan_out), jnp.float32)
    weight_terms = []
    for t in range(27):
        i, j, k = (t // 9, t // 3 % 3, t % 3)
        grad_slab = grad_pad[2 - i:2 - i + deep_n, 2 - j:2 - j + side_n, 2 - k:2 - k + side_n].reshape(-1, chan_out)
        grad_deep = grad_deep + jnp.dot(grad_slab, conv_weight[t].T, preferred_element_type=jnp.float32)
        slab = padded[i:i + deep_n, j:j + side_n, k:k + side_n].reshape(-1, chan_out)
        weight_terms.append(jnp.dot(slab.T, grad_pre, preferred_element_type=jnp.float32))
    factor = 1.0 / (side_n * math.sqrt(deep_n))
    conv_grad = jnp.stack(weight_terms) * factor
    grad_deep = grad_deep.astype(jnp.bfloat16)
    down_grad = jnp.dot(patches.T, grad_deep, preferred_element_type=jnp.float32) * factor
    volume_grad = jnp.dot(grad_deep, down_weight.T, preferred_element_type=jnp.float32).astype(jnp.bfloat16)
    volume_grad = volume_grad.reshape(deep_n, side_n, side_n, 2, 2, 2, chan_in)
    volume_grad = volume_grad.transpose(0, 3, 1, 4, 2, 5, 6).reshape(2 * deep_n, 2 * side_n, 2 * side_n, chan_in)
    return (activated, volume_grad, down_grad, conv_grad)
```

```python
import functools
import math

import jax
import jax.numpy as jnp
from jax import lax
from jax.experimental import pallas as pl
from jax.experimental.pallas import tpu as pltpu
from jax.sharding import PartitionSpec as P

MESH = pl.DeviceIdType.MESH
BF = jnp.bfloat16
F32 = jnp.float32
NY, NZ = 4, 8

COT = 0
DEEP_HALO = 3
DEEP_SHARE = 11
ACT = 20
GRAD_HALO = 23
GRAD_SHARE = 31
CONV_Y = 34
CONV_Z = 43
DOWN_N = 64
DOWN_Y = 67
DOWN_Z = 70
LAST = 77
MESSAGES = 80


def matmul(a, b):
    return jnp.dot(a, b, preferred_element_type=F32)


def matmul_nt(a, b):
    return lax.dot_general(a, b, (((1,), (1,)), ((), ())), preferred_element_type=F32)


def kernel(
    factor,
    vol_ref,
    dw_ref,
    cw_ref,
    cot_ref,
    act_out,
    vg_out,
    dg_out,
    cg_out,
    vol,
    dw,
    cw,
    cot,
    wide_f32,
    patches,
    patches_t,
    deep,
    grad,
    deep_all,
    grad_t_send,
    grad_t,
    grad_rows,
    acc,
    cot_send,
    cot_recv,
    act_send,
    act_recv,
    cy_send,
    cy_recv,
    sum_rows,
    z_rows,
    cz_send,
    cz_recv,
    dn_rows,
    dn_send,
    dn_recv,
    dy_send,
    dy_recv,
    dz_send,
    dz_recv,
    last_send,
    last_recv,
    local_sem,
    send_sem,
    recv_sem,
):
    w = lax.axis_index("wide")
    n = lax.axis_index("narrow")
    y, z, xh = w // 16, (w // 2) % NZ, w % 2
    l, c = n // 2, n % 2

    def wide_of(yy, zz, xx):
        return ((yy % NY) * NZ + zz % NZ) * 2 + xx

    near = [(w, (n + d) % 4) for d in range(1, 4)]
    up, down = (w + 1) % 64, (w + 63) % 64
    right, left = (n + 1) % 4, (n + 3) % 4
    depth = [(s, m) for s in (up, down) for m in (n, right, left)]
    ys = [(wide_of(y + d, z, xh), n) for d in range(1, NY)]
    zs = [(wide_of(y, z + d, xh), n) for d in range(1, NZ)]
    other_c = n + 1 - 2 * c
    lasts = [(wide_of(y, z, 1 - xh), n), (wide_of(y, z, 1 - xh), other_c), (w, other_c)]

    barrier = pltpu.get_barrier_semaphore()
    partners = near + depth + ys + zs + lasts[:2]
    for who in partners:
        pl.semaphore_signal(barrier, inc=1, device_id=who, device_id_type=MESH)

    started = []

    def send(number, src, dst, who):
        copy = pltpu.make_async_remote_copy(
            src_ref=src,
            dst_ref=dst,
            send_sem=send_sem.at[number],
            recv_sem=recv_sem.at[number],
            device_id=who,
            device_id_type=MESH,
        )
        copy.start()
        started.append(copy)
        return copy

    loads = [
        pltpu.make_async_copy(src, dst, local_sem.at[s])
        for s, (src, dst) in enumerate(((cot_ref, cot), (vol_ref, vol), (dw_ref, dw), (cw_ref, cw)))
    ]
    for copy in loads:
        copy.start()

    deep_all[:, 0:1] = jnp.zeros((3, 1, 32, 128), BF)
    deep_all[:, 33:34] = jnp.zeros((3, 1, 32, 128), BF)
    z_rows[...] = jnp.zeros_like(z_rows)

    loads[0].wait()
    for m in range(4):
        cot_send[m] = jnp.concatenate([cot[m, :128], cot[m, 128:]], axis=1)
    cot_recv[pl.ds(n, 1)] = cot_send[pl.ds(n, 1)]
    pl.semaphore_wait(barrier, len(partners))
    cot_copies = [
        send(COT + d - 1, cot_send.at[(n + d) % 4], cot_recv.at[n], near[d - 1]) for d in range(1, 4)
    ]

    loads[1].wait()
    wide_f32[...] = vol[...].astype(F32)
    for a in range(2):
        for b in range(2):
            for e in range(2):
                part = wide_f32[a, :, b, pl.ds(e, 32, stride=2), :].reshape(256, 128).astype(BF)
                at = (4 * a + 2 * b + e) * 128
                patches[:, at : at + 128] = part
    loads[2].wait()
    cells = matmul(patches[...], dw[...]).astype(BF)
    for half in range(2):
        deep[half, 1, 1:9] = cells[:, 128 * half : 128 * half + 128].reshape(8, 32, 128)

    def send_halos(buf, base):
        copies = []
        for s, (to, plane) in enumerate(((up, 0), (down, 2))):
            copies.append(
                send(base + s, buf.at[:, 1, pl.ds(1, 8)], buf.at[:, plane, pl.ds(1, 8)], (to, n))
            )
        for s, (to, plane) in enumerate(((w, 1), (up, 0), (down, 2))):
            copies.append(
                send(base + 2 + 2 * s, buf.at[:, 1, pl.ds(8, 1)], buf.at[:, plane, pl.ds(0, 1)], (to, right))
            )
            copies.append(
                send(base + 3 + 2 * s, buf.at[:, 1, pl.ds(1, 1)], buf.at[:, plane, pl.ds(9, 1)], (to, left))
            )
        return copies

    def rows_arrive(buf, copies, plane):
        s = {1: 0, 0: 1, 2: 2}[plane]
        copies[2 + 2 * s].wait_recv()
        copies[3 + 2 * s].wait_recv()

        @pl.when(n == 0)
        def _():
            buf[:, plane, 0:1] = jnp.zeros((2, 1, 32, 128), BF)

        @pl.when(n == 3)
        def _():
            buf[:, plane, 9:10] = jnp.zeros((2, 1, 32, 128), BF)

    def plane_arrives(buf, copies, plane):
        copies[0 if plane == 0 else 1].wait_recv()
        rows_arrive(buf, copies, plane)

        @pl.when(w == (0 if plane == 0 else 63))
        def _():
            buf[:, plane] = jnp.zeros((2, 10, 32, 128), BF)

    def share_deep(plane):
        deep_all[plane, pl.ds(1 + 8 * n, 8)] = deep[pl.ds(l, 1), plane, 1:9].reshape(8, 32, 128)
        return [
            send(
                DEEP_SHARE + 3 * plane + d - 1,
                deep.at[((n + d) % 4) // 2, plane, pl.ds(1, 8)],
                deep_all.at[plane, pl.ds(1 + 8 * n, 8)],
                near[d - 1],
            )
            for d in range(1, 4)
        ]

    deep_halos = send_halos(deep, DEEP_HALO)
    shared = {1: share_deep(1)}
    for s in range(4):
        block = patches[:, 256 * s : 256 * s + 256].astype(F32)
        patches_t[256 * s : 256 * s + 256, :] = block.T.astype(BF)

    def window(buf, plane, first):
        return [buf[half, plane, first : first + 8].reshape(256, 128) for half in range(2)]

    def shifted(value, by, masked):
        column = lax.broadcasted_iota(jnp.int32, value.shape, 0) % 32
        return jnp.where(column == masked, 0.0, pltpu.roll(value, by, 0))

    loads[3].wait()
    for i in (1, 0, 2):
        if i == 1:
            rows_arrive(deep, deep_halos, 1)
        else:
            plane_arrives(deep, deep_halos, i)
            shared[i] = share_deep(i)
        slab = jnp.concatenate(window(deep, i, 0) + window(deep, i, 1) + window(deep, i, 2), axis=1)
        for k in range(3):
            weights = jnp.concatenate([cw[9 * i + 3 * j + k] for j in range(3)], axis=0)
            term = matmul(slab, weights)
            acc[k] = term if i == 1 else acc[k] + term
    preact = shifted(acc[0], 1, 0) + acc[1] + shifted(acc[2], 255, 31)

    for copy in cot_copies:
        copy.wait_recv()
    cotangent = jnp.concatenate(
        [
            jnp.concatenate([cot_recv[m][:, :64], cot_recv[m][:, 64:]], axis=0)
            for m in range(4)
        ],
        axis=1,
    ).astype(F32)
    sigma = 1.0 / (1.0 + jnp.exp(-preact))
    activated = (preact * sigma).astype(BF)
    grad_pre = (cotangent * (sigma * (1.0 + preact * (1.0 - sigma)))).astype(BF)
    for half in range(2):
        grad[half, 1, 1:9] = grad_pre[:, 128 * half : 128 * half + 128].reshape(8, 32, 128)

    row = lax.broadcasted_iota(jnp.int32, (256, 256), 0)
    column = lax.broadcasted_iota(jnp.int32, (256, 256), 1)
    q = row % 128
    source = (q // 32) * 64 + ((q // 4) % 8) * 8 + (row // 128) * 4 + q % 4
    order = jnp.where(column == source, 1.0, 0.0).astype(BF)
    turned = matmul_nt(order, grad_pre).astype(BF)
    grad_t_send[0] = turned[:128]
    grad_t_send[1] = turned[128:]
    grad_t[pl.ds(n, 1)] = grad_t_send[pl.ds(c, 1)]
    grad_shared = [
        send(GRAD_SHARE + d - 1, grad_t_send.at[(n + d) % 2], grad_t.at[n], near[d - 1])
        for d in range(1, 4)
    ]
    grad_halos = send_halos(grad, GRAD_HALO)

    for m in range(4):
        part = activated[:, 64 * m : 64 * m + 64]
        act_send[m] = jnp.concatenate([part[:128], part[128:]], axis=1)
    act_recv[pl.ds(n, 1)] = act_send[pl.ds(n, 1)]
    act_copies = [
        send(ACT + d - 1, act_send.at[(n + d) % 4], act_recv.at[n], near[d - 1]) for d in range(1, 4)
    ]

    for copy in grad_shared:
        copy.wait_recv()
    lane = lax.broadcasted_iota(jnp.int32, (128, 256), 1) % 32
    for m in range(4):
        block = grad_t[m].astype(F32)
        at = 256 * m
        grad_rows[0:128, at : at + 256] = jnp.where(lane == 31, 0.0, pltpu.roll(block, 255, 1)).astype(BF)
        grad_rows[128:256, at : at + 256] = grad_t[m]
        grad_rows[256:384, at : at + 256] = jnp.where(lane == 0, 0.0, pltpu.roll(block, 1, 1)).astype(BF)
    conv_y = {}
    for i in (1, 0, 2):
        for copy in shared[i]:
            copy.wait_recv()
        slab = jnp.concatenate([deep_all[i, j : j + 32].reshape(1024, 128) for j in range(3)], axis=1)
        term = matmul(grad_rows[...], slab).astype(BF)
        for yy in range(NY):
            for k in range(3):
                at = 128 * k + 32 * yy
                cy_send[i, yy, k] = term[at : at + 32]
        conv_y[i] = [
            send(CONV_Y + 3 * i + d - 1, cy_send.at[i, (y + d) % NY], cy_recv.at[i, d - 1], ys[d - 1])
            for d in range(1, NY)
        ]

    for i in (1, 2, 0):
        plane = 2 - i
        if i == 1:
            rows_arrive(grad, grad_halos, 1)
        else:
            plane_arrives(grad, grad_halos, plane)
        slab = jnp.concatenate(
            window(grad, plane, 2) + window(grad, plane, 1) + window(grad, plane, 0), axis=1
        )
        for k in range(3):
            weights = jnp.concatenate([cw[9 * i + 3 * j + k] for j in range(3)], axis=1)
            term = matmul_nt(slab, weights)
            acc[k] = term if i == 1 else acc[k] + term
    grad_deep = (shifted(acc[0], 255, 31) + acc[1] + shifted(acc[2], 1, 0)).astype(BF)

    partial = matmul(patches_t[...], grad_deep).reshape(32, 2, 2, 8, 256)
    for ll in range(2):
        for cc in range(2):
            for xx in range(2):
                dn_rows[ll, cc, :, 8 * xx : 8 * xx + 8] = partial[:, xx, ll, :, 128 * cc : 128 * cc + 128]
    dn_send[...] = dn_rows[...].astype(BF)
    down_n = [
        send(
            DOWN_N + d - 1,
            dn_send.at[((n + d) % 4) // 2, (n + d) % 2],
            dn_recv.at[d - 1],
            near[d - 1],
        )
        for d in range(1, 4)
    ]

    spread = matmul_nt(grad_deep, dw[...])
    for a in range(2):
        for b in range(2):
            for e in range(2):
                at = (4 * a + 2 * b + e) * 128
                wide_f32[a, :, b, pl.ds(e, 32, stride=2), :] = spread[:, at : at + 128].reshape(8, 32, 128)
    vg_out[...] = wide_f32[...].astype(BF)

    def conv_after_y(i):
        for copy in conv_y[i]:
            copy.wait_recv()
        total = cy_send[pl.ds(i, 1), pl.ds(y, 1)].reshape(3, 32, 384).astype(F32)
        for d in range(3):
            total = total + cy_recv[i, d].astype(F32)
        sum_rows[...] = total
        for zz in range(NZ):
            for k in range(3):
                z_rows[zz, 4 * k : 4 * k + 4] = sum_rows[k, 4 * zz : 4 * zz + 4]
        cz_send[i] = z_rows[...].astype(BF)
        return [
            send(CONV_Z + 7 * i + d - 1, cz_send.at[i, (z + d) % NZ], cz_recv.at[i, d - 1], zs[d - 1])
            for d in range(1, NZ)
        ]

    conv_z = {}
    conv_z[1] = conv_after_y(1)

    for copy in down_n:
        copy.wait_recv()
    total = dn_send[pl.ds(l, 1), pl.ds(c, 1)].reshape(32, 16, 128).astype(F32)
    for d in range(3):
        total = total + dn_recv[d].astype(F32)
    dy_send[...] = total.reshape(NY, NZ, 16, 128).astype(BF)
    down_y = [
        send(DOWN_Y + d - 1, dy_send.at[(y + d) % NY], dy_recv.at[d - 1], ys[d - 1]) for d in range(1, NY)
    ]

    conv_z[0] = conv_after_y(0)

    for copy in act_copies:
        copy.wait_recv()
    for m in range(4):
        act_out[256 * m : 256 * m + 128] = act_recv[m][:, :64]
        act_out[256 * m + 128 : 256 * m + 256] = act_recv[m][:, 64:]

    conv_z[2] = conv_after_y(2)

    for copy in down_y:
        copy.wait_recv()
    total = dy_send[pl.ds(y, 1)].reshape(NZ, 16, 128).astype(F32)
    for d in range(3):
        total = total + dy_recv[d].astype(F32)
    dz_send[...] = total.astype(BF)
    down_z = [
        send(DOWN_Z + d - 1, dz_send.at[(z + d) % NZ], dz_recv.at[d - 1], zs[d - 1]) for d in range(1, NZ)
    ]

    for i in (1, 0, 2):
        for copy in conv_z[i]:
            copy.wait_recv()
        total = cz_send[pl.ds(i, 1), pl.ds(z, 1)].reshape(16, 384).astype(F32)
        for d in range(7):
            total = total + cz_recv[i, d].astype(F32)
        last_send[:, 384 * i : 384 * i + 384] = total.astype(BF)
    for copy in down_z:
        copy.wait_recv()
    total = dz_send[pl.ds(z, 1)].reshape(16, 128).astype(F32)
    for d in range(7):
        total = total + dz_recv[d].astype(F32)
    last_send[:, 1152:1280] = total.astype(BF)
    last_copies = [send(LAST + s, last_send, last_recv.at[s], lasts[s]) for s in range(3)]
    for copy in last_copies:
        copy.wait_recv()

    same = last_send[...].astype(F32) + last_recv[0].astype(F32)
    crossed = last_recv[2].astype(F32) + last_recv[1].astype(F32)
    conv = jnp.where(c == xh, same, crossed) * factor
    for s in range(9):
        own = jnp.where(c == 0, conv[:, 128 * s : 128 * s + 64], conv[:, 128 * s + 64 : 128 * s + 128])
        for k in range(3):
            cg_out[3 * s + k] = own[4 * k : 4 * k + 4]
    same, crossed = same[:, 1152:], crossed[:, 1152:]
    both = jnp.concatenate(
        [jnp.where(c == 0, same, crossed), jnp.where(c == 0, crossed, same)], axis=1
    )
    mine = jnp.zeros((4, 256), F32)
    for s in range(4):
        mine = mine + jnp.where(2 * xh + c == s, both[4 * s : 4 * s + 4], 0.0)
    dg_out[...] = mine * factor

    for copy in started:
        copy.wait_send()


def on_device(volume, down_weight, conv_weight, cotangent):
    factor = 1.0 / (32 * math.sqrt(64))
    hbm = pl.BlockSpec(memory_space=pl.ANY)
    vmem = pl.BlockSpec(memory_space=pltpu.VMEM)
    scratch = [
        ((2, 8, 2, 64, 128), BF),
        ((1024, 256), BF),
        ((27, 256, 256), BF),
        ((4, 256, 64), BF),
        ((2, 8, 2, 64, 128), F32),
        ((256, 1024), BF),
        ((1024, 256), BF),
        ((2, 3, 10, 32, 128), BF),
        ((2, 3, 10, 32, 128), BF),
        ((3, 34, 32, 128), BF),
        ((2, 128, 256), BF),
        ((4, 128, 256), BF),
        ((384, 1024), BF),
        ((3, 256, 256), F32),
        ((4, 128, 128), BF),
        ((4, 128, 128), BF),
        ((4, 128, 128), BF),
        ((4, 128, 128), BF),
        ((3, 4, 3, 32, 384), BF),
        ((3, 3, 3, 32, 384), BF),
        ((3, 32, 384), F32),
        ((8, 16, 384), F32),
        ((3, 8, 16, 384), BF),
        ((3, 7, 16, 384), BF),
        ((2, 2, 32, 16, 128), F32),
        ((2, 2, 32, 16, 128), BF),
        ((3, 32, 16, 128), BF),
        ((4, 8, 16, 128), BF),
        ((3, 8, 16, 128), BF),
        ((8, 16, 128), BF),
        ((7, 16, 128), BF),
        ((16, 1280), BF),
        ((3, 16, 1280), BF),
    ]
    activated, volume_grad, down_grad, conv_grad = pl.pallas_call(
        functools.partial(kernel, factor),
        name="unet_level",
        out_shape=(
            jax.ShapeDtypeStruct((1024, 64), BF),
            jax.ShapeDtypeStruct((2, 8, 2, 64, 128), BF),
            jax.ShapeDtypeStruct((4, 256), F32),
            jax.ShapeDtypeStruct((27, 4, 64), F32),
        ),
        in_specs=[hbm] * 4,
        out_specs=(vmem,) * 4,
        scratch_shapes=[pltpu.VMEM(shape, dtype) for shape, dtype in scratch]
        + [
            pltpu.SemaphoreType.DMA((4,)),
            pltpu.SemaphoreType.DMA((MESSAGES,)),
            pltpu.SemaphoreType.DMA((MESSAGES,)),
        ],
        compiler_params=pltpu.CompilerParams(
            collective_id=0, has_side_effects=True, vmem_limit_bytes=48 * 1024 * 1024
        ),
        cost_estimate=pl.CostEstimate(flops=3200000000, bytes_accessed=8000000, transcendentals=65536),
    )(
        volume.reshape(2, 8, 2, 64, 128),
        down_weight,
        conv_weight,
        cotangent.reshape(4, 256, 64),
    )
    return (
        activated.reshape(1, 32, 32, 64),
        volume_grad.reshape(2, 16, 64, 128),
        down_grad,
        conv_grad.transpose(0, 2, 1),
    )


def solution(mesh):
    placed = (P("wide", "narrow", None, None), P(), P(), P("wide", None, None, "narrow"))
    return jax.shard_map(
        on_device,
        mesh=mesh,
        in_specs=placed,
        out_specs=(
            P("wide", None, None, "narrow"),
            P("wide", "narrow", None, None),
            P(("wide", "narrow"), None),
            P(None, "narrow", "wide"),
        ),
        check_vma=False,
    )
```

```python
import functools
import math

import jax
import jax.numpy as jnp
from jax import lax
from jax.experimental import pallas as pl
from jax.experimental.pallas import tpu as pltpu
from jax.sharding import PartitionSpec as P

MESH = pl.DeviceIdType.MESH
BF = jnp.bfloat16
F32 = jnp.float32
NY, NZ = 4, 8

COT = 0
DEEP_HALO = 3
DEEP_SHARE = 11
ACT = 20
GRAD_HALO = 23
GRAD_SHARE = 31
CONV_Y = 34
CONV_Z = 43
DOWN_C = 64
DOWN_X = 65
DOWN_Y = 68
DOWN_Z = 71
DOWN_LAST = 78
CONV_LAST = 79
MESSAGES = 82


def matmul(a, b):
    return jnp.dot(a, b, preferred_element_type=F32)


def matmul_nt(a, b):
    return lax.dot_general(a, b, (((1,), (1,)), ((), ())), preferred_element_type=F32)


def kernel(
    factor,
    vol_ref,
    dw_ref,
    cw_ref,
    cot_ref,
    act_out,
    vg_out,
    dg_out,
    cg_out,
    vol,
    dw,
    cw,
    cot,
    wide_f32,
    patches,
    patches_t,
    deep,
    grad,
    deep_all,
    grad_t_send,
    grad_t,
    grad_rows,
    acc,
    cot_send,
    cot_recv,
    act_send,
    act_recv,
    cy_send,
    cy_recv,
    sum_rows,
    z_rows,
    cz_send,
    cz_recv,
    dc_send,
    dc_recv,
    dx_rows,
    dx_send,
    dx_recv,
    dy_send,
    dy_recv,
    dz_send,
    dz_recv,
    dl_send,
    dl_recv,
    last_send,
    last_recv,
    local_sem,
    send_sem,
    recv_sem,
):
    w = lax.axis_index("wide")
    n = lax.axis_index("narrow")
    y, z, xh = w // 16, (w // 2) % NZ, w % 2
    l, c = n // 2, n % 2

    def wide_of(yy, zz, xx):
        return ((yy % NY) * NZ + zz % NZ) * 2 + xx

    near = [(w, (n + d) % 4) for d in range(1, 4)]
    up, down = (w + 1) % 64, (w + 63) % 64
    right, left = (n + 1) % 4, (n + 3) % 4
    depth = [(s, m) for s in (up, down) for m in (n, right, left)]
    ys = [(wide_of(y + d, z, xh), n) for d in range(1, NY)]
    zs = [(wide_of(y, z + d, xh), n) for d in range(1, NZ)]
    other_c = n + 1 - 2 * c
    across = wide_of(y, z, 1 - xh)
    other_l = (n + 2) % 4
    xs = [(across, n), (w, other_l), (across, other_l)]
    lasts = [(across, n), (across, other_c), (w, other_c)]

    barrier = pltpu.get_barrier_semaphore()
    partners = near + depth + ys + zs + [(across, n), (across, other_c), (across, other_l)]
    for who in partners:
        pl.semaphore_signal(barrier, inc=1, device_id=who, device_id_type=MESH)

    started = []

    def remote(number, src, dst, who):
        return pltpu.make_async_remote_copy(
            src_ref=src,
            dst_ref=dst,
            send_sem=send_sem.at[number],
            recv_sem=recv_sem.at[number],
            device_id=who,
            device_id_type=MESH,
        )

    def send(number, src, dst, who):
        copy = remote(number, src, dst, who)
        copy.start()
        started.append(copy)
        return copy

    loads = [
        pltpu.make_async_copy(src, dst, local_sem.at[s])
        for s, (src, dst) in enumerate(((cot_ref, cot), (vol_ref, vol), (dw_ref, dw), (cw_ref, cw)))
    ]
    for copy in loads:
        copy.start()

    deep_all[:, 0:1] = jnp.zeros((3, 1, 32, 128), BF)
    deep_all[:, 33:34] = jnp.zeros((3, 1, 32, 128), BF)
    z_rows[...] = jnp.zeros_like(z_rows)

    def send_halos(buf, base):
        copies = []
        for s, (to, plane) in enumerate(((up, 0), (down, 2))):
            copies.append(
                send(base + s, buf.at[:, 1, pl.ds(1, 8)], buf.at[:, plane, pl.ds(1, 8)], (to, n))
            )
        for s, (to, plane) in enumerate(((w, 1), (up, 0), (down, 2))):
            copies.append(
                send(base + 2 + 2 * s, buf.at[:, 1, pl.ds(8, 1)], buf.at[:, plane, pl.ds(0, 1)], (to, right))
            )
            copies.append(
                send(base + 3 + 2 * s, buf.at[:, 1, pl.ds(1, 1)], buf.at[:, plane, pl.ds(9, 1)], (to, left))
            )
        return copies

    def rows_arrive(buf, copies, plane):
        s = {1: 0, 0: 1, 2: 2}[plane]
        copies[2 + 2 * s].wait_recv()
        copies[3 + 2 * s].wait_recv()

        @pl.when(n == 0)
        def _():
            buf[:, plane, 0:1] = jnp.zeros((2, 1, 32, 128), BF)

        @pl.when(n == 3)
        def _():
            buf[:, plane, 9:10] = jnp.zeros((2, 1, 32, 128), BF)

    def plane_arrives(buf, copies, plane):
        copies[0 if plane == 0 else 1].wait_recv()
        rows_arrive(buf, copies, plane)

        @pl.when(w == (0 if plane == 0 else 63))
        def _():
            buf[:, plane] = jnp.zeros((2, 10, 32, 128), BF)

    loads[0].wait()
    for m in range(4):
        cot_send[m] = jnp.concatenate([cot[m, :128], cot[m, 128:]], axis=1)
    cot_recv[pl.ds(n, 1)] = cot_send[pl.ds(n, 1)]
    loads[1].wait()
    wide_f32[...] = vol[...].astype(F32)
    for a in range(2):
        for b in range(2):
            for e in range(2):
                part = wide_f32[a, :, b, pl.ds(e, 32, stride=2), :].reshape(256, 128).astype(BF)
                at = (4 * a + 2 * b + e) * 128
                patches[:, at : at + 128] = part
    loads[2].wait()
    cells = matmul(patches[...], dw[...]).astype(BF)
    for half in range(2):
        deep[half, 1, 1:9] = cells[:, 128 * half : 128 * half + 128].reshape(8, 32, 128)

    def share_deep(plane):
        mine = pl.ds(1 + 8 * n, 8)
        deep_all[plane, mine] = deep[pl.ds(l, 1), plane, 1:9].reshape(8, 32, 128)
        return [
            send(DEEP_SHARE + 3 * plane, deep.at[1 - l, plane, pl.ds(1, 8)], deep_all.at[plane, mine], (w, other_l)),
            send(DEEP_SHARE + 3 * plane + 1, deep.at[l, plane, pl.ds(1, 8)], deep_all.at[plane, mine], (w, other_c)),
        ]

    def pass_on(plane):
        shared[plane][0].wait_recv()
        theirs = pl.ds(1 + 8 * other_l, 8)
        shared[plane].append(
            send(
                DEEP_SHARE + 3 * plane + 2,
                deep_all.at[plane, theirs],
                deep_all.at[plane, theirs],
                (w, other_c),
            )
        )

    pl.semaphore_wait(barrier, len(partners))
    deep_halos = send_halos(deep, DEEP_HALO)
    cot_copies = [
        send(COT + d - 1, cot_send.at[(n + d) % 4], cot_recv.at[n], near[d - 1]) for d in range(1, 4)
    ]
    shared = {}
    for s in range(4):
        block = patches[:, 256 * s : 256 * s + 256].astype(F32)
        patches_t[256 * s : 256 * s + 256, :] = block.T.astype(BF)

    def window(buf, plane, first):
        return [buf[half, plane, first : first + 8].reshape(256, 128) for half in range(2)]

    def shifted(value, by, masked):
        column = lax.broadcasted_iota(jnp.int32, value.shape, 0) % 32
        return jnp.where(column == masked, 0.0, pltpu.roll(value, by, 0))

    loads[3].wait()
    for i in (1, 0, 2):
        if i == 1:
            rows_arrive(deep, deep_halos, 1)
        else:
            plane_arrives(deep, deep_halos, i)
            shared[i] = share_deep(i)
        slab = jnp.concatenate(window(deep, i, 0) + window(deep, i, 1) + window(deep, i, 2), axis=1)
        for k in range(3):
            weights = jnp.concatenate([cw[9 * i + 3 * j + k] for j in range(3)], axis=0)
            term = matmul(slab, weights)
            acc[k] = term if i == 1 else acc[k] + term
        if i == 1:
            shared[1] = share_deep(1)
    preact = shifted(acc[0], 1, 0) + acc[1] + shifted(acc[2], 255, 31)

    for copy in cot_copies:
        copy.wait_recv()
    cotangent = jnp.concatenate(
        [
            jnp.concatenate([cot_recv[m][:, :64], cot_recv[m][:, 64:]], axis=0)
            for m in range(4)
        ],
        axis=1,
    ).astype(F32)
    sigma = 1.0 / (1.0 + jnp.exp(-preact))
    activated = (preact * sigma).astype(BF)
    grad_pre = (cotangent * (sigma * (1.0 + preact * (1.0 - sigma)))).astype(BF)
    for half in range(2):
        grad[half, 1, 1:9] = grad_pre[:, 128 * half : 128 * half + 128].reshape(8, 32, 128)

    row = lax.broadcasted_iota(jnp.int32, (256, 256), 0)
    column = lax.broadcasted_iota(jnp.int32, (256, 256), 1)
    q = row % 128
    source = (q // 32) * 64 + ((q // 4) % 8) * 8 + (row // 128) * 4 + q % 4
    order = jnp.where(column == source, 1.0, 0.0).astype(BF)
    turned = matmul_nt(order, grad_pre).astype(BF)
    grad_t_send[0] = turned[:128]
    grad_t_send[1] = turned[128:]
    grad_t[pl.ds(n, 1)] = grad_t_send[pl.ds(c, 1)]
    grad_shared = [
        send(GRAD_SHARE + d - 1, grad_t_send.at[(n + d) % 2], grad_t.at[n], near[d - 1])
        for d in range(1, 4)
    ]
    grad_halos = send_halos(grad, GRAD_HALO)

    for i in (1, 0, 2):
        pass_on(i)

    for copy in grad_shared:
        copy.wait_recv()
    lane = lax.broadcasted_iota(jnp.int32, (128, 256), 1) % 32
    for m in range(4):
        block = grad_t[m].astype(F32)
        at = 256 * m
        grad_rows[0:128, at : at + 256] = jnp.where(lane == 31, 0.0, pltpu.roll(block, 255, 1)).astype(BF)
        grad_rows[128:256, at : at + 256] = grad_t[m]
        grad_rows[256:384, at : at + 256] = jnp.where(lane == 0, 0.0, pltpu.roll(block, 1, 1)).astype(BF)
    conv_y = {}
    for i in (1, 0, 2):
        for copy in shared[i][1:]:
            copy.wait_recv()
        slab = jnp.concatenate([deep_all[i, j : j + 32].reshape(1024, 128) for j in range(3)], axis=1)
        term = matmul(grad_rows[...], slab).astype(BF)
        for yy in range(NY):
            for k in range(3):
                at = 128 * k + 32 * yy
                cy_send[i, yy, k] = term[at : at + 32]
        conv_y[i] = [
            send(CONV_Y + 3 * i + d - 1, cy_send.at[i, (y + d) % NY], cy_recv.at[i, d - 1], ys[d - 1])
            for d in range(1, NY)
        ]

    for i in (1, 2, 0):
        plane = 2 - i
        if i == 1:
            rows_arrive(grad, grad_halos, 1)
        else:
            plane_arrives(grad, grad_halos, plane)
        slab = jnp.concatenate(
            window(grad, plane, 2) + window(grad, plane, 1) + window(grad, plane, 0), axis=1
        )
        for k in range(3):
            weights = jnp.concatenate([cw[9 * i + 3 * j + k] for j in range(3)], axis=1)
            term = matmul_nt(slab, weights)
            acc[k] = term if i == 1 else acc[k] + term
    grad_deep = (shifted(acc[0], 255, 31) + acc[1] + shifted(acc[2], 1, 0)).astype(BF)

    partial = matmul(patches_t[...], grad_deep)
    low, high = partial[:, :128], partial[:, 128:]
    dc_send[...] = jnp.where(c == 0, high, low).astype(BF)
    down_c = send(DOWN_C, dc_send, dc_recv, (w, other_c))
    kept = jnp.where(c == 0, low, high)

    for m in range(4):
        part = activated[:, 64 * m : 64 * m + 64]
        act_send[m] = jnp.concatenate([part[:128], part[128:]], axis=1)
    act_recv[pl.ds(n, 1)] = act_send[pl.ds(n, 1)]
    act_copies = [
        send(ACT + d - 1, act_send.at[(n + d) % 4], act_recv.at[n], near[d - 1]) for d in range(1, 4)
    ]

    spread = matmul_nt(grad_deep, dw[...])
    for a in range(2):
        for b in range(2):
            for e in range(2):
                at = (4 * a + 2 * b + e) * 128
                wide_f32[a, :, b, pl.ds(e, 32, stride=2), :] = spread[:, at : at + 128].reshape(8, 32, 128)
    vg_out[...] = wide_f32[...].astype(BF)

    def conv_after_y(i):
        for copy in conv_y[i]:
            copy.wait_recv()
        total = cy_send[pl.ds(i, 1), pl.ds(y, 1)].reshape(3, 32, 384).astype(F32)
        for d in range(3):
            total = total + cy_recv[i, d].astype(F32)
        sum_rows[...] = total
        for zz in range(NZ):
            for k in range(3):
                z_rows[zz, 4 * k : 4 * k + 4] = sum_rows[k, 4 * zz : 4 * zz + 4]
        cz_send[i] = z_rows[...].astype(BF)
        return [
            send(CONV_Z + 7 * i + d - 1, cz_send.at[i, (z + d) % NZ], cz_recv.at[i, d - 1], zs[d - 1])
            for d in range(1, NZ)
        ]

    down_c.wait_recv()
    total = (kept + dc_recv[...].astype(F32)).reshape(16, 2, 2, 2, 8, 128)
    for xx in range(2):
        for ll in range(2):
            for zz in range(2):
                dx_rows[xx, ll, :, 8 * zz : 8 * zz + 8] = total[:, zz, xx, ll]
    dx_send[...] = dx_rows[...].astype(BF)
    down_x = [
        send(DOWN_X + s, dx_send.at[xx, ll], dx_recv.at[s], xs[s])
        for s, (xx, ll) in enumerate(((1 - xh, l), (xh, 1 - l), (1 - xh, 1 - l)))
    ]

    conv_z = {}
    conv_z[1] = conv_after_y(1)

    conv_z[0] = conv_after_y(0)

    conv_z[2] = conv_after_y(2)

    for copy in down_x:
        copy.wait_recv()
    total = dx_rows[pl.ds(xh, 1), pl.ds(l, 1)].reshape(16, 16, 128)
    for d in range(3):
        total = total + dx_recv[d].astype(F32)
    dy_send[...] = total.reshape(NY, 4, 16, 128).astype(BF)
    down_y = [
        send(DOWN_Y + d - 1, dy_send.at[(y + d) % NY], dy_recv.at[d - 1], ys[d - 1]) for d in range(1, NY)
    ]

    for copy in act_copies:
        copy.wait_recv()
    for m in range(4):
        act_out[256 * m : 256 * m + 128] = act_recv[m][:, :64]
        act_out[256 * m + 128 : 256 * m + 256] = act_recv[m][:, 64:]

    for copy in down_y:
        copy.wait_recv()
    total = dy_send[pl.ds(y, 1)].reshape(4, 16, 128).astype(F32)
    for d in range(3):
        total = total + dy_recv[d].astype(F32)
    dz_send[...] = total.reshape(NZ, 8, 128)
    down_z = [
        send(DOWN_Z + d - 1, dz_send.at[(z + d) % NZ], dz_recv.at[d - 1], zs[d - 1]) for d in range(1, NZ)
    ]

    for i in (1, 0, 2):
        for copy in conv_z[i]:
            copy.wait_recv()
        total = cz_send[pl.ds(i, 1), pl.ds(z, 1)].reshape(16, 384).astype(F32)
        for d in range(7):
            total = total + cz_recv[i, d].astype(F32)
        last_send[:, 384 * i : 384 * i + 384] = total.astype(BF)
    @pl.when(xh == c)
    def _():
        copy = remote(CONV_LAST + 2, last_send, last_recv.at[2], (w, other_c))
        copy.start()
        remote(CONV_LAST, last_send, last_recv.at[0], (across, n)).wait_recv()
        copy.wait_send()

    @pl.when(xh != c)
    def _():
        one = remote(CONV_LAST, last_send, last_recv.at[0], (across, n))
        two = remote(CONV_LAST + 1, last_send, last_recv.at[1], (across, other_c))
        one.start()
        two.start()
        two.wait_recv()
        remote(CONV_LAST + 2, last_send, last_recv.at[2], (w, other_c)).wait_recv()
        one.wait_send()
        two.wait_send()

    for copy in down_z:
        copy.wait_recv()
    total = dz_send[pl.ds(z, 1)].reshape(8, 128)
    for d in range(7):
        total = total + dz_recv[d]
    dl_send[...] = total
    down_last = send(DOWN_LAST, dl_send, dl_recv, (w, other_c))

    one = jnp.where(c == xh, last_send[...], last_recv[2])
    two = jnp.where(c == xh, last_recv[0], last_recv[1])
    conv = (one.astype(F32) + two.astype(F32)) * factor
    for s in range(9):
        own = jnp.where(c == 0, conv[:, 128 * s : 128 * s + 64], conv[:, 128 * s + 64 : 128 * s + 128])
        for k in range(3):
            cg_out[3 * s + k] = own[4 * k : 4 * k + 4]
    down_last.wait_recv()
    theirs = dl_recv[...]
    both = jnp.concatenate([jnp.where(c == 0, total, theirs), jnp.where(c == 0, theirs, total)], axis=1)
    dg_out[...] = jnp.where(c == 0, both[:4], both[4:]) * factor

    for copy in started:
        copy.wait_send()


def write_out(*refs):
    arrays = (len(refs) - 1) // 2
    sems = refs[-1]
    copies = [
        pltpu.make_async_copy(src, dst, sems.at[s])
        for s, (src, dst) in enumerate(zip(refs[:arrays], refs[arrays:-1]))
    ]
    for copy in copies:
        copy.start()
    for copy in copies:
        copy.wait()


def on_device(volume, down_weight, conv_weight, cotangent):
    factor = 1.0 / (32 * math.sqrt(64))
    hbm = pl.BlockSpec(memory_space=pltpu.HBM)
    vmem = pl.BlockSpec(memory_space=pltpu.VMEM)
    scratch = [
        ((2, 8, 2, 64, 128), BF),
        ((1024, 256), BF),
        ((27, 256, 256), BF),
        ((4, 256, 64), BF),
        ((2, 8, 2, 64, 128), F32),
        ((256, 1024), BF),
        ((1024, 256), BF),
        ((2, 3, 10, 32, 128), BF),
        ((2, 3, 10, 32, 128), BF),
        ((3, 34, 32, 128), BF),
        ((2, 128, 256), BF),
        ((4, 128, 256), BF),
        ((384, 1024), BF),
        ((3, 256, 256), F32),
        ((4, 128, 128), BF),
        ((4, 128, 128), BF),
        ((4, 128, 128), BF),
        ((4, 128, 128), BF),
        ((3, 4, 3, 32, 384), BF),
        ((3, 3, 3, 32, 384), BF),
        ((3, 32, 384), F32),
        ((8, 16, 384), F32),
        ((3, 8, 16, 384), BF),
        ((3, 7, 16, 384), BF),
        ((1024, 128), BF),
        ((1024, 128), BF),
        ((2, 2, 16, 16, 128), F32),
        ((2, 2, 16, 16, 128), BF),
        ((3, 16, 16, 128), BF),
        ((4, 4, 16, 128), BF),
        ((3, 4, 16, 128), BF),
        ((8, 8, 128), F32),
        ((7, 8, 128), F32),
        ((8, 128), F32),
        ((8, 128), F32),
        ((16, 1152), BF),
        ((3, 16, 1152), BF),
    ]
    results = pl.pallas_call(
        functools.partial(kernel, factor),
        name="unet_level",
        out_shape=(
            jax.ShapeDtypeStruct((1024, 64), BF),
            jax.ShapeDtypeStruct((2, 8, 2, 64, 128), BF),
            jax.ShapeDtypeStruct((4, 256), F32),
            jax.ShapeDtypeStruct((27, 4, 64), F32),
        ),
        in_specs=[hbm] * 4,
        out_specs=(vmem,) * 4,
        scratch_shapes=[pltpu.VMEM(shape, dtype) for shape, dtype in scratch]
        + [
            pltpu.SemaphoreType.DMA((4,)),
            pltpu.SemaphoreType.DMA((MESSAGES,)),
            pltpu.SemaphoreType.DMA((MESSAGES,)),
        ],
        compiler_params=pltpu.CompilerParams(
            collective_id=0, has_side_effects=True, vmem_limit_bytes=56 * 1024 * 1024
        ),
        cost_estimate=pl.CostEstimate(flops=3200000000, bytes_accessed=8000000, transcendentals=65536),
    )(
        volume.reshape(2, 8, 2, 64, 128),
        down_weight,
        conv_weight,
        cotangent.reshape(4, 256, 64),
    )
    activated, volume_grad, down_grad, conv_grad = pl.pallas_call(
        write_out,
        name="write_out",
        out_shape=tuple(jax.ShapeDtypeStruct(r.shape, r.dtype) for r in results),
        in_specs=[vmem] * 4,
        out_specs=(hbm,) * 4,
        scratch_shapes=[pltpu.SemaphoreType.DMA((4,))],
    )(*results)
    return (
        activated.reshape(1, 32, 32, 64),
        volume_grad.reshape(2, 16, 64, 128),
        down_grad,
        conv_grad.transpose(0, 2, 1),
    )


def solution(mesh):
    placed = (P("wide", "narrow", None, None), P(), P(), P("wide", None, None, "narrow"))
    return jax.shard_map(
        on_device,
        mesh=mesh,
        in_specs=placed,
        out_specs=(
            P("wide", None, None, "narrow"),
            P("wide", "narrow", None, None),
            P(("wide", "narrow"), None),
            P(None, "narrow", "wide"),
        ),
        check_vma=False,
    )
```

```python
import functools
import math

import jax
import jax.numpy as jnp
from jax import lax
from jax.experimental import pallas as pl
from jax.experimental.pallas import tpu as pltpu
from jax.sharding import PartitionSpec as P

MESH = pl.DeviceIdType.MESH
BF = jnp.bfloat16
F32 = jnp.float32
NY, NZ = 4, 8

COT = 0
DEEP_HALO = 3
DEEP_ACROSS = 11
DEEP_CORE = 13
ACT = 20
GRAD_HALO = 23
GRAD_SHARE = 31
CONV_Y = 35
CONV_YZ = 38
CONV_Z = 45
CONV_ZY = 52
DOWN_C = 55
DOWN_X = 56
DOWN_Y = 59
DOWN_Z = 62
DOWN_LAST = 69
CONV_LAST = 70
MESSAGES = 76


def matmul(a, b):
    return jnp.dot(a, b, preferred_element_type=F32)


def matmul_nt(a, b):
    return lax.dot_general(a, b, (((1,), (1,)), ((), ())), preferred_element_type=F32)


def kernel(
    factor,
    vol_ref,
    dw_ref,
    cw_ref,
    cot_ref,
    act_out,
    vg_out,
    dg_out,
    cg_out,
    vol,
    dw,
    cw,
    cot,
    wide_f32,
    patches,
    patches_t,
    deep,
    grad,
    deep_all,
    grad_t_send,
    grad_t,
    grad_rows,
    grad_rows_z,
    acc,
    cot_send,
    cot_recv,
    act_send,
    act_recv,
    cy_send,
    cy_recv,
    sum_rows,
    cyz_rows,
    cyz_send,
    cyz_recv,
    cz_send,
    cz_recv,
    czy_rows,
    czy_send,
    czy_recv,
    dc_send,
    dc_recv,
    dx_rows,
    dx_send,
    dx_recv,
    dy_send,
    dy_recv,
    dz_send,
    dz_recv,
    dl_send,
    dl_recv,
    last_sum,
    last_send,
    last_recv,
    local_sem,
    send_sem,
    recv_sem,
):
    w = lax.axis_index("wide")
    n = lax.axis_index("narrow")
    y, z, xh = w // 16, (w // 2) % NZ, w % 2
    l, c = n // 2, n % 2
    pair = z % 2

    def wide_of(yy, zz, xx):
        return ((yy % NY) * NZ + zz % NZ) * 2 + xx

    near = [(w, (n + d) % 4) for d in range(1, 4)]
    up, down = (w + 1) % 64, (w + 63) % 64
    right, left = (n + 1) % 4, (n + 3) % 4
    depth = [(s, (n + d) % 4) for s in (up, down) for d in range(4)]
    ys = [(wide_of(y + d, z, xh), n) for d in range(1, NY)]
    zs = [(wide_of(y, z + d, xh), n) for d in range(1, NZ)]
    other_c = n + 1 - 2 * c
    across = wide_of(y, z, 1 - xh)
    other_l = (n + 2) % 4
    beside = wide_of(y, z + 1 - 2 * pair, xh)
    xs = [(across, n), (w, other_l), (across, other_l)]

    barrier = pltpu.get_barrier_semaphore()
    partners = near + depth + ys + zs
    for who in partners:
        pl.semaphore_signal(barrier, inc=1, device_id=who, device_id_type=MESH)

    started = []

    def remote(number, src, dst, who):
        return pltpu.make_async_remote_copy(
            src_ref=src,
            dst_ref=dst,
            send_sem=send_sem.at[number],
            recv_sem=recv_sem.at[number],
            device_id=who,
            device_id_type=MESH,
        )

    def send(number, src, dst, who):
        copy = remote(number, src, dst, who)
        copy.start()
        started.append(copy)
        return copy

    loads = [
        pltpu.make_async_copy(src, dst, local_sem.at[s])
        for s, (src, dst) in enumerate(((cot_ref, cot), (vol_ref, vol), (dw_ref, dw), (cw_ref, cw)))
    ]
    for copy in loads:
        copy.start()

    cyz_rows[...] = jnp.zeros_like(cyz_rows)
    czy_rows[...] = jnp.zeros_like(czy_rows)

    def send_halos(buf, base):
        copies = []
        for s, (to, plane) in enumerate(((up, 0), (down, 2))):
            copies.append(
                send(base + s, buf.at[:, 1, pl.ds(1, 8)], buf.at[:, plane, pl.ds(1, 8)], (to, n))
            )
        for s, (to, plane) in enumerate(((w, 1), (up, 0), (down, 2))):
            copies.append(
                send(base + 2 + 2 * s, buf.at[:, 1, pl.ds(8, 1)], buf.at[:, plane, pl.ds(0, 1)], (to, right))
            )
            copies.append(
                send(base + 3 + 2 * s, buf.at[:, 1, pl.ds(1, 1)], buf.at[:, plane, pl.ds(9, 1)], (to, left))
            )
        return copies

    def rows_arrive(buf, copies, plane):
        s = {1: 0, 0: 1, 2: 2}[plane]
        copies[2 + 2 * s].wait_recv()
        copies[3 + 2 * s].wait_recv()

        @pl.when(n == 0)
        def _():
            buf[:, plane, 0:1] = jnp.zeros((2, 1, 32, 128), BF)

        @pl.when(n == 3)
        def _():
            buf[:, plane, 9:10] = jnp.zeros((2, 1, 32, 128), BF)

    def plane_arrives(buf, copies, plane):
        copies[0 if plane == 0 else 1].wait_recv()
        rows_arrive(buf, copies, plane)

        @pl.when(w == (0 if plane == 0 else 63))
        def _():
            buf[:, plane] = jnp.zeros((2, 10, 32, 128), BF)

    loads[0].wait()
    for m in range(4):
        cot_send[m] = jnp.concatenate([cot[m, :128], cot[m, 128:]], axis=1)
    cot_recv[pl.ds(n, 1)] = cot_send[pl.ds(n, 1)]
    loads[1].wait()
    wide_f32[...] = vol[...].astype(F32)
    for a in range(2):
        for b in range(2):
            for e in range(2):
                part = wide_f32[a, :, b, pl.ds(e, 32, stride=2), :].reshape(256, 128).astype(BF)
                at = (4 * a + 2 * b + e) * 128
                patches[:, at : at + 128] = part
    loads[2].wait()
    cells = matmul(patches[...], dw[...]).astype(BF)
    for half in range(2):
        deep[half, 1, 1:9] = cells[:, 128 * half : 128 * half + 128].reshape(8, 32, 128)

    from_rows, to_rows = pl.ds(c, 9), pl.ds(9 * c, 9)
    outer, inner = 2 * pair, 2 - 2 * pair

    def to_core(number, src, plane, chip):
        return remote(DEEP_CORE + number, src, deep_all.at[plane, chip, to_rows], (w, other_c))

    def share_core(plane):
        deep_all[plane, pl.ds(pair, 1), to_rows] = deep[pl.ds(pair, 1), plane, from_rows]
        copy = to_core(plane, deep.at[pair, plane, from_rows], plane, pair)
        copy.start()
        started.append(copy)
        return copy

    across_own = remote(
        DEEP_ACROSS, deep.at[1 - pair, 1, from_rows], deep_all.at[1, pair, to_rows], (beside, n)
    )
    across_outer = remote(
        DEEP_ACROSS + 1, deep.at[1 - pair, outer, from_rows], deep_all.at[outer, pair, to_rows], (beside, n)
    )
    theirs_own = deep_all.at[1, 1 - pair, to_rows]
    theirs_outer = deep_all.at[inner, 1 - pair, to_rows]
    pass_own = to_core(3, theirs_own, 1, 1 - pair)
    pass_outer = to_core(4, theirs_outer, inner, 1 - pair)
    inner_core = to_core(5, deep.at[pair, inner, from_rows], outer, 1 - pair)

    pl.semaphore_wait(barrier, len(partners))
    deep_halos = send_halos(deep, DEEP_HALO)
    cot_copies = [
        send(COT + d - 1, cot_send.at[(n + d) % 4], cot_recv.at[n], near[d - 1]) for d in range(1, 4)
    ]
    shared = []
    for s in range(4):
        block = patches[:, 256 * s : 256 * s + 256].astype(F32)
        patches_t[256 * s : 256 * s + 256, :] = block.T.astype(BF)

    def window(buf, plane, first):
        return [buf[half, plane, first : first + 8].reshape(256, 128) for half in range(2)]

    def shifted(value, by, masked):
        column = lax.broadcasted_iota(jnp.int32, value.shape, 0) % 32
        return jnp.where(column == masked, 0.0, pltpu.roll(value, by, 0))

    loads[3].wait()
    for i in (1, 0, 2):
        if i == 1:
            rows_arrive(deep, deep_halos, 1)
        else:
            plane_arrives(deep, deep_halos, i)
        shared.append(share_core(i))
        if i == 1:
            across_own.start()
        else:
            @pl.when(outer == i)
            def _():
                across_outer.start()

        slab = jnp.concatenate(window(deep, i, 0) + window(deep, i, 1) + window(deep, i, 2), axis=1)
        for k in range(3):
            weights = jnp.concatenate([cw[9 * i + 3 * j + k] for j in range(3)], axis=0)
            term = matmul(slab, weights)
            acc[k] = term if i == 1 else acc[k] + term
    deep_all[pl.ds(outer, 1), pl.ds(1 - pair, 1), to_rows] = deep[pl.ds(pair, 1), pl.ds(inner, 1), from_rows]
    inner_core.start()
    preact = shifted(acc[0], 1, 0) + acc[1] + shifted(acc[2], 255, 31)

    for copy in cot_copies:
        copy.wait_recv()
    cotangent = jnp.concatenate(
        [
            jnp.concatenate([cot_recv[m][:, :64], cot_recv[m][:, 64:]], axis=0)
            for m in range(4)
        ],
        axis=1,
    ).astype(F32)
    sigma = 1.0 / (1.0 + jnp.exp(-preact))
    activated = (preact * sigma).astype(BF)
    grad_pre = (cotangent * (sigma * (1.0 + preact * (1.0 - sigma)))).astype(BF)
    for half in range(2):
        grad[half, 1, 1:9] = grad_pre[:, 128 * half : 128 * half + 128].reshape(8, 32, 128)

    row = lax.broadcasted_iota(jnp.int32, (256, 256), 0)
    column = lax.broadcasted_iota(jnp.int32, (256, 256), 1)
    q = row % 128
    source = (q // 32) * 64 + ((q // 4) % 8) * 8 + (row // 128) * 4 + q % 4
    order = jnp.where(column == source, 1.0, 0.0).astype(BF)
    turned = matmul_nt(order, grad_pre).astype(BF)
    grad_t_send[0] = turned[:128]
    grad_t_send[1] = turned[128:]
    slot = 2 * pair + c
    grad_t[pl.ds(slot, 1)] = grad_t_send[pl.ds(c, 1)]
    mine = grad_t.at[slot]
    grad_shared = [
        send(GRAD_SHARE, grad_t_send.at[1 - c], mine, (beside, other_c)),
        send(GRAD_SHARE + 1, grad_t_send.at[c], mine, (beside, n)),
        send(GRAD_SHARE + 2, grad_t_send.at[1 - c], mine, (w, other_c)),
    ]
    grad_halos = send_halos(grad, GRAD_HALO)

    across_own.wait_recv()
    pass_own.start()
    across_outer.wait_recv()
    pass_outer.start()
    started.extend([across_own, across_outer, pass_own, pass_outer, inner_core])
    shared.extend([pass_own, pass_outer, inner_core])

    for copy in grad_shared:
        copy.wait_recv()
    lane = lax.broadcasted_iota(jnp.int32, (128, 256), 1) % 32
    for m in range(4):
        block = grad_t[m].astype(F32)
        at = 256 * m
        grad_rows[0:128, at : at + 256] = jnp.where(lane == 31, 0.0, pltpu.roll(block, 255, 1)).astype(BF)
        grad_rows[128:256, at : at + 256] = grad_t[m]
        grad_rows[256:384, at : at + 256] = jnp.where(lane == 0, 0.0, pltpu.roll(block, 1, 1)).astype(BF)
    def cells_at(i, j):
        return jnp.concatenate([deep_all[i, s, j : j + 16].reshape(512, 128) for s in range(2)], axis=0)

    for copy in shared:
        copy.wait_recv()
    slab = jnp.concatenate([cells_at(i, j) for i in range(2) for j in range(3)], axis=1)
    term = matmul(grad_rows[...], slab).astype(BF)
    for yy in range(NY):
        for k in range(3):
            at = 128 * k + 32 * yy
            cy_send[yy, k] = term[at : at + 32]
    conv_y = [
        send(CONV_Y + d - 1, cy_send.at[(y + d) % NY], cy_recv.at[d - 1], ys[d - 1]) for d in range(1, NY)
    ]
    row = lax.broadcasted_iota(jnp.int32, (128, 128), 0)
    column = lax.broadcasted_iota(jnp.int32, (128, 128), 1)
    source = ((row // 4) % 4) * 32 + (row // 16) * 4 + row % 4
    order = jnp.where(column == source, 1.0, 0.0).astype(BF)
    for k in range(3):
        grad_rows_z[128 * k : 128 * k + 128, :] = matmul(order, grad_rows[128 * k : 128 * k + 128, :]).astype(BF)
    slab = jnp.concatenate([cells_at(2, j) for j in range(3)], axis=1)
    term = matmul(grad_rows_z[...], slab).astype(BF)
    for zz in range(NZ):
        for k in range(3):
            at = 128 * k + 16 * zz
            cz_send[zz, k] = term[at : at + 16]
    conv_z = [
        send(CONV_Z + d - 1, cz_send.at[(z + d) % NZ], cz_recv.at[d - 1], zs[d - 1]) for d in range(1, NZ)
    ]

    for i in (1, 2, 0):
        plane = 2 - i
        if i == 1:
            rows_arrive(grad, grad_halos, 1)
        else:
            plane_arrives(grad, grad_halos, plane)
        slab = jnp.concatenate(
            window(grad, plane, 2) + window(grad, plane, 1) + window(grad, plane, 0), axis=1
        )
        for k in range(3):
            weights = jnp.concatenate([cw[9 * i + 3 * j + k] for j in range(3)], axis=1)
            term = matmul_nt(slab, weights)
            acc[k] = term if i == 1 else acc[k] + term
    grad_deep = (shifted(acc[0], 255, 31) + acc[1] + shifted(acc[2], 1, 0)).astype(BF)

    partial = matmul(patches_t[...], grad_deep)
    low, high = partial[:, :128], partial[:, 128:]
    dc_send[...] = jnp.where(c == 0, high, low).astype(BF)
    down_c = send(DOWN_C, dc_send, dc_recv, (w, other_c))
    kept = jnp.where(c == 0, low, high)

    for m in range(4):
        part = activated[:, 64 * m : 64 * m + 64]
        act_send[m] = jnp.concatenate([part[:128], part[128:]], axis=1)
    act_recv[pl.ds(n, 1)] = act_send[pl.ds(n, 1)]
    act_copies = [
        send(ACT + d - 1, act_send.at[(n + d) % 4], act_recv.at[n], near[d - 1]) for d in range(1, 4)
    ]

    spread = matmul_nt(grad_deep, dw[...])
    for a in range(2):
        for b in range(2):
            for e in range(2):
                at = (4 * a + 2 * b + e) * 128
                wide_f32[a, :, b, pl.ds(e, 32, stride=2), :] = spread[:, at : at + 128].reshape(8, 32, 128)
    vg_out[...] = wide_f32[...].astype(BF)

    down_c.wait_recv()
    total = (kept + dc_recv[...].astype(F32)).reshape(16, 2, 2, 2, 8, 128)
    for xx in range(2):
        for ll in range(2):
            for zz in range(2):
                dx_rows[xx, ll, :, 8 * zz : 8 * zz + 8] = total[:, zz, xx, ll]
    dx_send[...] = dx_rows[...].astype(BF)
    down_x = [
        send(DOWN_X + s, dx_send.at[xx, ll], dx_recv.at[s], xs[s])
        for s, (xx, ll) in enumerate(((1 - xh, l), (xh, 1 - l), (1 - xh, 1 - l)))
    ]

    for copy in conv_y:
        copy.wait_recv()
    total = cy_send[pl.ds(y, 1)].reshape(3, 32, 768).astype(F32)
    for d in range(3):
        total = total + cy_recv[d].astype(F32)
    sum_rows[...] = total
    for zz in range(NZ):
        for k in range(3):
            cyz_rows[zz, 4 * k : 4 * k + 4] = sum_rows[k, 4 * zz : 4 * zz + 4]
    cyz_send[...] = cyz_rows[...].astype(BF)
    conv_yz = [
        send(CONV_YZ + d - 1, cyz_send.at[(z + d) % NZ], cyz_recv.at[d - 1], zs[d - 1]) for d in range(1, NZ)
    ]

    for copy in conv_z:
        copy.wait_recv()
    halves = [cz_send[pl.ds(z, 1)].reshape(3, 16, 384).astype(F32), 0.0]
    for d in range(1, NZ):
        halves[d % 2] = halves[d % 2] + cz_recv[d - 1].astype(F32)
    for h in range(2):
        sum_rows[:, :16, :384] = halves[h]
        for yy in range(NY):
            for k in range(3):
                czy_rows[yy, h, 4 * k : 4 * k + 4] = sum_rows[k, 4 * yy : 4 * yy + 4, :384]
    czy_send[...] = czy_rows[...].astype(BF)
    conv_zy = [
        send(CONV_ZY + d - 1, czy_send.at[(y + d) % NY], czy_recv.at[d - 1], ys[d - 1]) for d in range(1, NY)
    ]

    for copy in down_x:
        copy.wait_recv()
    total = dx_rows[pl.ds(xh, 1), pl.ds(l, 1)].reshape(16, 16, 128)
    for d in range(3):
        total = total + dx_recv[d].astype(F32)
    dy_send[...] = total.reshape(NY, 4, 16, 128).astype(BF)
    down_y = [
        send(DOWN_Y + d - 1, dy_send.at[(y + d) % NY], dy_recv.at[d - 1], ys[d - 1]) for d in range(1, NY)
    ]

    for copy in act_copies:
        copy.wait_recv()
    for m in range(4):
        act_out[256 * m : 256 * m + 128] = act_recv[m][:, :64]
        act_out[256 * m + 128 : 256 * m + 256] = act_recv[m][:, 64:]

    for copy in down_y:
        copy.wait_recv()
    total = dy_send[pl.ds(y, 1)].reshape(4, 16, 128).astype(F32)
    for d in range(3):
        total = total + dy_recv[d].astype(F32)
    dz_send[...] = total.reshape(NZ, 8, 128)
    down_z = [
        send(DOWN_Z + d - 1, dz_send.at[(z + d) % NZ], dz_recv.at[d - 1], zs[d - 1]) for d in range(1, NZ)
    ]

    for copy in conv_zy:
        copy.wait_recv()
    total = czy_send[pl.ds(y, 1)].reshape(2, 16, 384).astype(F32)
    for d in range(3):
        total = total + czy_recv[d].astype(F32)
    last_sum[pl.ds(pair, 1), :, 768:] = total[0:1]
    last_sum[pl.ds(1 - pair, 1), :, 768:] = total[1:2]
    for copy in conv_yz:
        copy.wait_recv()
    halves = [cyz_send[pl.ds(z, 1)].astype(F32), 0.0]
    for d in range(1, NZ):
        halves[d % 2] = halves[d % 2] + cyz_recv[d - 1 : d].astype(F32)
    last_sum[pl.ds(pair, 1), :, :768] = halves[0]
    last_sum[pl.ds(1 - pair, 1), :, :768] = halves[1]
    for h in range(2):
        whole = last_sum[h]
        for q in range(2):
            pieces = [whole[:, 128 * s + 64 * q : 128 * s + 64 * q + 64] for s in range(9)]
            last_send[h, q] = jnp.concatenate(pieces + [jnp.zeros((16, 64), F32)], axis=1).astype(BF)

    def last(slot, h, q, to, sent_by=None):
        return pltpu.make_async_remote_copy(
            src_ref=last_send.at[h, q],
            dst_ref=last_recv.at[slot],
            send_sem=send_sem.at[CONV_LAST + (slot if sent_by is None else sent_by)],
            recv_sem=recv_sem.at[CONV_LAST + slot],
            device_id=to,
            device_id_type=MESH,
        )

    near_l, far_l = 2 * l, 2 - 2 * l

    @pl.when(xh == c)
    def _():
        copies = [
            last(1, 1 - l, 0, (w, far_l)),
            last(1, 1 - l, 1, (w, far_l + 1), 4),
            last(0, l, 1 - c, (w, other_c)),
        ]
        for copy in copies:
            copy.start()
        for copy in copies:
            copy.wait_send()

    @pl.when(xh != c)
    def _():
        copies = [
            last(2, l, 0, (across, near_l)),
            last(2, l, 1, (across, near_l + 1), 4),
            last(3, 1 - l, 0, (across, far_l)),
            last(3, 1 - l, 1, (across, far_l + 1), 5),
        ]
        for copy in copies:
            copy.start()
        for copy in copies:
            copy.wait_send()
        last(0, l, c, (w, other_c)).wait_recv()

    for slot in range(1, 4):
        last(slot, l, c, (w, other_c)).wait_recv()

    for copy in down_z:
        copy.wait_recv()
    total = dz_send[pl.ds(z, 1)].reshape(8, 128)
    for d in range(7):
        total = total + dz_recv[d]
    dl_send[...] = total
    down_last = send(DOWN_LAST, dl_send, dl_recv, (w, other_c))

    own = last_send[pl.ds(l, 1), pl.ds(c, 1)].reshape(16, 640)
    conv = jnp.where(c == xh, own, last_recv[0]).astype(F32)
    for slot in range(1, 4):
        conv = conv + last_recv[slot].astype(F32)
    conv = conv * factor
    for s in range(9):
        for k in range(3):
            cg_out[3 * s + k] = conv[4 * k : 4 * k + 4, 64 * s : 64 * s + 64]
    down_last.wait_recv()
    theirs = dl_recv[...]
    both = jnp.concatenate([jnp.where(c == 0, total, theirs), jnp.where(c == 0, theirs, total)], axis=1)
    dg_out[...] = jnp.where(c == 0, both[:4], both[4:]) * factor

    for copy in started:
        copy.wait_send()


def write_out(*refs):
    arrays = (len(refs) - 1) // 2
    sems = refs[-1]
    copies = [
        pltpu.make_async_copy(src, dst, sems.at[s])
        for s, (src, dst) in enumerate(zip(refs[:arrays], refs[arrays:-1]))
    ]
    for copy in copies:
        copy.start()
    for copy in copies:
        copy.wait()


def on_device(volume, down_weight, conv_weight, cotangent):
    factor = 1.0 / (32 * math.sqrt(64))
    hbm = pl.BlockSpec(memory_space=pltpu.HBM)
    vmem = pl.BlockSpec(memory_space=pltpu.VMEM)
    scratch = [
        ((2, 8, 2, 64, 128), BF),
        ((1024, 256), BF),
        ((27, 256, 256), BF),
        ((4, 256, 64), BF),
        ((2, 8, 2, 64, 128), F32),
        ((256, 1024), BF),
        ((1024, 256), BF),
        ((2, 3, 10, 32, 128), BF),
        ((2, 3, 10, 32, 128), BF),
        ((3, 2, 18, 32, 128), BF),
        ((2, 128, 256), BF),
        ((4, 128, 256), BF),
        ((384, 1024), BF),
        ((384, 1024), BF),
        ((3, 256, 256), F32),
        ((4, 128, 128), BF),
        ((4, 128, 128), BF),
        ((4, 128, 128), BF),
        ((4, 128, 128), BF),
        ((4, 3, 32, 768), BF),
        ((3, 3, 32, 768), BF),
        ((3, 32, 768), F32),
        ((8, 16, 768), F32),
        ((8, 16, 768), BF),
        ((7, 16, 768), BF),
        ((8, 3, 16, 384), BF),
        ((7, 3, 16, 384), BF),
        ((4, 2, 16, 384), F32),
        ((4, 2, 16, 384), BF),
        ((3, 2, 16, 384), BF),
        ((1024, 128), BF),
        ((1024, 128), BF),
        ((2, 2, 16, 16, 128), F32),
        ((2, 2, 16, 16, 128), BF),
        ((3, 16, 16, 128), BF),
        ((4, 4, 16, 128), BF),
        ((3, 4, 16, 128), BF),
        ((8, 8, 128), F32),
        ((7, 8, 128), F32),
        ((8, 128), F32),
        ((8, 128), F32),
        ((2, 16, 1152), F32),
        ((2, 2, 16, 640), BF),
        ((4, 16, 640), BF),
    ]
    results = pl.pallas_call(
        functools.partial(kernel, factor),
        name="unet_level",
        out_shape=(
            jax.ShapeDtypeStruct((1024, 64), BF),
            jax.ShapeDtypeStruct((2, 8, 2, 64, 128), BF),
            jax.ShapeDtypeStruct((4, 256), F32),
            jax.ShapeDtypeStruct((27, 4, 64), F32),
        ),
        in_specs=[hbm] * 4,
        out_specs=(vmem,) * 4,
        scratch_shapes=[pltpu.VMEM(shape, dtype) for shape, dtype in scratch]
        + [
            pltpu.SemaphoreType.DMA((4,)),
            pltpu.SemaphoreType.DMA((MESSAGES,)),
            pltpu.SemaphoreType.DMA((MESSAGES,)),
        ],
        compiler_params=pltpu.CompilerParams(
            collective_id=0, has_side_effects=True, vmem_limit_bytes=56 * 1024 * 1024
        ),
        cost_estimate=pl.CostEstimate(flops=3200000000, bytes_accessed=8000000, transcendentals=65536),
    )(
        volume.reshape(2, 8, 2, 64, 128),
        down_weight,
        conv_weight,
        cotangent.reshape(4, 256, 64),
    )
    activated, volume_grad, down_grad, conv_grad = pl.pallas_call(
        write_out,
        name="write_out",
        out_shape=tuple(jax.ShapeDtypeStruct(r.shape, r.dtype) for r in results),
        in_specs=[vmem] * 4,
        out_specs=(hbm,) * 4,
        scratch_shapes=[pltpu.SemaphoreType.DMA((4,))],
    )(*results)
    return (
        activated.reshape(1, 32, 32, 64),
        volume_grad.reshape(2, 16, 64, 128),
        down_grad,
        conv_grad.transpose(0, 2, 1),
    )


def solution(mesh):
    placed = (P("wide", "narrow", None, None), P(), P(), P("wide", None, None, "narrow"))
    return jax.shard_map(
        on_device,
        mesh=mesh,
        in_specs=placed,
        out_specs=(
            P("wide", None, None, "narrow"),
            P("wide", "narrow", None, None),
            P(("wide", "narrow"), None),
            P(None, "narrow", "wide"),
        ),
        check_vma=False,
    )
```

```python
import functools
import math

import jax
import jax.numpy as jnp
from jax import lax
from jax.experimental import pallas as pl
from jax.experimental.pallas import tpu as pltpu
from jax.sharding import PartitionSpec as P

MESH = pl.DeviceIdType.MESH
BF = jnp.bfloat16
F32 = jnp.float32
Y_TAPS = ((0, 0), (0, 1), (0, 2), (1, 0), (1, 1), (1, 2))
Z_TAPS = ((2, 0), (2, 1), (2, 2))
YL, ZL = 128 * len(Y_TAPS), 128 * len(Z_TAPS)
NY, NZ = 4, 8

COT, DEEP_ROWS, DEEP_LOW, DEEP_HIGH, DEEP_OWN, DEEP_OUTER, DEEP_CORE, ACT = range(8)
GRAD_ROWS, GRAD_LOW, GRAD_HIGH, GRAD_SHARE, CONV_Y, CONV_YZ, CONV_Z, CONV_ZY = range(8, 16)
DOWN_C, DOWN_XY, DOWN_Z, DOWN_LAST, CONV_LAST, CONV_CORE = range(16, 22)
GROUPS = 22
Y_BLOCKS, Z_BLOCKS = -(-3 * len(Y_TAPS) // 4), -(-3 * len(Z_TAPS) // 4)


def matmul(a, b):
    return jnp.dot(a, b, preferred_element_type=F32)


def matmul_nt(a, b):
    return lax.dot_general(a, b, (((1,), (1,)), ((), ())), preferred_element_type=F32)


def kernel(
    factor,
    vol_ref,
    dw_ref,
    cw_ref,
    cot_ref,
    act_out,
    vg_out,
    dg_out,
    cg_out,
    vol,
    dw,
    cw,
    cot,
    wide_f32,
    patches,
    patches_t,
    deep,
    grad,
    deep_all,
    grad_t_send,
    grad_t,
    grad_rows,
    grad_rows_z,
    acc,
    cot_send,
    cot_recv,
    act_send,
    act_recv,
    act_vmem,
    cy_send,
    cy_recv,
    sum_rows,
    cyz_rows,
    cyz_send,
    cyz_recv,
    cz_send,
    cz_recv,
    czy_rows,
    czy_send,
    czy_recv,
    dc_send,
    dc_recv,
    dx_rows,
    dx_send,
    dx_recv,
    dz_send,
    dz_recv,
    dl_send,
    dl_recv,
    cg_vmem,
    dg_vmem,
    last_sum,
    last_send,
    last_recv,
    local_sem,
    send_sem,
    recv_sem,
):
    w = lax.axis_index("wide")
    n = lax.axis_index("narrow")
    y, z, xh = w // 16, (w // 2) % NZ, w % 2
    l, c = n // 2, n % 2
    pair = z % 2

    def wide_of(yy, zz, xx):
        return ((yy % NY) * NZ + zz % NZ) * 2 + xx

    near = [(w, (n + d) % 4) for d in range(1, 4)]
    up, down = (w + 1) % 64, (w + 63) % 64
    right, left = (n + 1) % 4, (n + 3) % 4
    depth = [(s, (n + d) % 4) for s in (up, down) for d in range(4)]
    ys = [(wide_of(y + d, z, xh), n) for d in range(1, NY)]
    zs = [(wide_of(y, z + d, xh), n) for d in range(1, NZ)]
    other_c = n + 1 - 2 * c
    across = wide_of(y, z, 1 - xh)
    other_l = (n + 2) % 4
    beside = wide_of(y, z + 1 - 2 * pair, xh)
    xys = [
        (dy, dx, dl, (wide_of(y + dy, z, (xh + dx) % 2), n + 2 * dl * (1 - 2 * l)))
        for dy in range(NY)
        for dx in range(2)
        for dl in range(2)
        if dy or dx or dl
    ]

    barrier = pltpu.get_barrier_semaphore()
    partners = near + depth + ys + zs + [to for dy, dx, dl, to in xys if dy and (dx or dl)]
    for who in partners:
        pl.semaphore_signal(barrier, inc=1, device_id=who, device_id_type=MESH)

    def remote(number, src, dst, who, received=None):
        return pltpu.make_async_remote_copy(
            src_ref=src,
            dst_ref=dst,
            send_sem=send_sem.at[number],
            recv_sem=recv_sem.at[number if received is None else received],
            device_id=who,
            device_id_type=MESH,
        )

    def send(*args, **kwargs):
        remote(*args, **kwargs).start()

    def arrived(number, ref):
        remote(number, ref, ref, near[0]).wait_recv()

    outgoing = []

    def sent(number, ref):
        outgoing.append(remote(number, ref, ref, near[0]))

    loads = [
        pltpu.make_async_copy(src, dst, local_sem.at[s])
        for s, (src, dst) in enumerate(((vol_ref, vol), (dw_ref, dw), (cot_ref, cot), (cw_ref, cw)))
    ]
    for copy in loads:
        copy.start()

    def send_halos(buf, base):
        def rows(to, plane, received):
            for who, first, at in ((right, 8, 0), (left, 1, 9)):
                src = buf.at[:, 1, pl.ds(first, 1)]
                send(base, src, buf.at[:, plane, pl.ds(at, 1)], (to, who), received=received)

        rows(w, 1, base)
        for s, (to, plane) in enumerate(((up, 0), (down, 2))):
            planes = buf.at[:, plane, pl.ds(1, 8)]
            send(base + 1, buf.at[:, 1, pl.ds(1, 8)], planes, (to, n), received=base + 1 + s)
            rows(to, plane, base + 1 + s)
        sent(base, buf.at[:, 1, pl.ds(0, 6)])
        sent(base + 1, buf.at[:, pl.ds(0, 2), pl.ds(0, 8)])

    def clear_rows(buf, plane):
        @pl.when(n == 0)
        def _():
            buf[:, plane, 0:1] = jnp.zeros((2, 1, 32, 128), BF)

        @pl.when(n == 3)
        def _():
            buf[:, plane, 9:10] = jnp.zeros((2, 1, 32, 128), BF)

    def rows_arrive(buf, base):
        arrived(base, buf.at[:, 1, pl.ds(0, 2)])
        clear_rows(buf, 1)

    def plane_arrives(buf, base, plane):
        arrived(base + 1 + plane // 2, buf.at[:, plane])
        clear_rows(buf, plane)

        @pl.when(w == (0 if plane == 0 else 63))
        def _():
            buf[:, plane] = jnp.zeros((2, 10, 32, 128), BF)

    loads[0].wait()
    wide_f32[...] = vol[...].astype(F32)
    for a in range(2):
        for b in range(2):
            for e in range(2):
                part = wide_f32[a, :, b, pl.ds(e, 32, stride=2), :].reshape(256, 128).astype(BF)
                at = (4 * a + 2 * b + e) * 128
                patches[:, at : at + 128] = part
    loads[1].wait()
    cells = matmul(patches[...], dw[...]).astype(BF)
    for half in range(2):
        deep[half, 1, 1:9] = cells[:, 128 * half : 128 * half + 128].reshape(8, 32, 128)

    from_rows, to_rows = pl.ds(c, 9), pl.ds(9 * c, 9)
    outer, inner = 2 * pair, 2 - 2 * pair

    def to_core(src, plane, chip):
        send(DEEP_CORE, src, deep_all.at[plane, chip, to_rows], (w, other_c))

    def share_core(plane):
        deep_all[plane, pl.ds(pair, 1), to_rows] = deep[pl.ds(pair, 1), plane, from_rows]
        to_core(deep.at[pair, plane, from_rows], plane, pair)

    def share_across(plane, received):
        src = deep.at[1 - pair, plane, from_rows]
        send(DEEP_OWN, src, deep_all.at[plane, pair, to_rows], (beside, n), received=received)

    def pass_on(plane, received):
        theirs = deep_all.at[plane, 1 - pair, to_rows]
        arrived(received, theirs)
        to_core(theirs, plane, 1 - pair)

    pl.semaphore_wait(barrier, len(partners))
    send_halos(deep, DEEP_ROWS)
    loads[2].wait()
    for m in range(4):
        cot_send[m] = jnp.concatenate([cot[m, :128], cot[m, 128:]], axis=1)
    cot_recv[pl.ds(n, 1)] = cot_send[pl.ds(n, 1)]
    for d in range(1, 4):
        send(COT, cot_send.at[(n + d) % 4], cot_recv.at[n], near[d - 1])
    sent(COT, cot_send.at[pl.ds(0, 3)])
    cyz_rows[...] = jnp.zeros_like(cyz_rows)
    czy_rows[...] = jnp.zeros_like(czy_rows)

    for s in range(4):
        block = patches[:, 256 * s : 256 * s + 256].astype(F32)
        patches_t[256 * s : 256 * s + 256, :] = block.T.astype(BF)

    def window(buf, plane, first):
        return [buf[half, plane, first : first + 8].reshape(256, 128) for half in range(2)]

    def shifted(value, by, masked):
        column = lax.broadcasted_iota(jnp.int32, value.shape, 0) % 32
        return jnp.where(column == masked, 0.0, pltpu.roll(value, by, 0))

    loads[3].wait()
    for i in (1, 0, 2):
        if i == 1:
            rows_arrive(deep, DEEP_ROWS)
        else:
            plane_arrives(deep, DEEP_ROWS, i)
        share_core(i)
        if i == 1:
            share_across(1, DEEP_OWN)
        else:

            @pl.when(outer == i)
            def _():
                share_across(i, DEEP_OUTER)

        slab = jnp.concatenate(window(deep, i, 0) + window(deep, i, 1) + window(deep, i, 2), axis=1)
        for k in range(3):
            weights = jnp.concatenate([cw[9 * i + 3 * j + k] for j in range(3)], axis=0)
            term = matmul(slab, weights)
            acc[k] = term if i == 1 else acc[k] + term
    deep_all[pl.ds(outer, 1), pl.ds(1 - pair, 1), to_rows] = deep[pl.ds(pair, 1), pl.ds(inner, 1), from_rows]
    to_core(deep.at[pair, inner, from_rows], outer, 1 - pair)
    sent(DEEP_OWN, deep.at[:, 1, pl.ds(0, 9)])
    preact = shifted(acc[0], 1, 0) + acc[1] + shifted(acc[2], 255, 31)

    arrived(COT, cot_recv.at[pl.ds(0, 3)])
    cotangent = jnp.concatenate(
        [
            jnp.concatenate([cot_recv[m][:, :64], cot_recv[m][:, 64:]], axis=0)
            for m in range(4)
        ],
        axis=1,
    ).astype(F32)
    sigma = 1.0 / (1.0 + jnp.exp(-preact))
    activated = (preact * sigma).astype(BF)
    grad_pre = (cotangent * (sigma * (1.0 + preact * (1.0 - sigma)))).astype(BF)
    for half in range(2):
        grad[half, 1, 1:9] = grad_pre[:, 128 * half : 128 * half + 128].reshape(8, 32, 128)

    row = lax.broadcasted_iota(jnp.int32, (256, 256), 0)
    column = lax.broadcasted_iota(jnp.int32, (256, 256), 1)
    q = row % 128
    source = (q // 32) * 64 + ((q // 4) % 8) * 8 + (row // 128) * 4 + q % 4
    order = jnp.where(column == source, 1.0, 0.0).astype(BF)
    turned = matmul_nt(order, grad_pre).astype(BF)
    grad_t_send[0] = turned[:128]
    grad_t_send[1] = turned[128:]
    slot = 2 * pair + c
    grad_t[pl.ds(slot, 1)] = grad_t_send[pl.ds(c, 1)]
    mine = grad_t.at[slot]
    send(GRAD_SHARE, grad_t_send.at[1 - c], mine, (beside, other_c))
    send(GRAD_SHARE, grad_t_send.at[c], mine, (beside, n))
    send(GRAD_SHARE, grad_t_send.at[1 - c], mine, (w, other_c))
    sent(GRAD_SHARE, grad_t.at[pl.ds(0, 3)])
    send_halos(grad, GRAD_ROWS)

    pass_on(1, DEEP_OWN)
    pass_on(inner, DEEP_OUTER)
    sent(DEEP_CORE, deep_all.at[:, :, pl.ds(0, 9)])

    arrived(GRAD_SHARE, grad_t.at[pl.ds(0, 3)])
    lane = lax.broadcasted_iota(jnp.int32, (128, 256), 1) % 32
    for m in range(4):
        block = grad_t[m].astype(F32)
        at = 256 * m
        grad_rows[0:128, at : at + 256] = jnp.where(lane == 31, 0.0, pltpu.roll(block, 255, 1)).astype(BF)
        grad_rows[128:256, at : at + 256] = grad_t[m]
        grad_rows[256:384, at : at + 256] = jnp.where(lane == 0, 0.0, pltpu.roll(block, 1, 1)).astype(BF)
    def cells_at(i, j):
        return jnp.concatenate([deep_all[i, s, j : j + 16].reshape(512, 128) for s in range(2)], axis=0)

    arrived(DEEP_CORE, deep_all.at[:, :, pl.ds(0, 9)])
    slab = jnp.concatenate([cells_at(i, j) for i, j in Y_TAPS], axis=1)
    term = matmul(grad_rows[...], slab).astype(BF)
    for yy in range(NY):
        for k in range(3):
            at = 128 * k + 32 * yy
            cy_send[yy, k] = term[at : at + 32]
    for d in range(1, NY):
        send(CONV_Y, cy_send.at[(y + d) % NY], cy_recv.at[d - 1], ys[d - 1])
    sent(CONV_Y, cy_recv)
    row = lax.broadcasted_iota(jnp.int32, (128, 128), 0)
    column = lax.broadcasted_iota(jnp.int32, (128, 128), 1)
    source = ((row // 4) % 4) * 32 + (row // 16) * 4 + row % 4
    order = jnp.where(column == source, 1.0, 0.0).astype(BF)
    for k in range(3):
        grad_rows_z[128 * k : 128 * k + 128, :] = matmul(order, grad_rows[128 * k : 128 * k + 128, :]).astype(BF)
    slab = jnp.concatenate([cells_at(i, j) for i, j in Z_TAPS], axis=1)
    term = matmul(grad_rows_z[...], slab).astype(BF)
    for zz in range(NZ):
        for k in range(3):
            at = 128 * k + 16 * zz
            cz_send[zz, k] = term[at : at + 16]
    for d in range(1, NZ):
        send(CONV_Z, cz_send.at[(z + d) % NZ], cz_recv.at[d - 1], zs[d - 1])
    sent(CONV_Z, cz_recv)

    for i in (1, 2, 0):
        plane = 2 - i
        if i == 1:
            rows_arrive(grad, GRAD_ROWS)
        else:
            plane_arrives(grad, GRAD_ROWS, plane)
        slab = jnp.concatenate(
            window(grad, plane, 2) + window(grad, plane, 1) + window(grad, plane, 0), axis=1
        )
        for k in range(3):
            weights = jnp.concatenate([cw[9 * i + 3 * j + k] for j in range(3)], axis=1)
            term = matmul_nt(slab, weights)
            acc[k] = term if i == 1 else acc[k] + term
    grad_deep = (shifted(acc[0], 255, 31) + acc[1] + shifted(acc[2], 1, 0)).astype(BF)

    partial = matmul(patches_t[...], grad_deep)
    low, high = partial[:, :128], partial[:, 128:]
    dc_send[...] = jnp.where(c == 0, high, low).astype(BF)
    send(DOWN_C, dc_send, dc_recv, (w, other_c))
    sent(DOWN_C, dc_send)
    kept = jnp.where(c == 0, low, high)

    for m in range(4):
        part = activated[:, 64 * m : 64 * m + 64]
        act_send[m] = jnp.concatenate([part[:128], part[128:]], axis=1)
    act_recv[pl.ds(n, 1)] = act_send[pl.ds(n, 1)]
    for d in range(1, 4):
        send(ACT, act_send.at[(n + d) % 4], act_recv.at[n], near[d - 1])
    sent(ACT, act_send.at[pl.ds(0, 3)])

    spread = matmul_nt(grad_deep, dw[...])
    for a in range(2):
        for b in range(2):
            for e in range(2):
                at = (4 * a + 2 * b + e) * 128
                wide_f32[a, :, b, pl.ds(e, 32, stride=2), :] = spread[:, at : at + 128].reshape(8, 32, 128)
    vol[...] = wide_f32[...].astype(BF)
    vg_write = pltpu.make_async_copy(vol, vg_out, local_sem.at[0])
    vg_write.start()

    arrived(DOWN_C, dc_recv)
    total = (kept + dc_recv[...].astype(F32)).reshape(16, 2, 2, 2, 8, 128)
    for xx in range(2):
        for ll in range(2):
            for zz in range(2):
                dx_rows[xx, ll, :, 8 * zz : 8 * zz + 8] = total[:, zz, xx, ll]
    dx_send[...] = dx_rows[...].astype(BF)
    for s, (dy, dx, dl, to) in enumerate(xys):
        src = dx_send.at[(xh + dx) % 2, (l + dl) % 2, pl.ds(4 * ((y + dy) % NY), 4)]
        send(DOWN_XY, src, dx_recv.at[s], to)
    sent(DOWN_XY, dx_recv)

    arrived(CONV_Y, cy_recv)
    total = cy_send[pl.ds(y, 1)].reshape(3, 32, YL).astype(F32)
    for d in range(3):
        total = total + cy_recv[d].astype(F32)
    sum_rows[...] = total
    for zz in range(NZ):
        for m in range(3 * len(Y_TAPS)):
            part = sum_rows[m % 3, 4 * zz : 4 * zz + 4, 128 * (m // 3) : 128 * (m // 3) + 128]
            cyz_rows[zz, 4 * (m % 4) : 4 * (m % 4) + 4, 128 * (m // 4) : 128 * (m // 4) + 128] = part
    cyz_send[...] = cyz_rows[...].astype(BF)
    for d in range(1, NZ):
        send(CONV_YZ, cyz_send.at[(z + d) % NZ], cyz_recv.at[d - 1], zs[d - 1])
    sent(CONV_YZ, cyz_recv)

    arrived(CONV_Z, cz_recv)
    halves = [cz_send[pl.ds(z, 1)].reshape(3, 16, ZL).astype(F32), 0.0]
    for d in range(1, NZ):
        halves[d % 2] = halves[d % 2] + cz_recv[d - 1].astype(F32)
    for h in range(2):
        sum_rows[:, :16, :ZL] = halves[h]
        for yy in range(NY):
            for m in range(3 * len(Z_TAPS)):
                part = sum_rows[m % 3, 4 * yy : 4 * yy + 4, 128 * (m // 3) : 128 * (m // 3) + 128]
                czy_rows[yy, h, 4 * (m % 4) : 4 * (m % 4) + 4, 128 * (m // 4) : 128 * (m // 4) + 128] = part
    czy_send[...] = czy_rows[...].astype(BF)
    for d in range(1, NY):
        send(CONV_ZY, czy_send.at[(y + d) % NY], czy_recv.at[d - 1], ys[d - 1])
    sent(CONV_ZY, czy_recv)

    arrived(DOWN_XY, dx_recv)
    total = dx_rows[pl.ds(xh, 1), pl.ds(l, 1), pl.ds(4 * y, 4)].reshape(4, 16, 128)
    for s in range(15):
        total = total + dx_recv[s].astype(F32)
    dz_send[...] = total.reshape(NZ, 8, 128)
    for d in range(1, NZ):
        send(DOWN_Z, dz_send.at[(z + d) % NZ], dz_recv.at[d - 1], zs[d - 1])
    sent(DOWN_Z, dz_recv)

    arrived(ACT, act_recv.at[pl.ds(0, 3)])
    for m in range(4):
        act_vmem[256 * m : 256 * m + 128] = act_recv[m][:, :64]
        act_vmem[256 * m + 128 : 256 * m + 256] = act_recv[m][:, 64:]
    act_write = pltpu.make_async_copy(act_vmem, act_out, local_sem.at[1])
    act_write.start()

    arrived(CONV_ZY, czy_recv)
    total = czy_send[pl.ds(y, 1)].reshape(2, 16, 128 * Z_BLOCKS).astype(F32)
    for d in range(3):
        total = total + czy_recv[d].astype(F32)
    last_sum[pl.ds(pair, 1), :, 128 * Y_BLOCKS :] = total[0:1]
    last_sum[pl.ds(1 - pair, 1), :, 128 * Y_BLOCKS :] = total[1:2]
    arrived(CONV_YZ, cyz_recv)
    halves = [cyz_send[pl.ds(z, 1)].astype(F32), 0.0]
    for d in range(1, NZ):
        halves[d % 2] = halves[d % 2] + cyz_recv[d - 1 : d].astype(F32)
    last_sum[pl.ds(pair, 1), :, : 128 * Y_BLOCKS] = halves[0]
    last_sum[pl.ds(1 - pair, 1), :, : 128 * Y_BLOCKS] = halves[1]
    for h in range(2):
        whole = last_sum[h]
        for q in range(2):
            pieces = [whole[:, 128 * b + 64 * q : 128 * b + 64 * q + 64] for b in range(Y_BLOCKS + Z_BLOCKS)]
            last_send[h, q] = jnp.concatenate(pieces, axis=1).astype(BF)

    def last(slot, h, q, to):
        send(CONV_LAST, last_send.at[h, q], last_recv.at[slot], to, received=CONV_LAST if slot else CONV_CORE)

    near_l, far_l = 2 * l, 2 - 2 * l

    @pl.when(xh == c)
    def _():
        last(1, 1 - l, 0, (w, far_l))
        last(1, 1 - l, 1, (w, far_l + 1))
        last(0, l, 1 - c, (w, other_c))

    @pl.when(xh != c)
    def _():
        last(2, l, 0, (across, near_l))
        last(2, l, 1, (across, near_l + 1))
        last(3, 1 - l, 0, (across, far_l))
        last(3, 1 - l, 1, (across, far_l + 1))

    arrived(DOWN_Z, dz_recv)
    total = dz_send[pl.ds(z, 1)].reshape(8, 128)
    for d in range(7):
        total = total + dz_recv[d]
    dl_send[...] = total
    send(DOWN_LAST, dl_send, dl_recv, (w, other_c))
    sent(DOWN_LAST, dl_send)

    @pl.when(xh == c)
    def _():
        remote(CONV_LAST, last_recv.at[pl.ds(0, 3)], last_recv.at[pl.ds(0, 3)], near[0]).wait_send()

    @pl.when(xh != c)
    def _():
        remote(CONV_LAST, last_recv, last_recv, near[0]).wait_send()
        arrived(CONV_CORE, last_recv.at[0])

    arrived(CONV_LAST, last_recv.at[pl.ds(1, 3)])
    own = last_send[pl.ds(l, 1), pl.ds(c, 1)].reshape(16, 64 * (Y_BLOCKS + Z_BLOCKS))
    conv = jnp.where(c == xh, own, last_recv[0]).astype(F32)
    for slot in range(1, 4):
        conv = conv + last_recv[slot].astype(F32)
    conv = conv * factor
    for first, taps in ((0, Y_TAPS), (Y_BLOCKS, Z_TAPS)):
        for m in range(3 * len(taps)):
            i, j = taps[m // 3]
            at = 64 * (first + m // 4)
            cg_vmem[9 * i + 3 * j + m % 3] = conv[4 * (m % 4) : 4 * (m % 4) + 4, at : at + 64]
    cg_write = pltpu.make_async_copy(cg_vmem, cg_out, local_sem.at[2])
    cg_write.start()
    arrived(DOWN_LAST, dl_recv)
    theirs = dl_recv[...]
    both = jnp.concatenate([jnp.where(c == 0, total, theirs), jnp.where(c == 0, theirs, total)], axis=1)
    dg_vmem[...] = jnp.where(c == 0, both[:4], both[4:]) * factor
    dg_write = pltpu.make_async_copy(dg_vmem, dg_out, local_sem.at[3])
    dg_write.start()

    for copy in outgoing:
        copy.wait_send()
    for copy in (vg_write, act_write, cg_write, dg_write):
        copy.wait()


def write_out(*refs):
    arrays = (len(refs) - 1) // 2
    sems = refs[-1]
    copies = [
        pltpu.make_async_copy(src, dst, sems.at[s])
        for s, (src, dst) in enumerate(zip(refs[:arrays], refs[arrays:-1]))
    ]
    for copy in copies:
        copy.start()
    for copy in copies:
        copy.wait()


def on_device(volume, down_weight, conv_weight, cotangent):
    factor = 1.0 / (32 * math.sqrt(64))
    hbm = pl.BlockSpec(memory_space=pltpu.HBM)
    vmem = pl.BlockSpec(memory_space=pltpu.VMEM)
    scratch = [
        ((2, 8, 2, 64, 128), BF),
        ((1024, 256), BF),
        ((27, 256, 256), BF),
        ((4, 256, 64), BF),
        ((2, 8, 2, 64, 128), F32),
        ((256, 1024), BF),
        ((1024, 256), BF),
        ((2, 3, 10, 32, 128), BF),
        ((2, 3, 10, 32, 128), BF),
        ((3, 2, 18, 32, 128), BF),
        ((2, 128, 256), BF),
        ((4, 128, 256), BF),
        ((384, 1024), BF),
        ((384, 1024), BF),
        ((3, 256, 256), F32),
        ((4, 128, 128), BF),
        ((4, 128, 128), BF),
        ((4, 128, 128), BF),
        ((4, 128, 128), BF),
        ((1024, 64), BF),
        ((4, 3, 32, YL), BF),
        ((3, 3, 32, YL), BF),
        ((3, 32, YL), F32),
        ((8, 16, 128 * Y_BLOCKS), F32),
        ((8, 16, 128 * Y_BLOCKS), BF),
        ((7, 16, 128 * Y_BLOCKS), BF),
        ((8, 3, 16, ZL), BF),
        ((7, 3, 16, ZL), BF),
        ((4, 2, 16, 128 * Z_BLOCKS), F32),
        ((4, 2, 16, 128 * Z_BLOCKS), BF),
        ((3, 2, 16, 128 * Z_BLOCKS), BF),
        ((1024, 128), BF),
        ((1024, 128), BF),
        ((2, 2, 16, 16, 128), F32),
        ((2, 2, 16, 16, 128), BF),
        ((15, 4, 16, 128), BF),
        ((8, 8, 128), F32),
        ((7, 8, 128), F32),
        ((8, 128), F32),
        ((8, 128), F32),
        ((27, 4, 64), F32),
        ((4, 256), F32),
        ((2, 16, 128 * (Y_BLOCKS + Z_BLOCKS)), F32),
        ((2, 2, 16, 64 * (Y_BLOCKS + Z_BLOCKS)), BF),
        ((4, 16, 64 * (Y_BLOCKS + Z_BLOCKS)), BF),
    ]
    results = pl.pallas_call(
        functools.partial(kernel, factor),
        name="unet_level",
        out_shape=(
            jax.ShapeDtypeStruct((1024, 64), BF),
            jax.ShapeDtypeStruct((2, 8, 2, 64, 128), BF),
            jax.ShapeDtypeStruct((4, 256), F32),
            jax.ShapeDtypeStruct((27, 4, 64), F32),
        ),
        in_specs=[hbm] * 4,
        out_specs=(hbm,) * 4,
        scratch_shapes=[pltpu.VMEM(shape, dtype) for shape, dtype in scratch]
        + [
            pltpu.SemaphoreType.DMA((4,)),
            pltpu.SemaphoreType.DMA((GROUPS,)),
            pltpu.SemaphoreType.DMA((GROUPS,)),
        ],
        compiler_params=pltpu.CompilerParams(
            collective_id=0, has_side_effects=True, vmem_limit_bytes=56 * 1024 * 1024
        ),
        cost_estimate=pl.CostEstimate(flops=3200000000, bytes_accessed=8000000, transcendentals=65536),
    )(
        volume.reshape(2, 8, 2, 64, 128),
        down_weight,
        conv_weight,
        cotangent.reshape(4, 256, 64),
    )
    activated, volume_grad, down_grad, conv_grad = pl.pallas_call(
        write_out,
        name="write_out",
        out_shape=tuple(jax.ShapeDtypeStruct(r.shape, r.dtype) for r in results),
        in_specs=[vmem] * 4,
        out_specs=(hbm,) * 4,
        scratch_shapes=[pltpu.SemaphoreType.DMA((4,))],
    )(*results)
    return (
        activated.reshape(1, 32, 32, 64),
        volume_grad.reshape(2, 16, 64, 128),
        down_grad,
        conv_grad.transpose(0, 2, 1),
    )


def solution(mesh):
    placed = (P("wide", "narrow", None, None), P(), P(), P("wide", None, None, "narrow"))
    return jax.shard_map(
        on_device,
        mesh=mesh,
        in_specs=placed,
        out_specs=(
            P("wide", None, None, "narrow"),
            P("wide", "narrow", None, None),
            P(("wide", "narrow"), None),
            P(None, "narrow", "wide"),
        ),
        check_vma=False,
    )
```

```python
import functools
import math

import jax
import jax.numpy as jnp
from jax import lax
from jax.experimental import pallas as pl
from jax.experimental.pallas import tpu as pltpu
from jax.sharding import PartitionSpec as P

MESH = pl.DeviceIdType.MESH
BF = jnp.bfloat16
F32 = jnp.float32
Y_TAPS = ((0, 0), (0, 1), (0, 2), (1, 0), (1, 1), (1, 2))
Z_TAPS = ((2, 0), (2, 1), (2, 2))
YL, ZL = 128 * len(Y_TAPS), 128 * len(Z_TAPS)
NY, NZ = 4, 8
Y_ORDER, Z_ORDER = (2, 1, 3), (4, 3, 5, 2, 6, 1, 7)

COT, DEEP_ROWS, DEEP_LOW, DEEP_HIGH, DEEP_OWN, DEEP_OUTER, DEEP_CORE, ACT = range(8)
GRAD_ROWS, GRAD_LOW, GRAD_HIGH, GRAD_SHARE, CONV_Y, CONV_YZ, CONV_Z, CONV_ZY = range(8, 16)
DOWN_C, DOWN_XY, DOWN_Z, DOWN_LAST, CONV_LAST, CONV_CORE = range(16, 22)
GROUPS = 22
Y_BLOCKS, Z_BLOCKS = -(-3 * len(Y_TAPS) // 4), -(-3 * len(Z_TAPS) // 4)


def matmul(a, b):
    return jnp.dot(a, b, preferred_element_type=F32)


def matmul_nt(a, b):
    return lax.dot_general(a, b, (((1,), (1,)), ((), ())), preferred_element_type=F32)


def kernel(
    factor,
    vol_ref,
    dw_ref,
    cw_ref,
    cot_ref,
    act_out,
    vg_out,
    dg_out,
    cg_out,
    vol,
    dw,
    cw,
    cot,
    wide_f32,
    patches,
    patches_t,
    deep,
    grad,
    deep_all,
    grad_t_send,
    grad_t,
    grad_rows,
    grad_rows_z,
    acc,
    cot_send,
    cot_recv,
    act_send,
    act_recv,
    act_vmem,
    cy_send,
    cy_recv,
    sum_rows,
    cyz_rows,
    cyz_send,
    cyz_recv,
    cz_send,
    cz_recv,
    czy_rows,
    czy_send,
    czy_recv,
    dc_send,
    dc_recv,
    dx_rows,
    dx_send,
    dx_recv,
    dz_send,
    dz_recv,
    dl_send,
    dl_recv,
    cg_vmem,
    dg_vmem,
    last_sum,
    last_send,
    last_recv,
    local_sem,
    send_sem,
    recv_sem,
):
    w = lax.axis_index("wide")
    n = lax.axis_index("narrow")
    y, z, xh = w // 16, (w // 2) % NZ, w % 2
    l, c = n // 2, n % 2
    pair = z % 2

    def wide_of(yy, zz, xx):
        return ((yy % NY) * NZ + zz % NZ) * 2 + xx

    near = [(w, (n + d) % 4) for d in range(1, 4)]
    up, down = (w + 1) % 64, (w + 63) % 64
    right, left = (n + 1) % 4, (n + 3) % 4
    depth = [(s, (n + d) % 4) for s in (up, down) for d in range(4)]
    ys = [(wide_of(y + d, z, xh), n) for d in range(1, NY)]
    zs = [(wide_of(y, z + d, xh), n) for d in range(1, NZ)]
    other_c = n + 1 - 2 * c
    across = wide_of(y, z, 1 - xh)
    other_l = (n + 2) % 4
    beside = wide_of(y, z + 1 - 2 * pair, xh)
    xys = [
        (dy, dx, dl, (wide_of(y + dy, z, (xh + dx) % 2), n + 2 * dl * (1 - 2 * l)))
        for dy in range(NY)
        for dx in range(2)
        for dl in range(2)
        if dy or dx or dl
    ]

    barrier = pltpu.get_barrier_semaphore()
    partners = near + depth + ys + zs + [to for dy, dx, dl, to in xys if dy and (dx or dl)]
    for who in partners:
        pl.semaphore_signal(barrier, inc=1, device_id=who, device_id_type=MESH)

    def remote(number, src, dst, who, received=None):
        return pltpu.make_async_remote_copy(
            src_ref=src,
            dst_ref=dst,
            send_sem=send_sem.at[number],
            recv_sem=recv_sem.at[number if received is None else received],
            device_id=who,
            device_id_type=MESH,
        )

    def send(*args, **kwargs):
        remote(*args, **kwargs).start()

    def finish(number, ref, edge_ref, receiving):
        def wait(ref):
            copy = remote(number, ref, ref, near[0])
            if receiving:
                copy.wait_recv()
            else:
                copy.wait_send()

        if edge_ref is None:
            wait(ref)
        else:
            pl.when(inside)(lambda: wait(ref))
            pl.when(jnp.logical_not(inside))(lambda: wait(edge_ref))

    def arrived(number, ref, edge_ref=None):
        finish(number, ref, edge_ref, True)

    outgoing = []

    def sent(number, ref, edge_ref=None):
        outgoing.append((number, ref, edge_ref))

    def flush(numbers):
        for group in [group for group in outgoing if group[0] in numbers]:
            finish(*group, False)
            outgoing.remove(group)

    loads = [
        pltpu.make_async_copy(src, dst, local_sem.at[s])
        for s, (src, dst) in enumerate(((vol_ref, vol), (dw_ref, dw), (cot_ref, cot), (cw_ref, cw)))
    ]
    for copy in loads:
        copy.start()

    inside = (n == 1) | (n == 2)
    far = (w + 63 + 2 * xh) % 64

    def send_halos(buf, base):
        def rows(to, plane, received):
            for missing, who, first, at in ((3, n + 1, 8, 0), (0, n - 1, 1, 9)):

                @pl.when(n != missing)
                def _():
                    src = buf.at[:, 1, pl.ds(first, 1)]
                    send(base, src, buf.at[:, plane, pl.ds(at, 1)], (to, who), received=received)

        rows(w, 1, base)
        for to, s in ((far, 1 - xh), (across, xh)):
            rows(to, 2 * s, base + 1 + s)
        for to, s in ((far, 1 - xh), (across, xh)):
            planes = buf.at[:, 2 * s, pl.ds(1, 8)]
            send(base + 1, buf.at[:, 1, pl.ds(1, 8)], planes, (to, n), received=base + 1 + s)
        sent(base, buf.at[:, 1, pl.ds(0, 6)], buf.at[:, 1, pl.ds(0, 3)])
        sent(base + 1, buf.at[:, pl.ds(0, 2), pl.ds(0, 8)])

    def clear_rows(buf, plane):
        @pl.when(n == 0)
        def _():
            buf[:, plane, 0:1] = jnp.zeros((2, 1, 32, 128), BF)

        @pl.when(n == 3)
        def _():
            buf[:, plane, 9:10] = jnp.zeros((2, 1, 32, 128), BF)

    def rows_arrive(buf, base):
        arrived(base, buf.at[:, 1, pl.ds(0, 2)], buf.at[:, 1, pl.ds(0, 1)])
        clear_rows(buf, 1)

    def plane_arrives(buf, base, plane):
        arrived(base + 1 + plane // 2, buf.at[:, plane], buf.at[:, plane, pl.ds(0, 9)])
        clear_rows(buf, plane)

        @pl.when(w == (0 if plane == 0 else 63))
        def _():
            buf[:, plane] = jnp.zeros((2, 10, 32, 128), BF)

    loads[0].wait()
    wide_f32[...] = vol[...].astype(F32)
    for a in range(2):
        for b in range(2):
            for e in range(2):
                part = wide_f32[a, :, b, pl.ds(e, 32, stride=2), :].reshape(256, 128).astype(BF)
                at = (4 * a + 2 * b + e) * 128
                patches[:, at : at + 128] = part
    loads[1].wait()
    cells = matmul(patches[...], dw[...]).astype(BF)
    for half in range(2):
        deep[half, 1, 1:9] = cells[:, 128 * half : 128 * half + 128].reshape(8, 32, 128)

    from_rows, to_rows = pl.ds(c, 9), pl.ds(9 * c, 9)
    outer, inner = 2 * pair, 2 - 2 * pair

    def to_core(src, plane, chip):
        send(DEEP_CORE, src, deep_all.at[plane, chip, to_rows], (w, other_c))

    def share_core(plane):
        deep_all[plane, pl.ds(pair, 1), to_rows] = deep[pl.ds(pair, 1), plane, from_rows]
        to_core(deep.at[pair, plane, from_rows], plane, pair)

    def share_across(plane, received):
        src = deep.at[1 - pair, plane, from_rows]
        send(DEEP_OWN, src, deep_all.at[plane, pair, to_rows], (beside, n), received=received)

    def pass_on(plane, received):
        theirs = deep_all.at[plane, 1 - pair, to_rows]
        arrived(received, theirs)
        to_core(theirs, plane, 1 - pair)

    pl.semaphore_wait(barrier, len(partners))
    send_halos(deep, DEEP_ROWS)
    loads[2].wait()
    for m in range(4):
        cot_send[m] = jnp.concatenate([cot[m, :128], cot[m, 128:]], axis=1)
    cot_recv[pl.ds(n, 1)] = cot_send[pl.ds(n, 1)]
    for d in range(1, 4):
        send(COT, cot_send.at[(n + d) % 4], cot_recv.at[n], near[d - 1])
    sent(COT, cot_send.at[pl.ds(0, 3)])
    cyz_rows[...] = jnp.zeros_like(cyz_rows)
    czy_rows[...] = jnp.zeros_like(czy_rows)

    for s in range(4):
        block = patches[:, 256 * s : 256 * s + 256].astype(F32)
        patches_t[256 * s : 256 * s + 256, :] = block.T.astype(BF)

    def window(buf, plane, first):
        return [buf[half, plane, first : first + 8].reshape(256, 128) for half in range(2)]

    def shifted(value, by, masked):
        column = lax.broadcasted_iota(jnp.int32, value.shape, 0) % 32
        return jnp.where(column == masked, 0.0, pltpu.roll(value, by, 0))

    loads[3].wait()
    for i in (1, 0, 2):
        if i == 1:
            rows_arrive(deep, DEEP_ROWS)
        else:
            plane_arrives(deep, DEEP_ROWS, i)
        share_core(i)
        if i == 1:
            share_across(1, DEEP_OWN)
        else:

            @pl.when(outer == i)
            def _():
                share_across(i, DEEP_OUTER)

        slab = jnp.concatenate(window(deep, i, 0) + window(deep, i, 1) + window(deep, i, 2), axis=1)
        for k in range(3):
            weights = jnp.concatenate([cw[9 * i + 3 * j + k] for j in range(3)], axis=0)
            term = matmul(slab, weights)
            acc[k] = term if i == 1 else acc[k] + term
    deep_all[pl.ds(outer, 1), pl.ds(1 - pair, 1), to_rows] = deep[pl.ds(pair, 1), pl.ds(inner, 1), from_rows]
    to_core(deep.at[pair, inner, from_rows], outer, 1 - pair)
    sent(DEEP_OWN, deep.at[:, 1, pl.ds(0, 9)])
    preact = shifted(acc[0], 1, 0) + acc[1] + shifted(acc[2], 255, 31)

    arrived(COT, cot_recv.at[pl.ds(0, 3)])
    cotangent = jnp.concatenate(
        [
            jnp.concatenate([cot_recv[m][:, :64], cot_recv[m][:, 64:]], axis=0)
            for m in range(4)
        ],
        axis=1,
    ).astype(F32)
    sigma = 1.0 / (1.0 + jnp.exp(-preact))
    activated = (preact * sigma).astype(BF)
    grad_pre = (cotangent * (sigma * (1.0 + preact * (1.0 - sigma)))).astype(BF)
    for half in range(2):
        grad[half, 1, 1:9] = grad_pre[:, 128 * half : 128 * half + 128].reshape(8, 32, 128)

    row = lax.broadcasted_iota(jnp.int32, (256, 256), 0)
    column = lax.broadcasted_iota(jnp.int32, (256, 256), 1)
    q = row % 128
    source = (q // 32) * 64 + ((q // 4) % 8) * 8 + (1 - row // 128) * 4 + q % 4
    order = jnp.where(column == source, 1.0, 0.0).astype(BF)
    turned = matmul_nt(order, grad_pre).astype(BF)
    grad_t_send[0] = turned[:128]
    grad_t_send[1] = turned[128:]
    slot = 2 * pair + c
    grad_t[pl.ds(slot, 1)] = grad_t_send[pl.ds(c, 1)]
    mine = grad_t.at[slot]
    send(GRAD_SHARE, grad_t_send.at[1 - c], mine, (beside, other_c))
    send(GRAD_SHARE, grad_t_send.at[c], mine, (beside, n))
    send(GRAD_SHARE, grad_t_send.at[1 - c], mine, (w, other_c))
    sent(GRAD_SHARE, grad_t.at[pl.ds(0, 3)])
    send_halos(grad, GRAD_ROWS)

    pass_on(1, DEEP_OWN)
    pass_on(inner, DEEP_OUTER)
    sent(DEEP_CORE, deep_all.at[:, :, pl.ds(0, 9)])

    arrived(GRAD_SHARE, grad_t.at[pl.ds(0, 3)])
    lane = lax.broadcasted_iota(jnp.int32, (128, 256), 1) % 32
    for m in range(4):
        block = grad_t[m].astype(F32)
        at = 256 * m
        grad_rows[0:128, at : at + 256] = jnp.where(lane == 31, 0.0, pltpu.roll(block, 255, 1)).astype(BF)
        grad_rows[128:256, at : at + 256] = grad_t[m]
        grad_rows[256:384, at : at + 256] = jnp.where(lane == 0, 0.0, pltpu.roll(block, 1, 1)).astype(BF)
    def cells_at(i, j):
        return jnp.concatenate([deep_all[i, s, j : j + 16].reshape(512, 128) for s in range(2)], axis=0)

    arrived(DEEP_CORE, deep_all.at[:, :, pl.ds(0, 9)])
    slab = jnp.concatenate([cells_at(i, j) for i, j in Y_TAPS], axis=1)
    term = matmul(grad_rows[...], slab).astype(BF)
    for yy in range(NY):
        for k in range(3):
            at = 128 * k + 32 * yy
            cy_send[yy, k] = term[at : at + 32]
    for d in Y_ORDER:
        send(CONV_Y, cy_send.at[(y + d) % NY], cy_recv.at[d - 1], ys[d - 1])
    sent(CONV_Y, cy_recv)
    row = lax.broadcasted_iota(jnp.int32, (128, 128), 0)
    column = lax.broadcasted_iota(jnp.int32, (128, 128), 1)
    source = ((row // 4) % 4) * 32 + (row // 16) * 4 + row % 4
    order = jnp.where(column == source, 1.0, 0.0).astype(BF)
    for k in range(3):
        grad_rows_z[128 * k : 128 * k + 128, :] = matmul(order, grad_rows[128 * k : 128 * k + 128, :]).astype(BF)
    slab = jnp.concatenate([cells_at(i, j) for i, j in Z_TAPS], axis=1)
    term = matmul(grad_rows_z[...], slab).astype(BF)
    for zz in range(NZ):
        for k in range(3):
            at = 128 * k + 16 * zz
            cz_send[zz, k] = term[at : at + 16]
    flush((GRAD_ROWS, GRAD_LOW))
    for d in Z_ORDER:
        send(CONV_Z, cz_send.at[(z + d) % NZ], cz_recv.at[d - 1], zs[d - 1])
    sent(CONV_Z, cz_recv)

    for i in (1, 2, 0):
        plane = 2 - i
        if i == 1:
            rows_arrive(grad, GRAD_ROWS)
        else:
            plane_arrives(grad, GRAD_ROWS, plane)
        slab = jnp.concatenate(
            window(grad, plane, 2) + window(grad, plane, 1) + window(grad, plane, 0), axis=1
        )
        for k in range(3):
            weights = jnp.concatenate([cw[9 * i + 3 * j + k] for j in range(3)], axis=1)
            term = matmul_nt(slab, weights)
            acc[k] = term if i == 1 else acc[k] + term
    grad_deep = (shifted(acc[0], 255, 31) + acc[1] + shifted(acc[2], 1, 0)).astype(BF)

    partial = matmul(patches_t[...], grad_deep)
    low, high = partial[:, :128], partial[:, 128:]
    dc_send[...] = jnp.where(c == 0, high, low).astype(BF)
    send(DOWN_C, dc_send, dc_recv, (w, other_c))
    sent(DOWN_C, dc_send)
    kept = jnp.where(c == 0, low, high)

    for m in range(4):
        part = activated[:, 64 * m : 64 * m + 64]
        act_send[m] = jnp.concatenate([part[:128], part[128:]], axis=1)
    act_recv[pl.ds(n, 1)] = act_send[pl.ds(n, 1)]
    for d in range(1, 4):
        send(ACT, act_send.at[(n + d) % 4], act_recv.at[n], near[d - 1])
    sent(ACT, act_send.at[pl.ds(0, 3)])

    spread = matmul_nt(grad_deep, dw[...])
    for a in range(2):
        for b in range(2):
            for e in range(2):
                at = (4 * a + 2 * b + e) * 128
                wide_f32[a, :, b, pl.ds(e, 32, stride=2), :] = spread[:, at : at + 128].reshape(8, 32, 128)
    vol[...] = wide_f32[...].astype(BF)
    vg_write = pltpu.make_async_copy(vol, vg_out, local_sem.at[0])
    vg_write.start()

    arrived(DOWN_C, dc_recv)
    total = (kept + dc_recv[...].astype(F32)).reshape(16, 2, 2, 2, 8, 128)
    for xx in range(2):
        for ll in range(2):
            for zz in range(2):
                dx_rows[xx, ll, :, 8 * zz : 8 * zz + 8] = total[:, zz, xx, ll]
    dx_send[...] = dx_rows[...].astype(BF)
    for s, (dy, dx, dl, to) in enumerate(xys):
        src = dx_send.at[(xh + dx) % 2, (l + dl) % 2, pl.ds(4 * ((y + dy) % NY), 4)]
        send(DOWN_XY, src, dx_recv.at[s], to)
    sent(DOWN_XY, dx_recv)

    arrived(CONV_Y, cy_recv)
    total = cy_send[pl.ds(y, 1)].reshape(3, 32, YL).astype(F32)
    for d in range(3):
        total = total + cy_recv[d].astype(F32)
    sum_rows[...] = total
    for zz in range(NZ):
        for m in range(3 * len(Y_TAPS)):
            part = sum_rows[m % 3, 4 * zz : 4 * zz + 4, 128 * (m // 3) : 128 * (m // 3) + 128]
            cyz_rows[zz, 4 * (m % 4) : 4 * (m % 4) + 4, 128 * (m // 4) : 128 * (m // 4) + 128] = part
    cyz_send[...] = cyz_rows[...].astype(BF)
    for d in Z_ORDER:
        send(CONV_YZ, cyz_send.at[(z + d) % NZ], cyz_recv.at[d - 1], zs[d - 1])
    sent(CONV_YZ, cyz_recv)

    arrived(CONV_Z, cz_recv)
    halves = [cz_send[pl.ds(z, 1)].reshape(3, 16, ZL).astype(F32), 0.0]
    for d in range(1, NZ):
        halves[d % 2] = halves[d % 2] + cz_recv[d - 1].astype(F32)
    for h in range(2):
        sum_rows[:, :16, :ZL] = halves[h]
        for yy in range(NY):
            for m in range(3 * len(Z_TAPS)):
                part = sum_rows[m % 3, 4 * yy : 4 * yy + 4, 128 * (m // 3) : 128 * (m // 3) + 128]
                czy_rows[yy, h, 4 * (m % 4) : 4 * (m % 4) + 4, 128 * (m // 4) : 128 * (m // 4) + 128] = part
    czy_send[...] = czy_rows[...].astype(BF)
    for d in Y_ORDER:
        send(CONV_ZY, czy_send.at[(y + d) % NY], czy_recv.at[d - 1], ys[d - 1])
    sent(CONV_ZY, czy_recv)

    arrived(DOWN_XY, dx_recv)
    total = dx_rows[pl.ds(xh, 1), pl.ds(l, 1), pl.ds(4 * y, 4)].reshape(4, 16, 128)
    for s in range(15):
        total = total + dx_recv[s].astype(F32)
    dz_send[...] = total.reshape(NZ, 8, 128)
    for d in Z_ORDER:
        send(DOWN_Z, dz_send.at[(z + d) % NZ], dz_recv.at[d - 1], zs[d - 1])
    sent(DOWN_Z, dz_recv)

    arrived(ACT, act_recv.at[pl.ds(0, 3)])
    for m in range(4):
        act_vmem[256 * m : 256 * m + 128] = act_recv[m][:, :64]
        act_vmem[256 * m + 128 : 256 * m + 256] = act_recv[m][:, 64:]
    act_write = pltpu.make_async_copy(act_vmem, act_out, local_sem.at[1])
    act_write.start()

    arrived(CONV_ZY, czy_recv)
    total = czy_send[pl.ds(y, 1)].reshape(2, 16, 128 * Z_BLOCKS).astype(F32)
    for d in range(3):
        total = total + czy_recv[d].astype(F32)
    last_sum[pl.ds(pair, 1), :, 128 * Y_BLOCKS :] = total[0:1]
    last_sum[pl.ds(1 - pair, 1), :, 128 * Y_BLOCKS :] = total[1:2]
    arrived(CONV_YZ, cyz_recv)
    halves = [cyz_send[pl.ds(z, 1)].astype(F32), 0.0]
    for d in range(1, NZ):
        halves[d % 2] = halves[d % 2] + cyz_recv[d - 1 : d].astype(F32)
    last_sum[pl.ds(pair, 1), :, : 128 * Y_BLOCKS] = halves[0]
    last_sum[pl.ds(1 - pair, 1), :, : 128 * Y_BLOCKS] = halves[1]
    for h in range(2):
        whole = last_sum[h]
        for q in range(2):
            pieces = [whole[:, 128 * b + 64 * q : 128 * b + 64 * q + 64] for b in range(Y_BLOCKS + Z_BLOCKS)]
            last_send[h, q] = jnp.concatenate(pieces, axis=1).astype(BF)

    def last(slot, h, q, to):
        send(CONV_LAST, last_send.at[h, q], last_recv.at[slot], to, received=CONV_LAST if slot else CONV_CORE)

    near_l, far_l = 2 * l, 2 - 2 * l

    @pl.when(xh != c)
    def _():
        last(1, 1 - l, 0, (w, far_l))
        last(1, 1 - l, 1, (w, far_l + 1))
        last(0, l, 1 - c, (w, other_c))

    @pl.when(xh == c)
    def _():
        last(2, l, 0, (across, near_l))
        last(2, l, 1, (across, near_l + 1))
        last(3, 1 - l, 0, (across, far_l))
        last(3, 1 - l, 1, (across, far_l + 1))

    arrived(DOWN_Z, dz_recv)
    total = dz_send[pl.ds(z, 1)].reshape(8, 128)
    for d in range(7):
        total = total + dz_recv[d]
    dl_send[...] = total
    send(DOWN_LAST, dl_send, dl_recv, (w, other_c))
    sent(DOWN_LAST, dl_send)

    @pl.when(xh != c)
    def _():
        remote(CONV_LAST, last_recv.at[pl.ds(0, 3)], last_recv.at[pl.ds(0, 3)], near[0]).wait_send()

    @pl.when(xh == c)
    def _():
        remote(CONV_LAST, last_recv, last_recv, near[0]).wait_send()
        arrived(CONV_CORE, last_recv.at[0])

    arrived(CONV_LAST, last_recv.at[pl.ds(1, 3)])
    own = last_send[pl.ds(l, 1), pl.ds(c, 1)].reshape(16, 64 * (Y_BLOCKS + Z_BLOCKS))
    conv = jnp.where(c == xh, last_recv[0], own).astype(F32)
    for slot in range(1, 4):
        conv = conv + last_recv[slot].astype(F32)
    conv = conv * factor
    for first, taps in ((0, Y_TAPS), (Y_BLOCKS, Z_TAPS)):
        for m in range(3 * len(taps)):
            i, j = taps[m // 3]
            at = 64 * (first + m // 4)
            cg_vmem[9 * i + 3 * j + m % 3] = conv[4 * (m % 4) : 4 * (m % 4) + 4, at : at + 64]
    cg_write = pltpu.make_async_copy(cg_vmem, cg_out, local_sem.at[2])
    cg_write.start()
    arrived(DOWN_LAST, dl_recv)
    theirs = dl_recv[...]
    both = jnp.concatenate([jnp.where(c == 0, total, theirs), jnp.where(c == 0, theirs, total)], axis=1)
    dg_vmem[...] = jnp.where(c == 0, both[:4], both[4:]) * factor
    dg_write = pltpu.make_async_copy(dg_vmem, dg_out, local_sem.at[3])
    dg_write.start()

    flush(range(GROUPS))
    for copy in (vg_write, act_write, cg_write, dg_write):
        copy.wait()


def write_out(*refs):
    arrays = (len(refs) - 1) // 2
    sems = refs[-1]
    copies = [
        pltpu.make_async_copy(src, dst, sems.at[s])
        for s, (src, dst) in enumerate(zip(refs[:arrays], refs[arrays:-1]))
    ]
    for copy in copies:
        copy.start()
    for copy in copies:
        copy.wait()


def on_device(volume, down_weight, conv_weight, cotangent):
    factor = 1.0 / (32 * math.sqrt(64))
    hbm = pl.BlockSpec(memory_space=pltpu.HBM)
    vmem = pl.BlockSpec(memory_space=pltpu.VMEM)
    scratch = [
        ((2, 8, 2, 64, 128), BF),
        ((1024, 256), BF),
        ((27, 256, 256), BF),
        ((4, 256, 64), BF),
        ((2, 8, 2, 64, 128), F32),
        ((256, 1024), BF),
        ((1024, 256), BF),
        ((2, 3, 10, 32, 128), BF),
        ((2, 3, 10, 32, 128), BF),
        ((3, 2, 18, 32, 128), BF),
        ((2, 128, 256), BF),
        ((4, 128, 256), BF),
        ((384, 1024), BF),
        ((384, 1024), BF),
        ((3, 256, 256), F32),
        ((4, 128, 128), BF),
        ((4, 128, 128), BF),
        ((4, 128, 128), BF),
        ((4, 128, 128), BF),
        ((1024, 64), BF),
        ((4, 3, 32, YL), BF),
        ((3, 3, 32, YL), BF),
        ((3, 32, YL), F32),
        ((8, 16, 128 * Y_BLOCKS), F32),
        ((8, 16, 128 * Y_BLOCKS), BF),
        ((7, 16, 128 * Y_BLOCKS), BF),
        ((8, 3, 16, ZL), BF),
        ((7, 3, 16, ZL), BF),
        ((4, 2, 16, 128 * Z_BLOCKS), F32),
        ((4, 2, 16, 128 * Z_BLOCKS), BF),
        ((3, 2, 16, 128 * Z_BLOCKS), BF),
        ((1024, 128), BF),
        ((1024, 128), BF),
        ((2, 2, 16, 16, 128), F32),
        ((2, 2, 16, 16, 128), BF),
        ((15, 4, 16, 128), BF),
        ((8, 8, 128), F32),
        ((7, 8, 128), F32),
        ((8, 128), F32),
        ((8, 128), F32),
        ((27, 4, 64), F32),
        ((4, 256), F32),
        ((2, 16, 128 * (Y_BLOCKS + Z_BLOCKS)), F32),
        ((2, 2, 16, 64 * (Y_BLOCKS + Z_BLOCKS)), BF),
        ((4, 16, 64 * (Y_BLOCKS + Z_BLOCKS)), BF),
    ]
    results = pl.pallas_call(
        functools.partial(kernel, factor),
        name="unet_level",
        out_shape=(
            jax.ShapeDtypeStruct((1024, 64), BF),
            jax.ShapeDtypeStruct((2, 8, 2, 64, 128), BF),
            jax.ShapeDtypeStruct((4, 256), F32),
            jax.ShapeDtypeStruct((27, 4, 64), F32),
        ),
        in_specs=[hbm] * 4,
        out_specs=(hbm,) * 4,
        scratch_shapes=[pltpu.VMEM(shape, dtype) for shape, dtype in scratch]
        + [
            pltpu.SemaphoreType.DMA((4,)),
            pltpu.SemaphoreType.DMA((GROUPS,)),
            pltpu.SemaphoreType.DMA((GROUPS,)),
        ],
        compiler_params=pltpu.CompilerParams(
            collective_id=0, has_side_effects=True, vmem_limit_bytes=56 * 1024 * 1024
        ),
        cost_estimate=pl.CostEstimate(flops=3200000000, bytes_accessed=8000000, transcendentals=65536),
    )(
        volume.reshape(2, 8, 2, 64, 128),
        down_weight,
        conv_weight,
        cotangent.reshape(4, 256, 64),
    )
    activated, volume_grad, down_grad, conv_grad = pl.pallas_call(
        write_out,
        name="write_out",
        out_shape=tuple(jax.ShapeDtypeStruct(r.shape, r.dtype) for r in results),
        in_specs=[vmem] * 4,
        out_specs=(hbm,) * 4,
        scratch_shapes=[pltpu.SemaphoreType.DMA((4,))],
    )(*results)
    return (
        activated.reshape(1, 32, 32, 64),
        volume_grad.reshape(2, 16, 64, 128),
        down_grad,
        conv_grad.transpose(0, 2, 1),
    )


def solution(mesh):
    placed = (P("wide", "narrow", None, None), P(), P(), P("wide", None, None, "narrow"))
    return jax.shard_map(
        on_device,
        mesh=mesh,
        in_specs=placed,
        out_specs=(
            P("wide", None, None, "narrow"),
            P("wide", "narrow", None, None),
            P(("wide", "narrow"), None),
            P(None, "narrow", "wide"),
        ),
        check_vma=False,
    )
```

```python
import functools
import math

import jax
import jax.numpy as jnp
from jax import lax
from jax.experimental import pallas as pl
from jax.experimental.pallas import tpu as pltpu
from jax.sharding import PartitionSpec as P

MESH = pl.DeviceIdType.MESH
VMEM_BYTES = 55040 * 1024
BF = jnp.bfloat16
F32 = jnp.float32
Y_TAPS = ((0, 0), (0, 1), (0, 2), (1, 0), (1, 1), (1, 2))
Z_TAPS = ((2, 0), (2, 1), (2, 2))
YL, ZL = 128 * len(Y_TAPS), 128 * len(Z_TAPS)
NY, NZ = 4, 8
Y_ORDER, Z_ORDER = (2, 1, 3), (4, 3, 5, 2, 6, 1, 7)

COT, DEEP_ROWS, DEEP_LOW, DEEP_HIGH, DEEP_OWN, DEEP_OUTER, DEEP_CORE, ACT = range(8)
GRAD_ROWS, GRAD_LOW, GRAD_HIGH, GRAD_SHARE, CONV_Y, CONV_YZ, CONV_Z, CONV_ZY = range(8, 16)
DOWN_C, DOWN_XY, DOWN_Z, CONV_LAST, CONV_CORE = range(16, 21)
GROUPS = 21
Y_BLOCKS, Z_BLOCKS = -(-3 * len(Y_TAPS) // 4), -(-3 * len(Z_TAPS) // 4)


def matmul(a, b):
    return jnp.dot(a, b, preferred_element_type=F32)


def matmul_nt(a, b):
    return lax.dot_general(a, b, (((1,), (1,)), ((), ())), preferred_element_type=F32)


def kernel(
    factor,
    vol_ref,
    dw_ref,
    cw_ref,
    cot_ref,
    act_out,
    vg_out,
    dg_out,
    cg_out,
    vol,
    dw,
    cw,
    cot,
    wide_f32,
    patches,
    patches_t,
    deep,
    grad,
    order,
    order_z,
    deep_all,
    grad_t_send,
    grad_t,
    grad_rows,
    grad_rows_z,
    acc,
    cot_send,
    cot_recv,
    act_send,
    act_recv,
    act_vmem,
    cy_send,
    cy_recv,
    sum_rows,
    cyz_rows,
    cyz_send,
    cyz_recv,
    cz_send,
    cz_recv,
    czy_rows,
    czy_send,
    czy_recv,
    dc_send,
    dc_recv,
    dx_rows,
    dx_send,
    dx_recv,
    dz_send,
    dz_recv,
    cg_vmem,
    dg_vmem,
    last_sum,
    last_send,
    last_recv,
    local_sem,
    send_sem,
    recv_sem,
):
    w = lax.axis_index("wide")
    n = lax.axis_index("narrow")
    y, z, xh = w // 16, (w // 2) % NZ, w % 2
    l, c = n // 2, n % 2
    pair = z % 2

    def wide_of(yy, zz, xx):
        return ((yy % NY) * NZ + zz % NZ) * 2 + xx

    near = [(w, (n + d) % 4) for d in range(1, 4)]
    up, down = (w + 1) % 64, (w + 63) % 64
    right, left = (n + 1) % 4, (n + 3) % 4
    depth = [(s, (n + d) % 4) for s in (up, down) for d in range(4)]
    ys = [(wide_of(y + d, z, xh), n) for d in range(1, NY)]
    zs = [(wide_of(y, z + d, xh), n) for d in range(1, NZ)]
    other_c = n + 1 - 2 * c
    zs_crossed = [(to, other_c) for to, _ in zs]
    across = wide_of(y, z, 1 - xh)
    other_l = (n + 2) % 4
    beside = wide_of(y, z + 1 - 2 * pair, xh)
    xys = [
        (dy, dx, dl, (wide_of(y + dy, z, (xh + dx) % 2), n + 2 * dl * (1 - 2 * l)))
        for dy in range(NY)
        for dx in range(2)
        for dl in range(2)
        if dy or dx or dl
    ]

    barrier = pltpu.get_barrier_semaphore()
    partners = near + depth + ys + zs + zs_crossed + [to for dy, dx, dl, to in xys if dy and (dx or dl)]
    for who in partners:
        pl.semaphore_signal(barrier, inc=1, device_id=who, device_id_type=MESH)

    def remote(number, src, dst, who, received=None):
        return pltpu.make_async_remote_copy(
            src_ref=src,
            dst_ref=dst,
            send_sem=send_sem.at[number],
            recv_sem=recv_sem.at[number if received is None else received],
            device_id=who,
            device_id_type=MESH,
        )

    def send(*args, **kwargs):
        remote(*args, **kwargs).start()

    def finish(number, ref, edge_ref, receiving):
        def wait(ref):
            copy = remote(number, ref, ref, near[0])
            if receiving:
                copy.wait_recv()
            else:
                copy.wait_send()

        if edge_ref is None:
            wait(ref)
        else:
            pl.when(inside)(lambda: wait(ref))
            pl.when(jnp.logical_not(inside))(lambda: wait(edge_ref))

    def arrived(number, ref, edge_ref=None):
        finish(number, ref, edge_ref, True)

    outgoing = []

    def sent(number, ref, edge_ref=None):
        outgoing.append((number, ref, edge_ref))

    def flush(numbers):
        for group in [group for group in outgoing if group[0] in numbers]:
            finish(*group, False)
            outgoing.remove(group)

    loads = [
        pltpu.make_async_copy(src, dst, local_sem.at[s])
        for s, (src, dst) in enumerate(((vol_ref, vol), (dw_ref, dw), (cot_ref, cot), (cw_ref, cw)))
    ]
    for copy in loads:
        copy.start()

    inside = (n == 1) | (n == 2)
    far = (w + 63 + 2 * xh) % 64

    def send_halos(buf, base):
        def rows(to, plane, received):
            for missing, who, first, at in ((3, n + 1, 8, 0), (0, n - 1, 1, 9)):

                @pl.when(n != missing)
                def _():
                    src = buf.at[:, 1, pl.ds(first, 1)]
                    send(base, src, buf.at[:, plane, pl.ds(at, 1)], (to, who), received=received)

        rows(w, 1, base)
        for to, s in ((far, 1 - xh), (across, xh)):
            rows(to, 2 * s, base + 1 + s)
        for to, s in ((far, 1 - xh), (across, xh)):
            planes = buf.at[:, 2 * s, pl.ds(1, 8)]
            send(base + 1, buf.at[:, 1, pl.ds(1, 8)], planes, (to, n), received=base + 1 + s)
        sent(base, buf.at[:, 1, pl.ds(0, 6)], buf.at[:, 1, pl.ds(0, 3)])
        sent(base + 1, buf.at[:, pl.ds(0, 2), pl.ds(0, 8)])

    def clear_rows(buf, plane):
        @pl.when(n == 0)
        def _():
            buf[:, plane, 0:1] = jnp.zeros((2, 1, 32, 128), BF)

        @pl.when(n == 3)
        def _():
            buf[:, plane, 9:10] = jnp.zeros((2, 1, 32, 128), BF)

    def rows_arrive(buf, base):
        arrived(base, buf.at[:, 1, pl.ds(0, 2)], buf.at[:, 1, pl.ds(0, 1)])
        clear_rows(buf, 1)

    def plane_arrives(buf, base, plane):
        arrived(base + 1 + plane // 2, buf.at[:, plane], buf.at[:, plane, pl.ds(0, 9)])
        clear_rows(buf, plane)

        @pl.when(w == (0 if plane == 0 else 63))
        def _():
            buf[:, plane] = jnp.zeros((2, 10, 32, 128), BF)

    loads[0].wait()
    wide_f32[...] = vol[...].astype(F32)
    for a in range(2):
        for b in range(2):
            for e in range(2):
                part = wide_f32[a, :, b, pl.ds(e, 32, stride=2), :].reshape(256, 128).astype(BF)
                at = (4 * a + 2 * b + e) * 128
                patches[:, at : at + 128] = part
    loads[1].wait()
    cells = matmul(patches[...], dw[...]).astype(BF)
    for half in range(2):
        deep[half, 1, 1:9] = cells[:, 128 * half : 128 * half + 128].reshape(8, 32, 128)

    from_rows, to_rows = pl.ds(c, 9), pl.ds(9 * c, 9)
    outer, inner = 2 * pair, 2 - 2 * pair

    def to_core(src, plane, chip):
        send(DEEP_CORE, src, deep_all.at[plane, chip, to_rows], (w, other_c))

    def share_core(plane):
        deep_all[plane, pl.ds(pair, 1), to_rows] = deep[pl.ds(pair, 1), plane, from_rows]
        to_core(deep.at[pair, plane, from_rows], plane, pair)

    def share_across(plane, received):
        src = deep.at[1 - pair, plane, from_rows]
        send(DEEP_OWN, src, deep_all.at[plane, pair, to_rows], (beside, n), received=received)

    def pass_on(plane, received):
        theirs = deep_all.at[plane, 1 - pair, to_rows]
        arrived(received, theirs)
        to_core(theirs, plane, 1 - pair)

    pl.semaphore_wait(barrier, len(partners))
    send_halos(deep, DEEP_ROWS)
    loads[2].wait()
    for m in range(4):
        cot_send[m] = jnp.concatenate([cot[m, :128], cot[m, 128:]], axis=1)
    cot_recv[pl.ds(n, 1)] = cot_send[pl.ds(n, 1)]
    for d in range(1, 4):
        send(COT, cot_send.at[(n + d) % 4], cot_recv.at[n], near[d - 1])
    sent(COT, cot_send.at[pl.ds(0, 3)])
    cyz_rows[...] = jnp.zeros_like(cyz_rows)
    czy_rows[...] = jnp.zeros_like(czy_rows)

    for s in range(4):
        block = patches[:, 256 * s : 256 * s + 256].astype(F32)
        patches_t[256 * s : 256 * s + 256, :] = block.T.astype(BF)

    row = lax.broadcasted_iota(jnp.int32, (256, 256), 0)
    column = lax.broadcasted_iota(jnp.int32, (256, 256), 1)
    q = row % 128
    source = (q // 32) * 64 + ((q // 4) % 8) * 8 + (1 - row // 128) * 4 + q % 4
    order[...] = jnp.where(column == source, 1.0, 0.0).astype(BF)
    row = lax.broadcasted_iota(jnp.int32, (128, 128), 0)
    column = lax.broadcasted_iota(jnp.int32, (128, 128), 1)
    source = ((row // 4) % 4) * 32 + (row // 16) * 4 + row % 4
    order_z[...] = jnp.where(column == source, 1.0, 0.0).astype(BF)

    def window(buf, plane, first):
        return [buf[half, plane, first : first + 8].reshape(256, 128) for half in range(2)]

    def shifted(value, by, masked):
        column = lax.broadcasted_iota(jnp.int32, value.shape, 0) % 32
        return jnp.where(column == masked, 0.0, pltpu.roll(value, by, 0))

    loads[3].wait()
    for i in (1, 0, 2):
        if i == 1:
            rows_arrive(deep, DEEP_ROWS)
        else:
            plane_arrives(deep, DEEP_ROWS, i)
        share_core(i)
        if i == 1:
            share_across(1, DEEP_OWN)
        else:

            @pl.when(outer == i)
            def _():
                share_across(i, DEEP_OUTER)

        slab = jnp.concatenate(window(deep, i, 0) + window(deep, i, 1) + window(deep, i, 2), axis=1)
        for k in range(3):
            weights = jnp.concatenate([cw[9 * i + 3 * j + k] for j in range(3)], axis=0)
            term = matmul(slab, weights)
            acc[k] = term if i == 1 else acc[k] + term
    deep_all[pl.ds(outer, 1), pl.ds(1 - pair, 1), to_rows] = deep[pl.ds(pair, 1), pl.ds(inner, 1), from_rows]
    to_core(deep.at[pair, inner, from_rows], outer, 1 - pair)
    sent(DEEP_OWN, deep.at[:, 1, pl.ds(0, 9)])
    preact = shifted(acc[0], 1, 0) + acc[1] + shifted(acc[2], 255, 31)

    arrived(COT, cot_recv.at[pl.ds(0, 3)])
    cotangent = jnp.concatenate(
        [
            jnp.concatenate([cot_recv[m][:, :64], cot_recv[m][:, 64:]], axis=0)
            for m in range(4)
        ],
        axis=1,
    ).astype(F32)
    sigma = 1.0 / (1.0 + jnp.exp(-preact))
    activated = (preact * sigma).astype(BF)
    grad_pre = (cotangent * (sigma * (1.0 + preact * (1.0 - sigma)))).astype(BF)
    for half in range(2):
        grad[half, 1, 1:9] = grad_pre[:, 128 * half : 128 * half + 128].reshape(8, 32, 128)

    turned = matmul_nt(order[...], grad_pre).astype(BF)
    grad_t_send[0] = turned[:128]
    grad_t_send[1] = turned[128:]
    slot = 2 * pair + c
    grad_t[pl.ds(slot, 1)] = grad_t_send[pl.ds(c, 1)]
    mine = grad_t.at[slot]
    send(GRAD_SHARE, grad_t_send.at[1 - c], mine, (beside, other_c))
    send(GRAD_SHARE, grad_t_send.at[c], mine, (beside, n))
    send(GRAD_SHARE, grad_t_send.at[1 - c], mine, (w, other_c))
    sent(GRAD_SHARE, grad_t.at[pl.ds(0, 3)])
    send_halos(grad, GRAD_ROWS)

    pass_on(1, DEEP_OWN)
    pass_on(inner, DEEP_OUTER)
    sent(DEEP_CORE, deep_all.at[:, :, pl.ds(0, 9)])

    arrived(GRAD_SHARE, grad_t.at[pl.ds(0, 3)])
    lane = lax.broadcasted_iota(jnp.int32, (128, 256), 1) % 32
    for m in range(4):
        block = grad_t[m].astype(F32)
        at = 256 * m
        grad_rows[0:128, at : at + 256] = jnp.where(lane == 31, 0.0, pltpu.roll(block, 255, 1)).astype(BF)
        grad_rows[128:256, at : at + 256] = grad_t[m]
        grad_rows[256:384, at : at + 256] = jnp.where(lane == 0, 0.0, pltpu.roll(block, 1, 1)).astype(BF)
    def cells_at(i, j):
        return jnp.concatenate([deep_all[i, s, j : j + 16].reshape(512, 128) for s in range(2)], axis=0)

    arrived(DEEP_CORE, deep_all.at[:, :, pl.ds(0, 9)])
    slab = jnp.concatenate([cells_at(i, j) for i, j in Y_TAPS], axis=1)
    term = matmul(grad_rows[...], slab).astype(BF)
    for yy in range(NY):
        for k in range(3):
            at = 128 * k + 32 * yy
            cy_send[yy, k] = term[at : at + 32]
    for d in Y_ORDER:
        send(CONV_Y, cy_send.at[(y + d) % NY], cy_recv.at[d - 1], ys[d - 1])
    sent(CONV_Y, cy_recv)
    for k in range(3):
        grad_rows_z[128 * k : 128 * k + 128, :] = matmul(order_z[...], grad_rows[128 * k : 128 * k + 128, :]).astype(BF)
    slab = jnp.concatenate([cells_at(i, j) for i, j in Z_TAPS], axis=1)
    term = matmul(grad_rows_z[...], slab).astype(BF)
    for zz in range(NZ):
        for k in range(3):
            at = 128 * k + 16 * zz
            cz_send[zz, k] = term[at : at + 16]
    flush((GRAD_ROWS, GRAD_LOW))
    for d in Z_ORDER:
        send(CONV_Z, cz_send.at[(z + d) % NZ], cz_recv.at[d - 1], zs[d - 1])
    sent(CONV_Z, cz_recv)

    for i in (1, 2, 0):
        plane = 2 - i
        if i == 1:
            rows_arrive(grad, GRAD_ROWS)
        else:
            plane_arrives(grad, GRAD_ROWS, plane)
        slab = jnp.concatenate(
            window(grad, plane, 2) + window(grad, plane, 1) + window(grad, plane, 0), axis=1
        )
        for k in range(3):
            weights = jnp.concatenate([cw[9 * i + 3 * j + k] for j in range(3)], axis=1)
            term = matmul_nt(slab, weights)
            acc[k] = term if i == 1 else acc[k] + term
    grad_deep = (shifted(acc[0], 255, 31) + acc[1] + shifted(acc[2], 1, 0)).astype(BF)

    partial = matmul(patches_t[...], grad_deep)
    low, high = partial[:, :128], partial[:, 128:]
    dc_send[...] = jnp.where(c == 0, high, low).astype(BF)
    send(DOWN_C, dc_send, dc_recv, (w, other_c))
    sent(DOWN_C, dc_send)
    kept = jnp.where(c == 0, low, high)

    for m in range(4):
        part = activated[:, 64 * m : 64 * m + 64]
        act_send[m] = jnp.concatenate([part[:128], part[128:]], axis=1)
    act_recv[pl.ds(n, 1)] = act_send[pl.ds(n, 1)]
    for d in range(1, 4):
        send(ACT, act_send.at[(n + d) % 4], act_recv.at[n], near[d - 1])
    sent(ACT, act_send.at[pl.ds(0, 3)])

    spread = matmul_nt(grad_deep, dw[...])
    for a in range(2):
        for b in range(2):
            for e in range(2):
                at = (4 * a + 2 * b + e) * 128
                wide_f32[a, :, b, pl.ds(e, 32, stride=2), :] = spread[:, at : at + 128].reshape(8, 32, 128)
    vol[...] = wide_f32[...].astype(BF)
    vg_write = pltpu.make_async_copy(vol, vg_out, local_sem.at[0])
    vg_write.start()

    arrived(DOWN_C, dc_recv)
    total = (kept + dc_recv[...].astype(F32)).reshape(16, 2, 2, 2, 8, 128)
    for xx in range(2):
        for ll in range(2):
            for zz in range(2):
                dx_rows[xx, ll, :, 8 * zz : 8 * zz + 8] = total[:, zz, xx, ll]
    dx_send[...] = dx_rows[...].astype(BF)
    for s, (dy, dx, dl, to) in enumerate(xys):
        src = dx_send.at[(xh + dx) % 2, (l + dl) % 2, pl.ds(4 * ((y + dy) % NY), 4)]
        send(DOWN_XY, src, dx_recv.at[s], to)
    sent(DOWN_XY, dx_recv)

    arrived(CONV_Y, cy_recv)
    total = cy_send[pl.ds(y, 1)].reshape(3, 32, YL).astype(F32)
    for d in range(3):
        total = total + cy_recv[d].astype(F32)
    sum_rows[...] = total
    for zz in range(NZ):
        for m in range(3 * len(Y_TAPS)):
            part = sum_rows[m % 3, 4 * zz : 4 * zz + 4, 128 * (m // 3) : 128 * (m // 3) + 128]
            cyz_rows[zz, 4 * (m % 4) : 4 * (m % 4) + 4, 128 * (m // 4) : 128 * (m // 4) + 128] = part
    cyz_send[...] = cyz_rows[...].astype(BF)
    for d in Z_ORDER:
        send(CONV_YZ, cyz_send.at[(z + d) % NZ], cyz_recv.at[d - 1], zs[d - 1])
    sent(CONV_YZ, cyz_recv)

    arrived(CONV_Z, cz_recv)
    halves = [cz_send[pl.ds(z, 1)].reshape(3, 16, ZL).astype(F32), 0.0]
    for d in range(1, NZ):
        halves[d % 2] = halves[d % 2] + cz_recv[d - 1].astype(F32)
    for h in range(2):
        sum_rows[:, :16, :ZL] = halves[h]
        for yy in range(NY):
            for m in range(3 * len(Z_TAPS)):
                part = sum_rows[m % 3, 4 * yy : 4 * yy + 4, 128 * (m // 3) : 128 * (m // 3) + 128]
                czy_rows[yy, h, 4 * (m % 4) : 4 * (m % 4) + 4, 128 * (m // 4) : 128 * (m // 4) + 128] = part
    czy_send[...] = czy_rows[...].astype(BF)
    for d in Y_ORDER:
        send(CONV_ZY, czy_send.at[(y + d) % NY], czy_recv.at[d - 1], ys[d - 1])
    sent(CONV_ZY, czy_recv)

    arrived(DOWN_XY, dx_recv)
    total = dx_rows[pl.ds(xh, 1), pl.ds(l, 1), pl.ds(4 * y, 4)].reshape(4, 16, 128)
    for s in range(15):
        total = total + dx_recv[s].astype(F32)
    dz_send[...] = total.reshape(NZ, 8, 128)
    for d in Z_ORDER:
        send(DOWN_Z, dz_send.at[(z + d) % NZ], dz_recv.at[NZ - 1 + d], zs_crossed[d - 1])
        send(DOWN_Z, dz_send.at[(z + d) % NZ], dz_recv.at[d - 1], zs[d - 1])
    send(DOWN_Z, dz_send.at[z], dz_recv.at[NZ - 1], (w, other_c))
    sent(DOWN_Z, dz_recv)

    arrived(ACT, act_recv.at[pl.ds(0, 3)])
    for m in range(4):
        act_vmem[256 * m : 256 * m + 128] = act_recv[m][:, :64]
        act_vmem[256 * m + 128 : 256 * m + 256] = act_recv[m][:, 64:]
    act_write = pltpu.make_async_copy(act_vmem, act_out, local_sem.at[1])
    act_write.start()

    arrived(CONV_ZY, czy_recv)
    total = czy_send[pl.ds(y, 1)].reshape(2, 16, 128 * Z_BLOCKS).astype(F32)
    for d in range(3):
        total = total + czy_recv[d].astype(F32)
    last_sum[pl.ds(pair, 1), :, 128 * Y_BLOCKS :] = total[0:1]
    last_sum[pl.ds(1 - pair, 1), :, 128 * Y_BLOCKS :] = total[1:2]
    arrived(CONV_YZ, cyz_recv)
    halves = [cyz_send[pl.ds(z, 1)].astype(F32), 0.0]
    for d in range(1, NZ):
        halves[d % 2] = halves[d % 2] + cyz_recv[d - 1 : d].astype(F32)
    last_sum[pl.ds(pair, 1), :, : 128 * Y_BLOCKS] = halves[0]
    last_sum[pl.ds(1 - pair, 1), :, : 128 * Y_BLOCKS] = halves[1]
    for h in range(2):
        whole = last_sum[h]
        for q in range(2):
            pieces = [whole[:, 128 * b + 64 * q : 128 * b + 64 * q + 64] for b in range(Y_BLOCKS + Z_BLOCKS)]
            last_send[h, q] = jnp.concatenate(pieces, axis=1).astype(BF)

    def last(slot, h, q, to):
        send(CONV_LAST, last_send.at[h, q], last_recv.at[slot], to, received=CONV_LAST if slot else CONV_CORE)

    near_l, far_l = 2 * l, 2 - 2 * l

    @pl.when(xh != c)
    def _():
        last(1, 1 - l, 0, (w, far_l))
        last(1, 1 - l, 1, (w, far_l + 1))
        last(0, l, 1 - c, (w, other_c))

    @pl.when(xh == c)
    def _():
        last(2, l, 0, (across, near_l))
        last(2, l, 1, (across, near_l + 1))
        last(3, 1 - l, 0, (across, far_l))
        last(3, 1 - l, 1, (across, far_l + 1))

    arrived(DOWN_Z, dz_recv)
    total = dz_send[pl.ds(z, 1)].reshape(8, 128)
    for d in range(NZ - 1):
        total = total + dz_recv[d]
    theirs = dz_recv[NZ - 1]
    for d in range(NZ, 2 * NZ - 1):
        theirs = theirs + dz_recv[d]
    both = jnp.concatenate([jnp.where(c == 0, total, theirs), jnp.where(c == 0, theirs, total)], axis=1)
    dg_vmem[...] = jnp.where(c == 0, both[:4], both[4:]) * factor
    dg_write = pltpu.make_async_copy(dg_vmem, dg_out, local_sem.at[3])
    dg_write.start()

    @pl.when(xh != c)
    def _():
        remote(CONV_LAST, last_recv.at[pl.ds(0, 3)], last_recv.at[pl.ds(0, 3)], near[0]).wait_send()

    @pl.when(xh == c)
    def _():
        remote(CONV_LAST, last_recv, last_recv, near[0]).wait_send()
        arrived(CONV_CORE, last_recv.at[0])

    arrived(CONV_LAST, last_recv.at[pl.ds(1, 3)])
    own = last_send[pl.ds(l, 1), pl.ds(c, 1)].reshape(16, 64 * (Y_BLOCKS + Z_BLOCKS))
    conv = jnp.where(c == xh, last_recv[0], own).astype(F32)
    for slot in range(1, 4):
        conv = conv + last_recv[slot].astype(F32)
    conv = conv * factor
    for first, taps in ((0, Y_TAPS), (Y_BLOCKS, Z_TAPS)):
        for m in range(3 * len(taps)):
            i, j = taps[m // 3]
            at = 64 * (first + m // 4)
            cg_vmem[9 * i + 3 * j + m % 3] = conv[4 * (m % 4) : 4 * (m % 4) + 4, at : at + 64]
    cg_write = pltpu.make_async_copy(cg_vmem, cg_out, local_sem.at[2])
    cg_write.start()
    flush(range(GROUPS))
    for copy in (vg_write, act_write, cg_write, dg_write):
        copy.wait()


def write_out(*refs):
    arrays = (len(refs) - 1) // 2
    sems = refs[-1]
    copies = [
        pltpu.make_async_copy(src, dst, sems.at[s])
        for s, (src, dst) in enumerate(zip(refs[:arrays], refs[arrays:-1]))
    ]
    for copy in copies:
        copy.start()
    for copy in copies:
        copy.wait()


def on_device(volume, down_weight, conv_weight, cotangent):
    factor = 1.0 / (32 * math.sqrt(64))
    hbm = pl.BlockSpec(memory_space=pltpu.HBM)
    vmem = pl.BlockSpec(memory_space=pltpu.VMEM)
    scratch = [
        ((2, 8, 2, 64, 128), BF),
        ((1024, 256), BF),
        ((27, 256, 256), BF),
        ((4, 256, 64), BF),
        ((2, 8, 2, 64, 128), F32),
        ((256, 1024), BF),
        ((1024, 256), BF),
        ((2, 3, 10, 32, 128), BF),
        ((2, 3, 10, 32, 128), BF),
        ((256, 256), BF),
        ((128, 128), BF),
        ((3, 2, 18, 32, 128), BF),
        ((2, 128, 256), BF),
        ((4, 128, 256), BF),
        ((384, 1024), BF),
        ((384, 1024), BF),
        ((3, 256, 256), F32),
        ((4, 128, 128), BF),
        ((4, 128, 128), BF),
        ((4, 128, 128), BF),
        ((4, 128, 128), BF),
        ((1024, 64), BF),
        ((4, 3, 32, YL), BF),
        ((3, 3, 32, YL), BF),
        ((3, 32, YL), F32),
        ((8, 16, 128 * Y_BLOCKS), F32),
        ((8, 16, 128 * Y_BLOCKS), BF),
        ((7, 16, 128 * Y_BLOCKS), BF),
        ((8, 3, 16, ZL), BF),
        ((7, 3, 16, ZL), BF),
        ((4, 2, 16, 128 * Z_BLOCKS), F32),
        ((4, 2, 16, 128 * Z_BLOCKS), BF),
        ((3, 2, 16, 128 * Z_BLOCKS), BF),
        ((1024, 128), BF),
        ((1024, 128), BF),
        ((2, 2, 16, 16, 128), F32),
        ((2, 2, 16, 16, 128), BF),
        ((15, 4, 16, 128), BF),
        ((8, 8, 128), F32),
        ((15, 8, 128), F32),
        ((27, 4, 64), F32),
        ((4, 256), F32),
        ((2, 16, 128 * (Y_BLOCKS + Z_BLOCKS)), F32),
        ((2, 2, 16, 64 * (Y_BLOCKS + Z_BLOCKS)), BF),
        ((4, 16, 64 * (Y_BLOCKS + Z_BLOCKS)), BF),
    ]
    results = pl.pallas_call(
        functools.partial(kernel, factor),
        name="unet_level",
        out_shape=(
            jax.ShapeDtypeStruct((1024, 64), BF),
            jax.ShapeDtypeStruct((2, 8, 2, 64, 128), BF),
            jax.ShapeDtypeStruct((4, 256), F32),
            jax.ShapeDtypeStruct((27, 4, 64), F32),
        ),
        in_specs=[hbm] * 4,
        out_specs=(hbm,) * 4,
        scratch_shapes=[pltpu.VMEM(shape, dtype) for shape, dtype in scratch]
        + [
            pltpu.SemaphoreType.DMA((4,)),
            pltpu.SemaphoreType.DMA((GROUPS,)),
            pltpu.SemaphoreType.DMA((GROUPS,)),
        ],
        compiler_params=pltpu.CompilerParams(
            collective_id=0, has_side_effects=True, vmem_limit_bytes=VMEM_BYTES
        ),
        cost_estimate=pl.CostEstimate(flops=3200000000, bytes_accessed=8000000, transcendentals=65536),
    )(
        volume.reshape(2, 8, 2, 64, 128),
        down_weight,
        conv_weight,
        cotangent.reshape(4, 256, 64),
    )
    activated, volume_grad, down_grad, conv_grad = pl.pallas_call(
        write_out,
        name="write_out",
        out_shape=tuple(jax.ShapeDtypeStruct(r.shape, r.dtype) for r in results),
        in_specs=[vmem] * 4,
        out_specs=(hbm,) * 4,
        scratch_shapes=[pltpu.SemaphoreType.DMA((4,))],
        compiler_params=pltpu.CompilerParams(vmem_limit_bytes=VMEM_BYTES),
    )(*results)
    return (
        activated.reshape(1, 32, 32, 64),
        volume_grad.reshape(2, 16, 64, 128),
        down_grad,
        conv_grad.transpose(0, 2, 1),
    )


def solution(mesh):
    placed = (P("wide", "narrow", None, None), P(), P(), P("wide", None, None, "narrow"))
    return jax.shard_map(
        on_device,
        mesh=mesh,
        in_specs=placed,
        out_specs=(
            P("wide", None, None, "narrow"),
            P("wide", "narrow", None, None),
            P(("wide", "narrow"), None),
            P(None, "narrow", "wide"),
        ),
        check_vma=False,
    )
```

```python
import functools
import math

import jax
import jax.numpy as jnp
from jax import lax
from jax.experimental import pallas as pl
from jax.experimental.pallas import tpu as pltpu
from jax.sharding import PartitionSpec as P

MESH = pl.DeviceIdType.MESH
VMEM_BYTES = 54784 * 1024
BF = jnp.bfloat16
F32 = jnp.float32
Y_TAPS = ((0, 0), (0, 1), (0, 2), (1, 0), (1, 1), (1, 2))
Z_TAPS = ((2, 0), (2, 1), (2, 2))
YL, ZL = 128 * len(Y_TAPS), 128 * len(Z_TAPS)
NY, NZ = 4, 8
Y_ORDER, Z_ORDER = (2, 1, 3), (4, 3, 5, 2, 6, 1, 7)

COT, DEEP_ROWS, DEEP_LOW, DEEP_HIGH, DEEP_OWN, DEEP_OUTER, DEEP_CORE, ACT = range(8)
GRAD_ROWS, GRAD_LOW, GRAD_HIGH, GRAD_SHARE, CONV_Y, CONV_YZ, CONV_Z, CONV_ZY = range(8, 16)
DOWN_C, DOWN_XY, DOWN_Z, CONV_LAST, CONV_CORE = range(16, 21)
GROUPS = 21
Y_BLOCKS, Z_BLOCKS = -(-3 * len(Y_TAPS) // 4), -(-3 * len(Z_TAPS) // 4)


def matmul(a, b):
    return jnp.dot(a, b, preferred_element_type=F32)


def matmul_nt(a, b):
    return lax.dot_general(a, b, (((1,), (1,)), ((), ())), preferred_element_type=F32)


def kernel(
    factor,
    vol_ref,
    dw_ref,
    cw_ref,
    cot_ref,
    act_out,
    vg_out,
    dg_out,
    cg_out,
    vol,
    dw,
    cw,
    cot,
    wide_f32,
    patches,
    patches_t,
    deep,
    grad,
    order,
    order_z,
    deep_all,
    grad_t_send,
    grad_t,
    grad_rows,
    grad_rows_z,
    acc,
    cot_send,
    cot_recv,
    act_send,
    act_recv,
    act_vmem,
    cy_send,
    cy_recv,
    sum_rows,
    cyz_rows,
    cyz_send,
    cyz_recv,
    cz_send,
    cz_recv,
    czy_rows,
    czy_send,
    czy_recv,
    dc_send,
    dc_recv,
    dx_rows,
    dx_send,
    dx_recv,
    dz_send,
    dz_recv,
    cg_vmem,
    dg_vmem,
    last_sum,
    last_send,
    last_recv,
    local_sem,
    send_sem,
    recv_sem,
):
    w = lax.axis_index("wide")
    n = lax.axis_index("narrow")
    y, z, xh = w // 16, (w // 2) % NZ, w % 2
    l, c = n // 2, n % 2
    pair = z % 2

    def wide_of(yy, zz, xx):
        return ((yy % NY) * NZ + zz % NZ) * 2 + xx

    near = [(w, (n + d) % 4) for d in range(1, 4)]
    up, down = (w + 1) % 64, (w + 63) % 64
    right, left = (n + 1) % 4, (n + 3) % 4
    depth = [(s, (n + d) % 4) for s in (up, down) for d in range(4)]
    ys = [(wide_of(y + d, z, xh), n) for d in range(1, NY)]
    zs = [(wide_of(y, z + d, xh), n) for d in range(1, NZ)]
    other_c = n + 1 - 2 * c
    zs_crossed = [(to, other_c) for to, _ in zs]
    across = wide_of(y, z, 1 - xh)
    other_l = (n + 2) % 4
    beside = wide_of(y, z + 1 - 2 * pair, xh)
    xys = [
        (dy, dx, dl, (wide_of(y + dy, z, (xh + dx) % 2), n + 2 * dl * (1 - 2 * l)))
        for dy in (2, 1, 3, 0)
        for dx, dl in ((1, 0), (0, 1), (1, 1), (0, 0))
        if dy or dx or dl
    ]

    loads = [
        pltpu.make_async_copy(src, dst, local_sem.at[s])
        for s, (src, dst) in enumerate(((vol_ref, vol), (dw_ref, dw), (cot_ref, cot), (cw_ref, cw)))
    ]
    for copy in loads[:3]:
        copy.start()

    barrier = pltpu.get_barrier_semaphore()
    partners = near + depth + ys + zs + zs_crossed + [to for dy, dx, dl, to in xys if dy and (dx or dl)]
    for who in partners:
        pl.semaphore_signal(barrier, inc=1, device_id=who, device_id_type=MESH)

    def remote(number, src, dst, who, received=None):
        return pltpu.make_async_remote_copy(
            src_ref=src,
            dst_ref=dst,
            send_sem=send_sem.at[number],
            recv_sem=recv_sem.at[number if received is None else received],
            device_id=who,
            device_id_type=MESH,
        )

    def send(*args, **kwargs):
        remote(*args, **kwargs).start()

    def finish(number, ref, edge_ref, receiving):
        def wait(ref):
            copy = remote(number, ref, ref, near[0])
            if receiving:
                copy.wait_recv()
            else:
                copy.wait_send()

        if edge_ref is None:
            wait(ref)
        else:
            pl.when(inside)(lambda: wait(ref))
            pl.when(jnp.logical_not(inside))(lambda: wait(edge_ref))

    def arrived(number, ref, edge_ref=None):
        finish(number, ref, edge_ref, True)

    outgoing = []

    def sent(number, ref, edge_ref=None):
        outgoing.append((number, ref, edge_ref))

    def flush(numbers):
        for group in [group for group in outgoing if group[0] in numbers]:
            finish(*group, False)
            outgoing.remove(group)


    inside = (n == 1) | (n == 2)
    far = (w + 63 + 2 * xh) % 64

    def send_halos(buf, base):
        def rows(to, plane, received):
            for missing, who, first, at in ((3, n + 1, 8, 0), (0, n - 1, 1, 9)):

                @pl.when(n != missing)
                def _():
                    src = buf.at[:, 1, pl.ds(first, 1)]
                    send(base, src, buf.at[:, plane, pl.ds(at, 1)], (to, who), received=received)

        rows(w, 1, base)
        for to, s in ((far, 1 - xh), (across, xh)):
            rows(to, 2 * s, base + 1 + s)
        for to, s in ((far, 1 - xh), (across, xh)):
            planes = buf.at[:, 2 * s, pl.ds(1, 8)]
            send(base + 1, buf.at[:, 1, pl.ds(1, 8)], planes, (to, n), received=base + 1 + s)
        sent(base, buf.at[:, 1, pl.ds(0, 6)], buf.at[:, 1, pl.ds(0, 3)])
        sent(base + 1, buf.at[:, pl.ds(0, 2), pl.ds(0, 8)])

    def clear_rows(buf, plane):
        @pl.when(n == 0)
        def _():
            buf[:, plane, 0:1] = jnp.zeros((2, 1, 32, 128), BF)

        @pl.when(n == 3)
        def _():
            buf[:, plane, 9:10] = jnp.zeros((2, 1, 32, 128), BF)

    def rows_arrive(buf, base):
        arrived(base, buf.at[:, 1, pl.ds(0, 2)], buf.at[:, 1, pl.ds(0, 1)])
        clear_rows(buf, 1)

    def plane_arrives(buf, base, plane):
        arrived(base + 1 + plane // 2, buf.at[:, plane], buf.at[:, plane, pl.ds(0, 9)])
        clear_rows(buf, plane)

        @pl.when(w == (0 if plane == 0 else 63))
        def _():
            buf[:, plane] = jnp.zeros((2, 10, 32, 128), BF)

    loads[0].wait()
    wide_f32[...] = vol[...].astype(F32)
    for a in range(2):
        for b in range(2):
            for e in range(2):
                part = wide_f32[a, :, b, pl.ds(e, 32, stride=2), :].reshape(256, 128).astype(BF)
                at = (4 * a + 2 * b + e) * 128
                patches[:, at : at + 128] = part
    loads[1].wait()
    loads[3].start()
    cells = matmul(patches[...], dw[...]).astype(BF)
    for half in range(2):
        deep[half, 1, 1:9] = cells[:, 128 * half : 128 * half + 128].reshape(8, 32, 128)

    from_rows, to_rows = pl.ds(c, 9), pl.ds(9 * c, 9)
    outer, inner = 2 * pair, 2 - 2 * pair

    def to_core(src, plane, chip):
        send(DEEP_CORE, src, deep_all.at[plane, chip, to_rows], (w, other_c))

    def share_core(plane):
        deep_all[plane, pl.ds(pair, 1), to_rows] = deep[pl.ds(pair, 1), plane, from_rows]
        to_core(deep.at[pair, plane, from_rows], plane, pair)

    def share_across(plane, received):
        src = deep.at[1 - pair, plane, from_rows]
        send(DEEP_OWN, src, deep_all.at[plane, pair, to_rows], (beside, n), received=received)

    def pass_on(plane, received):
        theirs = deep_all.at[plane, 1 - pair, to_rows]
        arrived(received, theirs)
        to_core(theirs, plane, 1 - pair)

    loads[2].wait()
    for m in range(4):
        cot_send[m] = jnp.concatenate([cot[m, :128], cot[m, 128:]], axis=1)
    cot_recv[pl.ds(n, 1)] = cot_send[pl.ds(n, 1)]
    pl.semaphore_wait(barrier, len(partners))
    send_halos(deep, DEEP_ROWS)
    for d in (1, 3, 2):
        send(COT, cot_send.at[(n + d) % 4], cot_recv.at[n], near[d - 1])
    sent(COT, cot_send.at[pl.ds(0, 3)])
    cyz_rows[...] = jnp.zeros_like(cyz_rows)
    czy_rows[...] = jnp.zeros_like(czy_rows)

    for s in range(4):
        block = patches[:, 256 * s : 256 * s + 256].astype(F32)
        patches_t[256 * s : 256 * s + 256, :] = block.T.astype(BF)

    row = lax.broadcasted_iota(jnp.int32, (256, 256), 0)
    column = lax.broadcasted_iota(jnp.int32, (256, 256), 1)
    q = row % 128
    source = (q // 32) * 64 + ((q // 4) % 8) * 8 + (1 - row // 128) * 4 + q % 4
    order[...] = jnp.where(column == source, 1.0, 0.0).astype(BF)
    row = lax.broadcasted_iota(jnp.int32, (128, 128), 0)
    column = lax.broadcasted_iota(jnp.int32, (128, 128), 1)
    source = ((row // 4) % 4) * 32 + (row // 16) * 4 + row % 4
    order_z[...] = jnp.where(column == source, 1.0, 0.0).astype(BF)

    def window(buf, plane, first):
        return [buf[half, plane, first : first + 8].reshape(256, 128) for half in range(2)]

    def shifted(value, by, masked):
        column = lax.broadcasted_iota(jnp.int32, value.shape, 0) % 32
        return jnp.where(column == masked, 0.0, pltpu.roll(value, by, 0))

    loads[3].wait()
    for i in (1, 0, 2):
        if i == 1:
            rows_arrive(deep, DEEP_ROWS)
        else:
            plane_arrives(deep, DEEP_ROWS, i)
        share_core(i)
        if i == 1:
            share_across(1, DEEP_OWN)
        else:

            @pl.when(outer == i)
            def _():
                share_across(i, DEEP_OUTER)

        slab = jnp.concatenate(window(deep, i, 0) + window(deep, i, 1) + window(deep, i, 2), axis=1)
        for k in range(3):
            weights = jnp.concatenate([cw[9 * i + 3 * j + k] for j in range(3)], axis=0)
            term = matmul(slab, weights)
            acc[k] = term if i == 1 else acc[k] + term
    deep_all[pl.ds(outer, 1), pl.ds(1 - pair, 1), to_rows] = deep[pl.ds(pair, 1), pl.ds(inner, 1), from_rows]
    to_core(deep.at[pair, inner, from_rows], outer, 1 - pair)
    sent(DEEP_OWN, deep.at[:, 1, pl.ds(0, 9)])
    preact = shifted(acc[0], 1, 0) + acc[1] + shifted(acc[2], 255, 31)

    arrived(COT, cot_recv.at[pl.ds(0, 3)])
    cotangent = jnp.concatenate(
        [
            jnp.concatenate([cot_recv[m][:, :64], cot_recv[m][:, 64:]], axis=0)
            for m in range(4)
        ],
        axis=1,
    ).astype(F32)
    sigma = 1.0 / (1.0 + jnp.exp(-preact))
    activated = (preact * sigma).astype(BF)
    grad_pre = (cotangent * (sigma * (1.0 + preact * (1.0 - sigma)))).astype(BF)
    for half in range(2):
        grad[half, 1, 1:9] = grad_pre[:, 128 * half : 128 * half + 128].reshape(8, 32, 128)

    turned = matmul_nt(order[...], grad_pre).astype(BF)
    grad_t_send[0] = turned[:128]
    grad_t_send[1] = turned[128:]
    slot = 2 * pair + c
    grad_t[pl.ds(slot, 1)] = grad_t_send[pl.ds(c, 1)]
    mine = grad_t.at[slot]
    send(GRAD_SHARE, grad_t_send.at[1 - c], mine, (beside, other_c))
    send(GRAD_SHARE, grad_t_send.at[c], mine, (beside, n))
    send(GRAD_SHARE, grad_t_send.at[1 - c], mine, (w, other_c))
    sent(GRAD_SHARE, grad_t.at[pl.ds(0, 3)])
    send_halos(grad, GRAD_ROWS)

    pass_on(1, DEEP_OWN)
    pass_on(inner, DEEP_OUTER)
    sent(DEEP_CORE, deep_all.at[:, :, pl.ds(0, 9)])

    arrived(GRAD_SHARE, grad_t.at[pl.ds(0, 3)])
    lane = lax.broadcasted_iota(jnp.int32, (128, 256), 1) % 32
    for m in range(4):
        block = grad_t[m].astype(F32)
        at = 256 * m
        grad_rows[0:128, at : at + 256] = jnp.where(lane == 31, 0.0, pltpu.roll(block, 255, 1)).astype(BF)
        grad_rows[128:256, at : at + 256] = grad_t[m]
        grad_rows[256:384, at : at + 256] = jnp.where(lane == 0, 0.0, pltpu.roll(block, 1, 1)).astype(BF)
    def cells_at(i, j):
        return jnp.concatenate([deep_all[i, s, j : j + 16].reshape(512, 128) for s in range(2)], axis=0)

    arrived(DEEP_CORE, deep_all.at[:, :, pl.ds(0, 9)])
    slab = jnp.concatenate([cells_at(i, j) for i, j in Y_TAPS], axis=1)
    term = matmul(grad_rows[...], slab).astype(BF)
    for yy in range(NY):
        for k in range(3):
            at = 128 * k + 32 * yy
            cy_send[yy, k] = term[at : at + 32]
    for d in Y_ORDER:
        send(CONV_Y, cy_send.at[(y + d) % NY], cy_recv.at[d - 1], ys[d - 1])
    sent(CONV_Y, cy_recv)
    for k in range(3):
        grad_rows_z[128 * k : 128 * k + 128, :] = matmul(order_z[...], grad_rows[128 * k : 128 * k + 128, :]).astype(BF)
    slab = jnp.concatenate([cells_at(i, j) for i, j in Z_TAPS], axis=1)
    term = matmul(grad_rows_z[...], slab).astype(BF)
    for zz in range(NZ):
        for k in range(3):
            at = 128 * k + 16 * zz
            cz_send[zz, k] = term[at : at + 16]
    flush((GRAD_ROWS, GRAD_LOW))
    for d in Z_ORDER:
        send(CONV_Z, cz_send.at[(z + d) % NZ], cz_recv.at[d - 1], zs[d - 1])
    sent(CONV_Z, cz_recv)

    for i in (1, 2, 0):
        plane = 2 - i
        if i == 1:
            rows_arrive(grad, GRAD_ROWS)
        else:
            plane_arrives(grad, GRAD_ROWS, plane)
        slab = jnp.concatenate(
            window(grad, plane, 2) + window(grad, plane, 1) + window(grad, plane, 0), axis=1
        )
        for k in range(3):
            weights = jnp.concatenate([cw[9 * i + 3 * j + k] for j in range(3)], axis=1)
            term = matmul_nt(slab, weights)
            acc[k] = term if i == 1 else acc[k] + term
    grad_deep = (shifted(acc[0], 255, 31) + acc[1] + shifted(acc[2], 1, 0)).astype(BF)

    partial = matmul(patches_t[...], grad_deep)
    low, high = partial[:, :128], partial[:, 128:]
    dc_send[...] = jnp.where(c == 0, high, low).astype(BF)
    send(DOWN_C, dc_send, dc_recv, (w, other_c))
    sent(DOWN_C, dc_send)
    kept = jnp.where(c == 0, low, high)

    for m in range(4):
        part = activated[:, 64 * m : 64 * m + 64]
        act_send[m] = jnp.concatenate([part[:128], part[128:]], axis=1)
    act_recv[pl.ds(n, 1)] = act_send[pl.ds(n, 1)]
    for d in (1, 3, 2):
        send(ACT, act_send.at[(n + d) % 4], act_recv.at[n], near[d - 1])
    sent(ACT, act_send.at[pl.ds(0, 3)])

    spread = matmul_nt(grad_deep, dw[...])
    for a in range(2):
        for b in range(2):
            for e in range(2):
                at = (4 * a + 2 * b + e) * 128
                wide_f32[a, :, b, pl.ds(e, 32, stride=2), :] = spread[:, at : at + 128].reshape(8, 32, 128)
    vol[...] = wide_f32[...].astype(BF)
    vg_write = pltpu.make_async_copy(vol, vg_out, local_sem.at[0])
    vg_write.start()

    arrived(DOWN_C, dc_recv)
    total = (kept + dc_recv[...].astype(F32)).reshape(16, 2, 2, 2, 8, 128)
    for xx in range(2):
        for ll in range(2):
            for zz in range(2):
                dx_rows[xx, ll, :, 8 * zz : 8 * zz + 8] = total[:, zz, xx, ll]
    dx_send[...] = dx_rows[...].astype(BF)
    for s, (dy, dx, dl, to) in enumerate(xys):
        src = dx_send.at[(xh + dx) % 2, (l + dl) % 2, pl.ds(4 * ((y + dy) % NY), 4)]
        send(DOWN_XY, src, dx_recv.at[s], to)
    sent(DOWN_XY, dx_recv)

    arrived(CONV_Y, cy_recv)
    total = cy_send[pl.ds(y, 1)].reshape(3, 32, YL).astype(F32)
    for d in range(3):
        total = total + cy_recv[d].astype(F32)
    sum_rows[...] = total
    for zz in range(NZ):
        for m in range(3 * len(Y_TAPS)):
            part = sum_rows[m % 3, 4 * zz : 4 * zz + 4, 128 * (m // 3) : 128 * (m // 3) + 128]
            cyz_rows[zz, 4 * (m % 4) : 4 * (m % 4) + 4, 128 * (m // 4) : 128 * (m // 4) + 128] = part
    cyz_send[...] = cyz_rows[...].astype(BF)
    for d in Z_ORDER:
        send(CONV_YZ, cyz_send.at[(z + d) % NZ], cyz_recv.at[d - 1], zs[d - 1])
    sent(CONV_YZ, cyz_recv)

    arrived(CONV_Z, cz_recv)
    halves = [cz_send[pl.ds(z, 1)].reshape(3, 16, ZL).astype(F32), 0.0]
    for d in range(1, NZ):
        halves[d % 2] = halves[d % 2] + cz_recv[d - 1].astype(F32)
    for h in range(2):
        sum_rows[:, :16, :ZL] = halves[h]
        for yy in range(NY):
            for m in range(3 * len(Z_TAPS)):
                part = sum_rows[m % 3, 4 * yy : 4 * yy + 4, 128 * (m // 3) : 128 * (m // 3) + 128]
                czy_rows[yy, h, 4 * (m % 4) : 4 * (m % 4) + 4, 128 * (m // 4) : 128 * (m // 4) + 128] = part
    czy_send[...] = czy_rows[...].astype(BF)
    for d in Y_ORDER:
        send(CONV_ZY, czy_send.at[(y + d) % NY], czy_recv.at[d - 1], ys[d - 1])
    sent(CONV_ZY, czy_recv)

    arrived(DOWN_XY, dx_recv)
    total = dx_rows[pl.ds(xh, 1), pl.ds(l, 1), pl.ds(4 * y, 4)].reshape(4, 16, 128)
    for s in range(15):
        total = total + dx_recv[s].astype(F32)
    dz_send[...] = total.reshape(NZ, 8, 128)
    for d in Z_ORDER:
        send(DOWN_Z, dz_send.at[(z + d) % NZ], dz_recv.at[NZ - 1 + d], zs_crossed[d - 1])
        send(DOWN_Z, dz_send.at[(z + d) % NZ], dz_recv.at[d - 1], zs[d - 1])
    send(DOWN_Z, dz_send.at[z], dz_recv.at[NZ - 1], (w, other_c))
    sent(DOWN_Z, dz_recv)

    arrived(ACT, act_recv.at[pl.ds(0, 3)])
    for m in range(4):
        act_vmem[256 * m : 256 * m + 128] = act_recv[m][:, :64]
        act_vmem[256 * m + 128 : 256 * m + 256] = act_recv[m][:, 64:]
    act_write = pltpu.make_async_copy(act_vmem, act_out, local_sem.at[1])
    act_write.start()

    arrived(CONV_ZY, czy_recv)
    total = czy_send[pl.ds(y, 1)].reshape(2, 16, 128 * Z_BLOCKS).astype(F32)
    for d in range(3):
        total = total + czy_recv[d].astype(F32)
    last_sum[pl.ds(pair, 1), :, 128 * Y_BLOCKS :] = total[0:1]
    last_sum[pl.ds(1 - pair, 1), :, 128 * Y_BLOCKS :] = total[1:2]
    arrived(CONV_YZ, cyz_recv)
    halves = [cyz_send[pl.ds(z, 1)].astype(F32), 0.0]
    for d in range(1, NZ):
        halves[d % 2] = halves[d % 2] + cyz_recv[d - 1 : d].astype(F32)
    last_sum[pl.ds(pair, 1), :, : 128 * Y_BLOCKS] = halves[0]
    last_sum[pl.ds(1 - pair, 1), :, : 128 * Y_BLOCKS] = halves[1]
    for h in range(2):
        whole = last_sum[h]
        for q in range(2):
            pieces = [whole[:, 128 * b + 64 * q : 128 * b + 64 * q + 64] for b in range(Y_BLOCKS + Z_BLOCKS)]
            last_send[h, q] = jnp.concatenate(pieces, axis=1).astype(BF)

    def last(slot, h, q, to):
        send(CONV_LAST, last_send.at[h, q], last_recv.at[slot], to, received=CONV_LAST if slot else CONV_CORE)

    near_l, far_l = 2 * l, 2 - 2 * l

    @pl.when(xh != c)
    def _():
        last(1, 1 - l, 0, (w, far_l))
        last(1, 1 - l, 1, (w, far_l + 1))
        last(0, l, 1 - c, (w, other_c))

    @pl.when(xh == c)
    def _():
        last(2, l, 0, (across, near_l))
        last(2, l, 1, (across, near_l + 1))
        last(3, 1 - l, 0, (across, far_l))
        last(3, 1 - l, 1, (across, far_l + 1))

    arrived(DOWN_Z, dz_recv)
    total = dz_send[pl.ds(z, 1)].reshape(8, 128)
    for d in range(NZ - 1):
        total = total + dz_recv[d]
    theirs = dz_recv[NZ - 1]
    for d in range(NZ, 2 * NZ - 1):
        theirs = theirs + dz_recv[d]
    both = jnp.concatenate([jnp.where(c == 0, total, theirs), jnp.where(c == 0, theirs, total)], axis=1)
    dg_vmem[...] = jnp.where(c == 0, both[:4], both[4:]) * factor
    dg_write = pltpu.make_async_copy(dg_vmem, dg_out, local_sem.at[3])
    dg_write.start()

    @pl.when(xh != c)
    def _():
        remote(CONV_LAST, last_recv.at[pl.ds(0, 3)], last_recv.at[pl.ds(0, 3)], near[0]).wait_send()

    @pl.when(xh == c)
    def _():
        remote(CONV_LAST, last_recv, last_recv, near[0]).wait_send()
        arrived(CONV_CORE, last_recv.at[0])

    arrived(CONV_LAST, last_recv.at[pl.ds(1, 3)])
    own = last_send[pl.ds(l, 1), pl.ds(c, 1)].reshape(16, 64 * (Y_BLOCKS + Z_BLOCKS))
    conv = jnp.where(c == xh, last_recv[0], own).astype(F32)
    for slot in range(1, 4):
        conv = conv + last_recv[slot].astype(F32)
    conv = conv * factor
    for first, taps in ((0, Y_TAPS), (Y_BLOCKS, Z_TAPS)):
        for m in range(3 * len(taps)):
            i, j = taps[m // 3]
            at = 64 * (first + m // 4)
            cg_vmem[9 * i + 3 * j + m % 3] = conv[4 * (m % 4) : 4 * (m % 4) + 4, at : at + 64]
    cg_write = pltpu.make_async_copy(cg_vmem, cg_out, local_sem.at[2])
    cg_write.start()
    flush(range(GROUPS))
    for copy in (vg_write, act_write, cg_write, dg_write):
        copy.wait()


def write_out(*refs):
    arrays = (len(refs) - 1) // 2
    sems = refs[-1]
    copies = [
        pltpu.make_async_copy(src, dst, sems.at[s])
        for s, (src, dst) in enumerate(zip(refs[:arrays], refs[arrays:-1]))
    ]
    for copy in copies:
        copy.start()
    for copy in copies:
        copy.wait()


def on_device(volume, down_weight, conv_weight, cotangent):
    factor = 1.0 / (32 * math.sqrt(64))
    hbm = pl.BlockSpec(memory_space=pltpu.HBM)
    vmem = pl.BlockSpec(memory_space=pltpu.VMEM)
    scratch = [
        ((2, 8, 2, 64, 128), BF),
        ((1024, 256), BF),
        ((27, 256, 256), BF),
        ((4, 256, 64), BF),
        ((2, 8, 2, 64, 128), F32),
        ((256, 1024), BF),
        ((1024, 256), BF),
        ((2, 3, 10, 32, 128), BF),
        ((2, 3, 10, 32, 128), BF),
        ((256, 256), BF),
        ((128, 128), BF),
        ((3, 2, 18, 32, 128), BF),
        ((2, 128, 256), BF),
        ((4, 128, 256), BF),
        ((384, 1024), BF),
        ((384, 1024), BF),
        ((3, 256, 256), F32),
        ((4, 128, 128), BF),
        ((4, 128, 128), BF),
        ((4, 128, 128), BF),
        ((4, 128, 128), BF),
        ((1024, 64), BF),
        ((4, 3, 32, YL), BF),
        ((3, 3, 32, YL), BF),
        ((3, 32, YL), F32),
        ((8, 16, 128 * Y_BLOCKS), F32),
        ((8, 16, 128 * Y_BLOCKS), BF),
        ((7, 16, 128 * Y_BLOCKS), BF),
        ((8, 3, 16, ZL), BF),
        ((7, 3, 16, ZL), BF),
        ((4, 2, 16, 128 * Z_BLOCKS), F32),
        ((4, 2, 16, 128 * Z_BLOCKS), BF),
        ((3, 2, 16, 128 * Z_BLOCKS), BF),
        ((1024, 128), BF),
        ((1024, 128), BF),
        ((2, 2, 16, 16, 128), F32),
        ((2, 2, 16, 16, 128), BF),
        ((15, 4, 16, 128), BF),
        ((8, 8, 128), F32),
        ((15, 8, 128), F32),
        ((27, 4, 64), F32),
        ((4, 256), F32),
        ((2, 16, 128 * (Y_BLOCKS + Z_BLOCKS)), F32),
        ((2, 2, 16, 64 * (Y_BLOCKS + Z_BLOCKS)), BF),
        ((4, 16, 64 * (Y_BLOCKS + Z_BLOCKS)), BF),
    ]
    results = pl.pallas_call(
        functools.partial(kernel, factor),
        name="unet_level",
        out_shape=(
            jax.ShapeDtypeStruct((1024, 64), BF),
            jax.ShapeDtypeStruct((2, 8, 2, 64, 128), BF),
            jax.ShapeDtypeStruct((4, 256), F32),
            jax.ShapeDtypeStruct((27, 4, 64), F32),
        ),
        in_specs=[hbm] * 4,
        out_specs=(hbm,) * 4,
        scratch_shapes=[pltpu.VMEM(shape, dtype) for shape, dtype in scratch]
        + [
            pltpu.SemaphoreType.DMA((4,)),
            pltpu.SemaphoreType.DMA((GROUPS,)),
            pltpu.SemaphoreType.DMA((GROUPS,)),
        ],
        compiler_params=pltpu.CompilerParams(
            collective_id=0, has_side_effects=True, vmem_limit_bytes=VMEM_BYTES
        ),
        cost_estimate=pl.CostEstimate(flops=3200000000, bytes_accessed=8000000, transcendentals=65536),
    )(
        volume.reshape(2, 8, 2, 64, 128),
        down_weight,
        conv_weight,
        cotangent.reshape(4, 256, 64),
    )
    activated, volume_grad, down_grad, conv_grad = pl.pallas_call(
        write_out,
        name="write_out",
        out_shape=tuple(jax.ShapeDtypeStruct(r.shape, r.dtype) for r in results),
        in_specs=[vmem] * 4,
        out_specs=(hbm,) * 4,
        scratch_shapes=[pltpu.SemaphoreType.DMA((4,))],
        compiler_params=pltpu.CompilerParams(vmem_limit_bytes=VMEM_BYTES),
    )(*results)
    return (
        activated.reshape(1, 32, 32, 64),
        volume_grad.reshape(2, 16, 64, 128),
        down_grad,
        conv_grad.transpose(0, 2, 1),
    )


def solution(mesh):
    placed = (P("wide", "narrow", None, None), P(), P(), P("wide", None, None, "narrow"))
    return jax.shard_map(
        on_device,
        mesh=mesh,
        in_specs=placed,
        out_specs=(
            P("wide", None, None, "narrow"),
            P("wide", "narrow", None, None),
            P(("wide", "narrow"), None),
            P(None, "narrow", "wide"),
        ),
        check_vma=False,
    )
```

```python
import functools
import math

import jax
import jax.numpy as jnp
from jax import lax
from jax.experimental import pallas as pl
from jax.experimental.pallas import tpu as pltpu
from jax.sharding import PartitionSpec as P

MESH = pl.DeviceIdType.MESH
VMEM_BYTES = 54784 * 1024
BF = jnp.bfloat16
F32 = jnp.float32
Y_TAPS = ((0, 0), (0, 1), (0, 2), (1, 0), (1, 1), (1, 2))
Z_TAPS = ((2, 0), (2, 1), (2, 2))
YL, ZL = 128 * len(Y_TAPS), 128 * len(Z_TAPS)
NY, NZ = 4, 8
Y_ORDER, Z_ORDER = (2, 1, 3), (4, 3, 5, 2, 6, 1, 7)

COT, DEEP_ROWS, DEEP_LOW, DEEP_HIGH, DEEP_OWN, DEEP_OUTER, DEEP_CORE, ACT = range(8)
GRAD_ROWS, GRAD_LOW, GRAD_HIGH, GRAD_SHARE, CONV_Y, CONV_YZ, CONV_Z, CONV_ZY = range(8, 16)
DOWN_C, DOWN_XY, DOWN_Z, CONV_LAST, CONV_CORE = range(16, 21)
GROUPS = 21
Y_BLOCKS, Z_BLOCKS = -(-3 * len(Y_TAPS) // 4), -(-3 * len(Z_TAPS) // 4)


def matmul(a, b):
    return jnp.dot(a, b, preferred_element_type=F32)


def matmul_nt(a, b):
    return lax.dot_general(a, b, (((1,), (1,)), ((), ())), preferred_element_type=F32)


def kernel(
    factor,
    vol_ref,
    dw_ref,
    cw_ref,
    cot_ref,
    act_out,
    vg_out,
    dg_out,
    cg_out,
    vol,
    dw,
    cw,
    cot,
    wide_f32,
    patches,
    patches_t,
    deep,
    grad,
    order,
    order_z,
    deep_all,
    grad_t_send,
    grad_t,
    grad_rows,
    grad_rows_z,
    acc,
    cot_send,
    cot_recv,
    act_send,
    act_recv,
    act_vmem,
    cy_send,
    cy_recv,
    sum_rows,
    cyz_rows,
    cyz_send,
    cyz_recv,
    cz_send,
    cz_recv,
    czy_rows,
    czy_send,
    czy_recv,
    dc_send,
    dc_recv,
    dx_rows,
    dx_send,
    dx_recv,
    dz_send,
    dz_recv,
    cg_vmem,
    dg_vmem,
    last_sum,
    last_send,
    last_recv,
    local_sem,
    send_sem,
    recv_sem,
):
    w = lax.axis_index("wide")
    n = lax.axis_index("narrow")
    y, z, xh = w // 16, (w // 2) % NZ, w % 2
    l, c = n // 2, n % 2
    pair = z % 2

    def wide_of(yy, zz, xx):
        return ((yy % NY) * NZ + zz % NZ) * 2 + xx

    near = [(w, (n + d) % 4) for d in range(1, 4)]
    up, down = (w + 1) % 64, (w + 63) % 64
    right, left = (n + 1) % 4, (n + 3) % 4
    depth = [(s, (n + d) % 4) for s in (up, down) for d in range(4)]
    ys = [(wide_of(y + d, z, xh), n) for d in range(1, NY)]
    zs = [(wide_of(y, z + d, xh), n) for d in range(1, NZ)]
    other_c = n + 1 - 2 * c
    zs_crossed = [(to, other_c) for to, _ in zs]
    across = wide_of(y, z, 1 - xh)
    other_l = (n + 2) % 4
    beside = wide_of(y, z + 1 - 2 * pair, xh)
    xys = [
        (dy, dx, dl, (wide_of(y + dy, z, (xh + dx) % 2), n + 2 * dl * (1 - 2 * l)))
        for dy in (2, 1, 3, 0)
        for dx, dl in ((1, 0), (0, 1), (1, 1), (0, 0))
        if dy or dx or dl
    ]

    loads = [
        pltpu.make_async_copy(src, dst, local_sem.at[s])
        for s, (src, dst) in enumerate(((vol_ref, vol), (dw_ref, dw), (cot_ref, cot), (cw_ref, cw)))
    ]
    for copy in loads[:3]:
        copy.start()

    barrier = pltpu.get_barrier_semaphore()
    partners = near + depth + ys + zs + zs_crossed + [to for dy, dx, dl, to in xys if dy and (dx or dl)]
    for who in partners:
        pl.semaphore_signal(barrier, inc=1, device_id=who, device_id_type=MESH)

    def remote(number, src, dst, who, received=None):
        return pltpu.make_async_remote_copy(
            src_ref=src,
            dst_ref=dst,
            send_sem=send_sem.at[number],
            recv_sem=recv_sem.at[number if received is None else received],
            device_id=who,
            device_id_type=MESH,
        )

    def send(*args, **kwargs):
        remote(*args, **kwargs).start()

    def finish(number, ref, edge_ref, receiving):
        def wait(ref):
            copy = remote(number, ref, ref, near[0])
            if receiving:
                copy.wait_recv()
            else:
                copy.wait_send()

        if edge_ref is None:
            wait(ref)
        else:
            pl.when(inside)(lambda: wait(ref))
            pl.when(jnp.logical_not(inside))(lambda: wait(edge_ref))

    def arrived(number, ref, edge_ref=None):
        finish(number, ref, edge_ref, True)

    outgoing = []

    def sent(number, ref, edge_ref=None):
        outgoing.append((number, ref, edge_ref))

    def flush(numbers):
        for group in [group for group in outgoing if group[0] in numbers]:
            finish(*group, False)
            outgoing.remove(group)


    inside = (n == 1) | (n == 2)
    far = (w + 63 + 2 * xh) % 64

    def send_halos(buf, base):
        def rows(to, plane, received):
            for missing, who, first, at in ((3, n + 1, 8, 0), (0, n - 1, 1, 9)):

                @pl.when(n != missing)
                def _():
                    src = buf.at[:, 1, pl.ds(first, 1)]
                    send(base, src, buf.at[:, plane, pl.ds(at, 1)], (to, who), received=received)

        rows(w, 1, base)
        for to, s in ((far, 1 - xh), (across, xh)):
            rows(to, 2 * s, base + 1 + s)
        for to, s in ((far, 1 - xh), (across, xh)):
            planes = buf.at[:, 2 * s, pl.ds(1, 8)]
            send(base + 1, buf.at[:, 1, pl.ds(1, 8)], planes, (to, n), received=base + 1 + s)
        sent(base, buf.at[:, 1, pl.ds(0, 6)], buf.at[:, 1, pl.ds(0, 3)])
        sent(base + 1, buf.at[:, pl.ds(0, 2), pl.ds(0, 8)])

    def clear_rows(buf, plane):
        @pl.when(n == 0)
        def _():
            buf[:, plane, 0:1] = jnp.zeros((2, 1, 32, 128), BF)

        @pl.when(n == 3)
        def _():
            buf[:, plane, 9:10] = jnp.zeros((2, 1, 32, 128), BF)

    def rows_arrive(buf, base):
        arrived(base, buf.at[:, 1, pl.ds(0, 2)], buf.at[:, 1, pl.ds(0, 1)])
        clear_rows(buf, 1)

    def plane_arrives(buf, base, plane):
        arrived(base + 1 + plane // 2, buf.at[:, plane], buf.at[:, plane, pl.ds(0, 9)])
        clear_rows(buf, plane)

        @pl.when(w == (0 if plane == 0 else 63))
        def _():
            buf[:, plane] = jnp.zeros((2, 10, 32, 128), BF)

    loads[0].wait()
    wide_f32[...] = vol[...].astype(F32)
    for a in range(2):
        for b in range(2):
            for e in range(2):
                part = wide_f32[a, :, b, pl.ds(e, 32, stride=2), :].reshape(256, 128).astype(BF)
                at = (4 * a + 2 * b + e) * 128
                patches[:, at : at + 128] = part
    loads[1].wait()
    loads[3].start()
    cells = matmul(patches[...], dw[...]).astype(BF)
    for half in range(2):
        deep[half, 1, 1:9] = cells[:, 128 * half : 128 * half + 128].reshape(8, 32, 128)

    from_rows, to_rows = pl.ds(c, 9), pl.ds(9 * c, 9)
    outer, inner = 2 * pair, 2 - 2 * pair

    def to_core(src, plane, chip):
        send(DEEP_CORE, src, deep_all.at[plane, chip, to_rows], (w, other_c))

    def share_core(plane):
        deep_all[plane, pl.ds(pair, 1), to_rows] = deep[pl.ds(pair, 1), plane, from_rows]
        to_core(deep.at[pair, plane, from_rows], plane, pair)

    def share_across(plane, received):
        src = deep.at[1 - pair, plane, from_rows]
        send(DEEP_OWN, src, deep_all.at[plane, pair, to_rows], (beside, n), received=received)

    def pass_on(plane, received):
        theirs = deep_all.at[plane, 1 - pair, to_rows]
        arrived(received, theirs)
        to_core(theirs, plane, 1 - pair)

    loads[2].wait()
    for m in range(4):
        cot_send[m] = jnp.concatenate([cot[m, :128], cot[m, 128:]], axis=1)
    cot_recv[pl.ds(n, 1)] = cot_send[pl.ds(n, 1)]
    pl.semaphore_wait(barrier, len(partners))
    send_halos(deep, DEEP_ROWS)
    for d in (1, 3, 2):
        send(COT, cot_send.at[(n + d) % 4], cot_recv.at[n], near[d - 1])
    sent(COT, cot_send.at[pl.ds(0, 3)])
    cyz_rows[...] = jnp.zeros_like(cyz_rows)
    czy_rows[...] = jnp.zeros_like(czy_rows)

    for s in range(4):
        block = patches[:, 256 * s : 256 * s + 256].astype(F32)
        patches_t[256 * s : 256 * s + 256, :] = block.T.astype(BF)

    row = lax.broadcasted_iota(jnp.int32, (256, 256), 0)
    column = lax.broadcasted_iota(jnp.int32, (256, 256), 1)
    q = row % 128
    source = (q // 32) * 64 + ((q // 4) % 8) * 8 + (1 - row // 128) * 4 + q % 4
    order[...] = jnp.where(column == source, 1.0, 0.0).astype(BF)
    row = lax.broadcasted_iota(jnp.int32, (128, 128), 0)
    column = lax.broadcasted_iota(jnp.int32, (128, 128), 1)
    source = ((row // 4) % 4) * 32 + (row // 16) * 4 + row % 4
    order_z[...] = jnp.where(column == source, 1.0, 0.0).astype(BF)

    def window(buf, plane, first):
        return [buf[half, plane, first : first + 8].reshape(256, 128) for half in range(2)]

    def shifted(value, by, masked):
        column = lax.broadcasted_iota(jnp.int32, value.shape, 0) % 32
        return jnp.where(column == masked, 0.0, pltpu.roll(value, by, 0))

    loads[3].wait()
    for i in (1, 0, 2):
        if i == 1:
            rows_arrive(deep, DEEP_ROWS)
        else:
            plane_arrives(deep, DEEP_ROWS, i)
        share_core(i)
        if i == 1:
            share_across(1, DEEP_OWN)
        else:

            @pl.when(outer == i)
            def _():
                share_across(i, DEEP_OUTER)

        slab = jnp.concatenate(window(deep, i, 0) + window(deep, i, 1) + window(deep, i, 2), axis=1)
        for k in range(3):
            weights = jnp.concatenate([cw[9 * i + 3 * j + k] for j in range(3)], axis=0)
            term = matmul(slab, weights)
            acc[k] = term if i == 1 else acc[k] + term
    deep_all[pl.ds(outer, 1), pl.ds(1 - pair, 1), to_rows] = deep[pl.ds(pair, 1), pl.ds(inner, 1), from_rows]
    to_core(deep.at[pair, inner, from_rows], outer, 1 - pair)
    sent(DEEP_OWN, deep.at[:, 1, pl.ds(0, 9)])
    preact = shifted(acc[0], 1, 0) + acc[1] + shifted(acc[2], 255, 31)

    arrived(COT, cot_recv.at[pl.ds(0, 3)])
    cotangent = jnp.concatenate(
        [
            jnp.concatenate([cot_recv[m][:, :64], cot_recv[m][:, 64:]], axis=0)
            for m in range(4)
        ],
        axis=1,
    ).astype(F32)
    sigma = 1.0 / (1.0 + jnp.exp(-preact))
    activated = (preact * sigma).astype(BF)
    grad_pre = (cotangent * (sigma * (1.0 + preact * (1.0 - sigma)))).astype(BF)
    for half in range(2):
        grad[half, 1, 1:9] = grad_pre[:, 128 * half : 128 * half + 128].reshape(8, 32, 128)

    turned = matmul_nt(order[...], grad_pre).astype(BF)
    grad_t_send[0] = turned[:128]
    grad_t_send[1] = turned[128:]
    slot = 2 * pair + c
    grad_t[pl.ds(slot, 1)] = grad_t_send[pl.ds(c, 1)]
    mine = grad_t.at[slot]
    send(GRAD_SHARE, grad_t_send.at[1 - c], mine, (beside, other_c))
    send(GRAD_SHARE, grad_t_send.at[c], mine, (beside, n))
    send(GRAD_SHARE, grad_t_send.at[1 - c], mine, (w, other_c))
    sent(GRAD_SHARE, grad_t.at[pl.ds(0, 3)])
    send_halos(grad, GRAD_ROWS)

    pass_on(1, DEEP_OWN)
    pass_on(inner, DEEP_OUTER)
    sent(DEEP_CORE, deep_all.at[:, :, pl.ds(0, 9)])

    arrived(GRAD_SHARE, grad_t.at[pl.ds(0, 3)])
    lane = lax.broadcasted_iota(jnp.int32, (128, 256), 1) % 32
    for m in range(4):
        block = grad_t[m].astype(F32)
        at = 256 * m
        grad_rows[0:128, at : at + 256] = jnp.where(lane == 31, 0.0, pltpu.roll(block, 255, 1)).astype(BF)
        grad_rows[128:256, at : at + 256] = grad_t[m]
        grad_rows[256:384, at : at + 256] = jnp.where(lane == 0, 0.0, pltpu.roll(block, 1, 1)).astype(BF)
    def cells_at(i, j):
        return jnp.concatenate([deep_all[i, s, j : j + 16].reshape(512, 128) for s in range(2)], axis=0)

    arrived(DEEP_CORE, deep_all.at[:, :, pl.ds(0, 9)])
    for first in (0, YL // 2):
        lanes = pl.ds(first, YL // 2)
        some = Y_TAPS[first // 128 : (first + YL // 2) // 128]
        slab = jnp.concatenate([cells_at(i, j) for i, j in some], axis=1)
        term = matmul(grad_rows[...], slab).astype(BF)
        for yy in range(NY):
            for k in range(3):
                at = 128 * k + 32 * yy
                cy_send[yy, k, :, first : first + YL // 2] = term[at : at + 32]
        for d in Y_ORDER:
            src = cy_send.at[(y + d) % NY, :, :, lanes]
            send(CONV_Y, src, cy_recv.at[d - 1, :, :, lanes], ys[d - 1])
    sent(CONV_Y, cy_recv)
    for k in range(3):
        grad_rows_z[128 * k : 128 * k + 128, :] = matmul(order_z[...], grad_rows[128 * k : 128 * k + 128, :]).astype(BF)
    slab = jnp.concatenate([cells_at(i, j) for i, j in Z_TAPS], axis=1)
    term = matmul(grad_rows_z[...], slab).astype(BF)
    for zz in range(NZ):
        for k in range(3):
            at = 128 * k + 16 * zz
            cz_send[zz, k] = term[at : at + 16]
    flush((GRAD_ROWS, GRAD_LOW))
    for d in Z_ORDER:
        send(CONV_Z, cz_send.at[(z + d) % NZ], cz_recv.at[d - 1], zs[d - 1])
    sent(CONV_Z, cz_recv)

    for i in (1, 2, 0):
        plane = 2 - i
        if i == 1:
            rows_arrive(grad, GRAD_ROWS)
        else:
            plane_arrives(grad, GRAD_ROWS, plane)
        slab = jnp.concatenate(
            window(grad, plane, 2) + window(grad, plane, 1) + window(grad, plane, 0), axis=1
        )
        for k in range(3):
            weights = jnp.concatenate([cw[9 * i + 3 * j + k] for j in range(3)], axis=1)
            term = matmul_nt(slab, weights)
            acc[k] = term if i == 1 else acc[k] + term
    grad_deep = (shifted(acc[0], 255, 31) + acc[1] + shifted(acc[2], 1, 0)).astype(BF)

    partial = matmul(patches_t[...], grad_deep)
    low, high = partial[:, :128], partial[:, 128:]
    dc_send[...] = jnp.where(c == 0, high, low).astype(BF)
    send(DOWN_C, dc_send, dc_recv, (w, other_c))
    sent(DOWN_C, dc_send)
    kept = jnp.where(c == 0, low, high)

    for m in range(4):
        part = activated[:, 64 * m : 64 * m + 64]
        act_send[m] = jnp.concatenate([part[:128], part[128:]], axis=1)
    act_recv[pl.ds(n, 1)] = act_send[pl.ds(n, 1)]
    for d in (1, 3, 2):
        send(ACT, act_send.at[(n + d) % 4], act_recv.at[n], near[d - 1])
    sent(ACT, act_send.at[pl.ds(0, 3)])

    spread = matmul_nt(grad_deep, dw[...])
    for a in range(2):
        for b in range(2):
            for e in range(2):
                at = (4 * a + 2 * b + e) * 128
                wide_f32[a, :, b, pl.ds(e, 32, stride=2), :] = spread[:, at : at + 128].reshape(8, 32, 128)
    vol[...] = wide_f32[...].astype(BF)
    vg_write = pltpu.make_async_copy(vol, vg_out, local_sem.at[0])
    vg_write.start()

    arrived(DOWN_C, dc_recv)
    total = (kept + dc_recv[...].astype(F32)).reshape(16, 2, 2, 2, 8, 128)
    for xx in range(2):
        for ll in range(2):
            for zz in range(2):
                dx_rows[xx, ll, :, 8 * zz : 8 * zz + 8] = total[:, zz, xx, ll]
    dx_send[...] = dx_rows[...].astype(BF)
    for s, (dy, dx, dl, to) in enumerate(xys):
        src = dx_send.at[(xh + dx) % 2, (l + dl) % 2, pl.ds(4 * ((y + dy) % NY), 4)]
        send(DOWN_XY, src, dx_recv.at[s], to)
    sent(DOWN_XY, dx_recv)

    arrived(CONV_Y, cy_recv)
    total = cy_send[pl.ds(y, 1)].reshape(3, 32, YL).astype(F32)
    for d in range(3):
        total = total + cy_recv[d].astype(F32)
    sum_rows[...] = total
    for zz in range(NZ):
        for m in range(3 * len(Y_TAPS)):
            part = sum_rows[m % 3, 4 * zz : 4 * zz + 4, 128 * (m // 3) : 128 * (m // 3) + 128]
            cyz_rows[zz, 4 * (m % 4) : 4 * (m % 4) + 4, 128 * (m // 4) : 128 * (m // 4) + 128] = part
    cyz_send[...] = cyz_rows[...].astype(BF)
    for d in Z_ORDER:
        send(CONV_YZ, cyz_send.at[(z + d) % NZ], cyz_recv.at[d - 1], zs[d - 1])
    sent(CONV_YZ, cyz_recv)

    arrived(CONV_Z, cz_recv)
    halves = [cz_send[pl.ds(z, 1)].reshape(3, 16, ZL).astype(F32), 0.0]
    for d in range(1, NZ):
        halves[d % 2] = halves[d % 2] + cz_recv[d - 1].astype(F32)
    for h in range(2):
        sum_rows[:, :16, :ZL] = halves[h]
        for yy in range(NY):
            for m in range(3 * len(Z_TAPS)):
                part = sum_rows[m % 3, 4 * yy : 4 * yy + 4, 128 * (m // 3) : 128 * (m // 3) + 128]
                czy_rows[yy, h, 4 * (m % 4) : 4 * (m % 4) + 4, 128 * (m // 4) : 128 * (m // 4) + 128] = part
    czy_send[...] = czy_rows[...].astype(BF)
    for d in Y_ORDER:
        send(CONV_ZY, czy_send.at[(y + d) % NY], czy_recv.at[d - 1], ys[d - 1])
    sent(CONV_ZY, czy_recv)

    arrived(DOWN_XY, dx_recv)
    total = dx_rows[pl.ds(xh, 1), pl.ds(l, 1), pl.ds(4 * y, 4)].reshape(4, 16, 128)
    for s in range(15):
        total = total + dx_recv[s].astype(F32)
    dz_send[...] = total.reshape(NZ, 8, 128)
    for d in Z_ORDER:
        send(DOWN_Z, dz_send.at[(z + d) % NZ], dz_recv.at[NZ - 1 + d], zs_crossed[d - 1])
        send(DOWN_Z, dz_send.at[(z + d) % NZ], dz_recv.at[d - 1], zs[d - 1])
    send(DOWN_Z, dz_send.at[z], dz_recv.at[NZ - 1], (w, other_c))
    sent(DOWN_Z, dz_recv)

    arrived(ACT, act_recv.at[pl.ds(0, 3)])
    for m in range(4):
        act_vmem[256 * m : 256 * m + 128] = act_recv[m][:, :64]
        act_vmem[256 * m + 128 : 256 * m + 256] = act_recv[m][:, 64:]
    act_write = pltpu.make_async_copy(act_vmem, act_out, local_sem.at[1])
    act_write.start()

    arrived(CONV_ZY, czy_recv)
    total = czy_send[pl.ds(y, 1)].reshape(2, 16, 128 * Z_BLOCKS).astype(F32)
    for d in range(3):
        total = total + czy_recv[d].astype(F32)
    last_sum[pl.ds(pair, 1), :, 128 * Y_BLOCKS :] = total[0:1]
    last_sum[pl.ds(1 - pair, 1), :, 128 * Y_BLOCKS :] = total[1:2]
    arrived(CONV_YZ, cyz_recv)
    halves = [cyz_send[pl.ds(z, 1)].astype(F32), 0.0]
    for d in range(1, NZ):
        halves[d % 2] = halves[d % 2] + cyz_recv[d - 1 : d].astype(F32)
    last_sum[pl.ds(pair, 1), :, : 128 * Y_BLOCKS] = halves[0]
    last_sum[pl.ds(1 - pair, 1), :, : 128 * Y_BLOCKS] = halves[1]
    for h in range(2):
        whole = last_sum[h]
        for q in range(2):
            pieces = [whole[:, 128 * b + 64 * q : 128 * b + 64 * q + 64] for b in range(Y_BLOCKS + Z_BLOCKS)]
            last_send[h, q] = jnp.concatenate(pieces, axis=1).astype(BF)

    def last(slot, h, q, to):
        send(CONV_LAST, last_send.at[h, q], last_recv.at[slot], to, received=CONV_LAST if slot else CONV_CORE)

    near_l, far_l = 2 * l, 2 - 2 * l

    @pl.when(xh != c)
    def _():
        last(1, 1 - l, 0, (w, far_l))
        last(1, 1 - l, 1, (w, far_l + 1))
        last(0, l, 1 - c, (w, other_c))

    @pl.when(xh == c)
    def _():
        last(2, l, 0, (across, near_l))
        last(2, l, 1, (across, near_l + 1))
        last(3, 1 - l, 0, (across, far_l))
        last(3, 1 - l, 1, (across, far_l + 1))

    arrived(DOWN_Z, dz_recv)
    total = dz_send[pl.ds(z, 1)].reshape(8, 128)
    for d in range(NZ - 1):
        total = total + dz_recv[d]
    theirs = dz_recv[NZ - 1]
    for d in range(NZ, 2 * NZ - 1):
        theirs = theirs + dz_recv[d]
    both = jnp.concatenate([jnp.where(c == 0, total, theirs), jnp.where(c == 0, theirs, total)], axis=1)
    dg_vmem[...] = jnp.where(c == 0, both[:4], both[4:]) * factor
    dg_write = pltpu.make_async_copy(dg_vmem, dg_out, local_sem.at[3])
    dg_write.start()

    @pl.when(xh != c)
    def _():
        remote(CONV_LAST, last_recv.at[pl.ds(0, 3)], last_recv.at[pl.ds(0, 3)], near[0]).wait_send()

    @pl.when(xh == c)
    def _():
        remote(CONV_LAST, last_recv, last_recv, near[0]).wait_send()
        arrived(CONV_CORE, last_recv.at[0])

    arrived(CONV_LAST, last_recv.at[pl.ds(1, 3)])
    own = last_send[pl.ds(l, 1), pl.ds(c, 1)].reshape(16, 64 * (Y_BLOCKS + Z_BLOCKS))
    conv = jnp.where(c == xh, last_recv[0], own).astype(F32)
    for slot in range(1, 4):
        conv = conv + last_recv[slot].astype(F32)
    conv = conv * factor
    for first, taps in ((0, Y_TAPS), (Y_BLOCKS, Z_TAPS)):
        for m in range(3 * len(taps)):
            i, j = taps[m // 3]
            at = 64 * (first + m // 4)
            cg_vmem[9 * i + 3 * j + m % 3] = conv[4 * (m % 4) : 4 * (m % 4) + 4, at : at + 64]
    cg_write = pltpu.make_async_copy(cg_vmem, cg_out, local_sem.at[2])
    cg_write.start()
    flush(range(GROUPS))
    for copy in (vg_write, act_write, cg_write, dg_write):
        copy.wait()


def write_out(*refs):
    arrays = (len(refs) - 1) // 2
    sems = refs[-1]
    copies = [
        pltpu.make_async_copy(src, dst, sems.at[s])
        for s, (src, dst) in enumerate(zip(refs[:arrays], refs[arrays:-1]))
    ]
    for copy in copies:
        copy.start()
    for copy in copies:
        copy.wait()


def on_device(volume, down_weight, conv_weight, cotangent):
    factor = 1.0 / (32 * math.sqrt(64))
    hbm = pl.BlockSpec(memory_space=pltpu.HBM)
    vmem = pl.BlockSpec(memory_space=pltpu.VMEM)
    scratch = [
        ((2, 8, 2, 64, 128), BF),
        ((1024, 256), BF),
        ((27, 256, 256), BF),
        ((4, 256, 64), BF),
        ((2, 8, 2, 64, 128), F32),
        ((256, 1024), BF),
        ((1024, 256), BF),
        ((2, 3, 10, 32, 128), BF),
        ((2, 3, 10, 32, 128), BF),
        ((256, 256), BF),
        ((128, 128), BF),
        ((3, 2, 18, 32, 128), BF),
        ((2, 128, 256), BF),
        ((4, 128, 256), BF),
        ((384, 1024), BF),
        ((384, 1024), BF),
        ((3, 256, 256), F32),
        ((4, 128, 128), BF),
        ((4, 128, 128), BF),
        ((4, 128, 128), BF),
        ((4, 128, 128), BF),
        ((1024, 64), BF),
        ((4, 3, 32, YL), BF),
        ((3, 3, 32, YL), BF),
        ((3, 32, YL), F32),
        ((8, 16, 128 * Y_BLOCKS), F32),
        ((8, 16, 128 * Y_BLOCKS), BF),
        ((7, 16, 128 * Y_BLOCKS), BF),
        ((8, 3, 16, ZL), BF),
        ((7, 3, 16, ZL), BF),
        ((4, 2, 16, 128 * Z_BLOCKS), F32),
        ((4, 2, 16, 128 * Z_BLOCKS), BF),
        ((3, 2, 16, 128 * Z_BLOCKS), BF),
        ((1024, 128), BF),
        ((1024, 128), BF),
        ((2, 2, 16, 16, 128), F32),
        ((2, 2, 16, 16, 128), BF),
        ((15, 4, 16, 128), BF),
        ((8, 8, 128), F32),
        ((15, 8, 128), F32),
        ((27, 4, 64), F32),
        ((4, 256), F32),
        ((2, 16, 128 * (Y_BLOCKS + Z_BLOCKS)), F32),
        ((2, 2, 16, 64 * (Y_BLOCKS + Z_BLOCKS)), BF),
        ((4, 16, 64 * (Y_BLOCKS + Z_BLOCKS)), BF),
    ]
    results = pl.pallas_call(
        functools.partial(kernel, factor),
        name="unet_level",
        out_shape=(
            jax.ShapeDtypeStruct((1024, 64), BF),
            jax.ShapeDtypeStruct((2, 8, 2, 64, 128), BF),
            jax.ShapeDtypeStruct((4, 256), F32),
            jax.ShapeDtypeStruct((27, 4, 64), F32),
        ),
        in_specs=[hbm] * 4,
        out_specs=(hbm,) * 4,
        scratch_shapes=[pltpu.VMEM(shape, dtype) for shape, dtype in scratch]
        + [
            pltpu.SemaphoreType.DMA((4,)),
            pltpu.SemaphoreType.DMA((GROUPS,)),
            pltpu.SemaphoreType.DMA((GROUPS,)),
        ],
        compiler_params=pltpu.CompilerParams(
            collective_id=0, has_side_effects=True, vmem_limit_bytes=VMEM_BYTES
        ),
        cost_estimate=pl.CostEstimate(flops=3200000000, bytes_accessed=8000000, transcendentals=65536),
    )(
        volume.reshape(2, 8, 2, 64, 128),
        down_weight,
        conv_weight,
        cotangent.reshape(4, 256, 64),
    )
    activated, volume_grad, down_grad, conv_grad = pl.pallas_call(
        write_out,
        name="write_out",
        out_shape=tuple(jax.ShapeDtypeStruct(r.shape, r.dtype) for r in results),
        in_specs=[vmem] * 4,
        out_specs=(hbm,) * 4,
        scratch_shapes=[pltpu.SemaphoreType.DMA((4,))],
        compiler_params=pltpu.CompilerParams(vmem_limit_bytes=VMEM_BYTES),
    )(*results)
    return (
        activated.reshape(1, 32, 32, 64),
        volume_grad.reshape(2, 16, 64, 128),
        down_grad,
        conv_grad.transpose(0, 2, 1),
    )


def solution(mesh):
    placed = (P("wide", "narrow", None, None), P(), P(), P("wide", None, None, "narrow"))
    return jax.shard_map(
        on_device,
        mesh=mesh,
        in_specs=placed,
        out_specs=(
            P("wide", None, None, "narrow"),
            P("wide", "narrow", None, None),
            P(("wide", "narrow"), None),
            P(None, "narrow", "wide"),
        ),
        check_vma=False,
    )
```
